128 devices in a mesh: lon: 32 (over x_hi, y, z), lat: 4 (over x_lo, core).
Axes of the slice: x: 4 (x_hi: 2, x_lo: 2; x = x_hi * 2 + x_lo), y: 4, z: 4, core: 2. Of those that a mesh axis runs over, the one named last changes fastest.
Arguments:
- background: float32 [32, 512, 69], P('lat', 'lon'), may hold values from -6 to 6
- direction: float32 [32, 512, 69], P('lat', 'lon'), may hold values from -6 to 6
- obs_owner: int32 [65536, 1], P(('lon', 'lat')), may hold values from 0 to 127; in each aligned block of 512 rows (0 to 511, 512 to 1023, ...) at most 8 rows name the same one
- obs_site: int32 [65536], P(('lon', 'lat')), may hold values from 0 to 7658, as said below
- obs_weights: float32 [65536, 4], P(('lon', 'lat')), as said below
- obs_precision: float32 [65536], P(('lon', 'lat')), may hold values from 0.5 to 4
- embed_weight: bfloat16 [69, 1024], replicated, may hold values from -0.75 to 0.75
- attn_gain: float32 [1024], replicated, may hold values from 0.5 to 1.5
- qkv_weight: bfloat16 [1024, 3072], replicated, may hold values from -0.1875 to 0.1875
- logit_scale: float32 [16], replicated, may hold values from 2 to 10
- out_weight: bfloat16 [1024, 1024], replicated, may hold values from -0.1875 to 0.1875
- decode_gain: float32 [1024], replicated, may hold values from 0.5 to 1.5
- decode_weight: bfloat16 [1024, 69], replicated, may hold values from -0.1875 to 0.1875
Outputs:
- hvp: float32 [32, 512, 69], P('lat', 'lon')
- obs_increment: float32 [65536], P(('lon', 'lat'))
The draws below stay inside these ranges and needn't reach their ends.
Inputs may be any that keep to these rules, and one draw needn't show every extreme that they name: `obs_owner`: devices are numbered lon index times the lat axis' size plus lat index; among the 512 rows of one device no owner is named more than 8 times. `obs_site`: A base cell has row under 8 - 1 and column under 16 - 1 of the owner's block, so all four corners lie in that block. `obs_weights`: the four weights of a row are nonnegative and sum to one.
All inputs are finite; a program needn't handle non-finite values.
Results may differ from the reference program's by a relative error of at most 0.02.
Values may be sent and summed in bfloat16 or wider, within the bound.
No kernel may reach another device: no remote copies, remote signals or barrier semaphores. Data moves between devices by JAX's collectives and lax.ppermute only.
A program may use at most 128 MiB of HBM per device.

```python
import math
import jax
import jax.numpy as jnp
import numpy as np
from jax import lax

D = 1024
HEADS = 16
VARS = 69
WLAT = 8
WLON = 16
LAT_DEV = 8
LON_DEV = 16
OBS_DEV = 512
CAP = 8
NLAT = 32
NLON = 512
OBS = 65536
N_LAT = 4
DEVICES = 128


def draw_obs_site(key, part):
    key = jax.random.fold_in(key, 11)
    keys = jax.random.split(key, 3)
    row_pick = jax.random.randint(keys[0], (OBS,), 0, LAT_DEV - 1)
    col_pick = jax.random.randint(keys[1], (OBS,), 0, LON_DEV - 1)
    var_pick = jax.random.randint(keys[2], (OBS,), 0, VARS)
    packed = (row_pick * LON_DEV + col_pick) * VARS + var_pick
    highest = ((LAT_DEV - 2) * LON_DEV + LON_DEV - 2) * VARS + VARS - 1
    packed = packed.at[0].set(highest).at[1].set(0)
    return packed.astype(jnp.int32)


def draw_obs_weights(key, part):
    key = jax.random.fold_in(key, 23)
    keys = jax.random.split(key, 2)
    north = jax.random.uniform(keys[0], (OBS,), jnp.float32)
    east = jax.random.uniform(keys[1], (OBS,), jnp.float32)
    return jnp.stack([(1.0 - north) * (1.0 - east), (1.0 - north) * east, north * (1.0 - east), north * east], axis=1)


def levels(stream_key, dims, cuts, smallest, largest):
    level, own = 1.0, jax.random.fold_in(stream_key, 6)
    for dim, shards_of in cuts:
        draws = jnp.exp(jax.random.uniform(jax.random.fold_in(own, dim), (shards_of,), jnp.float32, smallest / len(cuts), largest / len(cuts)))
        level = level * jnp.repeat(draws, dims[dim] // shards_of).reshape([-1 if axis == dim else 1 for axis in range(len(dims))])
    return level


def assign_block(stream_key, own, number, rows, number_of, top, reach, skew):
    sequence = jax.random.permutation(stream_key, number_of)
    crowded, ordinary = shares(number_of, rows * top, reach, skew, True), shares(number_of, rows * top, reach, skew, False)
    places = jnp.arange(number_of)

    def named(sizes, turn):
        used = int((sizes > 0).sum())
        fixed = max(1, used // 4)
        passed = fixed + (places - fixed + turn * (used - fixed)) % max(1, number_of - fixed)
        return jnp.zeros((number_of,), jnp.int32).at[sequence[jnp.where(places < fixed, places, passed)]].set(jnp.asarray(sizes, jnp.int32))

    sizes = jnp.where(number % 4 == 0, named(crowded, number // 4), named(ordinary, number - number // 4 - 1))
    mixed = jax.random.permutation(jax.random.fold_in(own, 3), number_of)
    giver, taker = mixed[0:number_of // 2 * 2:2], mixed[1:number_of // 2 * 2:2]
    room = jnp.minimum(sizes[giver] - 1, reach - sizes[taker]) // 2
    room = jnp.where((giver == sequence[0]) | (taker == sequence[0]) | (sizes[taker] == 0), 0, jnp.maximum(room, 0))
    passed = jax.random.randint(jax.random.fold_in(own, 4), (number_of // 2,), 0, 1 << 20) % (room + 1)
    sizes = sizes.at[giver].add(-passed).at[taker].add(passed)
    labels = jnp.searchsorted(jnp.cumsum(sizes), jnp.arange(rows * top), side="right").astype(jnp.int32)
    grid = labels.reshape(top, rows).T
    grid = grid[jax.random.permutation(jax.random.fold_in(own, 1), rows)]
    turn = jax.random.randint(jax.random.fold_in(own, 2), (rows, 1), 0, top)
    return jnp.take_along_axis(grid, (jnp.arange(top)[None, :] + turn) % top, axis=1)


def shares(count, total, limit, slope, full):
    loads = [(1 << 20) // math.isqrt(grade ** slope) + 1 for grade in range(1, count + 1)]
    largest = limit if full else min(limit, max(-(-total // count), total * loads[0] // sum(loads)))
    least = 1 if total - largest >= count - 1 else 0
    counts, rest = [largest] + [least] * (count - 1), total - largest - least * (count - 1)
    while rest > 0:
        movable = [i for i in range(1, count) if counts[i] < largest] or [i for i in range(1, count) if counts[i] < limit]
        mass, remaining = sum([loads[i] for i in movable]), rest
        for i in movable:
            addition = min(limit - counts[i], max(1, remaining * loads[i] // mass), rest)
            counts[i] = counts[i] + addition
            rest = rest - addition
    return np.array(counts)


def gaussian(rng, extent, scale, reach, shards=(), held_as=jnp.bfloat16):
    values = scale * jax.random.normal(rng, extent, jnp.float32)
    if shards:
        values = values * levels(rng, extent, shards, -0.22, 0.18)
    return jnp.clip(values, -reach, reach).astype(held_as)


def setup_inputs(seed: int = 0) -> dict:
    seeds = jax.random.split(jax.random.key(seed), 14)
    background = gaussian(seeds[0], (NLAT, NLON, VARS), 1.0, 6.0, ((0, 4), (1, 32)), jnp.float32)
    direction = gaussian(seeds[1], (NLAT, NLON, VARS), 1.0, 6.0, ((0, 4), (1, 32)), jnp.float32)
    obs_owner_keys = jax.random.split(jax.random.fold_in(seeds[2], 1), OBS // OBS_DEV)
    obs_owner_turns = jax.random.permutation(jax.random.fold_in(seeds[2], 3), OBS // OBS_DEV)
    obs_owner = jax.vmap(lambda own, number: assign_block(jax.random.fold_in(seeds[2], 2), own, number, OBS_DEV, DEVICES, 1, CAP, 2))(obs_owner_keys, obs_owner_turns).reshape((OBS, 1))
    obs_site = draw_obs_site(jax.random.fold_in(seeds[13], 71), 0)
    obs_weights = draw_obs_weights(jax.random.fold_in(seeds[13], 71), 0)
    obs_precision = jnp.clip(jnp.exp(math.log(4.0) - 2.0794415 * jax.random.uniform(seeds[5], (OBS,), jnp.float32) ** levels(seeds[5], (OBS,), ((0, 128),), -0.2, 0.2)), 0.5, 4.0)
    embed_weight = gaussian(seeds[6], (VARS, D), VARS ** -0.5, 0.75)
    attn_gain = jnp.clip(1.0 + 0.1 * jax.random.normal(seeds[7], (D,), jnp.float32), 0.5, 1.5)
    qkv_weight = gaussian(seeds[8], (D, 3 * D), D ** -0.5, 0.1875)
    logit_scale = jnp.clip(jnp.exp(jax.random.uniform(seeds[9], (HEADS,), jnp.float32, math.log(2.0), math.log(10.0))), 2.0, 10.0)
    out_weight = gaussian(seeds[10], (D, D), D ** -0.5, 0.1875)
    decode_gain = jnp.clip(1.0 + 0.1 * jax.random.normal(seeds[11], (D,), jnp.float32), 0.5, 1.5)
    decode_weight = gaussian(seeds[12], (D, VARS), D ** -0.5, 0.1875)
    return {"background": background, "direction": direction, "obs_owner": obs_owner, "obs_site": obs_site, "obs_weights": obs_weights, "obs_precision": obs_precision, "embed_weight": embed_weight, "attn_gain": attn_gain, "qkv_weight": qkv_weight, "logit_scale": logit_scale, "out_weight": out_weight, "decode_gain": decode_gain, "decode_weight": decode_weight}


eps_norm = 1e-05
eps_head = 1e-06

def layer_norm(values_in, gain):
    values = values_in.astype(jnp.float32)
    centred = values - lax.optimization_barrier(jnp.mean(values, axis=-1, keepdims=True))
    spread = lax.optimization_barrier(jnp.mean(centred * centred, axis=-1, keepdims=True))
    return centred * lax.rsqrt(spread + eps_norm) * gain

def embed_cells(state, embed_weight):
    return jnp.dot(state.astype(jnp.bfloat16), embed_weight, preferred_element_type=jnp.float32).astype(jnp.bfloat16)

def decode_cells(values_in, decode_gain, decode_weight):
    normed = layer_norm(values_in, decode_gain).astype(jnp.bfloat16)
    return jnp.dot(normed, decode_weight, preferred_element_type=jnp.float32).astype(jnp.bfloat16)

def window_block(values_in, wrapped, attn_gain, qkv_weight, logit_scale, out_weight):
    grid_rows, grid_cols, width = values_in.shape
    head_size = width // HEADS
    across = grid_rows // WLAT
    along = grid_cols // WLON

    def windows(source):
        depth = source.shape[-1]
        source = source.reshape(across, WLAT, along, WLON, depth).transpose(0, 2, 1, 3, 4)
        return source.reshape(across, along, WLAT * WLON, depth)

    def unit_heads(source):
        source = windows(source).reshape(across, along, WLAT * WLON, HEADS, head_size)
        return source * lax.rsqrt(lax.optimization_barrier(jnp.sum(source * source, axis=-1, keepdims=True)) + eps_head)
    normed = layer_norm(values_in, attn_gain).astype(jnp.bfloat16)
    packed = jnp.dot(normed, qkv_weight, preferred_element_type=jnp.float32)
    queries = unit_heads(packed[..., :width])
    key_part = unit_heads(packed[..., width:2 * width])
    value_part = windows(packed[..., 2 * width:].astype(jnp.bfloat16)).reshape(across, along, WLAT * WLON, HEADS, head_size)
    scores = jnp.einsum('abqhd,abkhd->abhqk', queries, key_part, precision=lax.Precision.HIGHEST)
    scores = scores * logit_scale[:, None, None]
    flags = windows(wrapped)[..., 0]
    allowed = (flags[:, :, None, :, None] == flags[:, :, None, None, :]).astype(jnp.float32)
    weights = jnp.exp(scores) * allowed
    probs = (weights / lax.optimization_barrier(jnp.sum(weights, axis=-1, keepdims=True))).astype(jnp.bfloat16)
    mixed = jnp.einsum('abhqk,abkhd->abqhd', probs.astype(jnp.float32), value_part.astype(jnp.float32), precision=lax.Precision.HIGHEST)
    mixed = mixed.astype(jnp.bfloat16).reshape(across, along, WLAT, WLON, width).transpose(0, 2, 1, 3, 4)
    mixed = mixed.reshape(grid_rows, grid_cols, width)
    update = jnp.dot(mixed, out_weight, preferred_element_type=jnp.float32)
    return (values_in.astype(jnp.float32) + update).astype(jnp.bfloat16)

def banded(function, arrays):
    bands = arrays[0].shape[0] // WLAT
    pieces = tuple((item.reshape((bands, WLAT) + item.shape[1:]) for item in arrays))
    result = lax.map(function, pieces)
    return result.reshape((bands * WLAT,) + result.shape[2:])

def reference(background, direction, obs_owner, obs_site, obs_weights, obs_precision, embed_weight, attn_gain, qkv_weight, logit_scale, out_weight, decode_gain, decode_weight):
    lat_cells, lon_cells, var_count = background.shape
    shift_lat = WLAT // 2
    shift_lon = WLON // 2
    row_index = lax.broadcasted_iota(jnp.int32, (lat_cells, lon_cells, 1), 0)
    wrapped = (row_index >= lat_cells - shift_lat).astype(jnp.float32)

    def embedding(state):
        return embed_cells(state, embed_weight)

    def decoding(values_in):
        return decode_cells(values_in, decode_gain, decode_weight)

    def attending(values_in, flags):
        return window_block(values_in, flags, attn_gain, qkv_weight, logit_scale, out_weight)

    def forward_roll(values_in):
        return jnp.roll(values_in, (-shift_lat, -shift_lon), axis=(0, 1))

    def backward_roll(values_in):
        return jnp.roll(values_in, (shift_lat, shift_lon), axis=(0, 1))
    hidden = embedding(background)
    rolled = forward_roll(hidden)
    block_out = banded(lambda members: attending(members[0], members[1]), (rolled, wrapped))
    settled = backward_roll(block_out)
    hidden_tan = jax.jvp(embedding, (background,), (direction,))[1]
    rolled_tan = forward_roll(hidden_tan)

    def tangent_band(members):
        return jax.jvp(lambda values_in: attending(values_in, members[1]), (members[0],), (members[2],))[1]
    block_tan = banded(tangent_band, (rolled, wrapped, rolled_tan))
    change_tan = jax.jvp(decoding, (settled,), (backward_roll(block_tan),))[1]
    tangent_field = direction + change_tan.astype(jnp.float32)
    owners = obs_owner[:, 0]
    owner_lon = owners // N_LAT
    owner_lat = owners % N_LAT
    cell_index = obs_site // var_count
    variable = obs_site % var_count
    grid_row = owner_lat * LAT_DEV + cell_index // LON_DEV
    grid_col = owner_lon * LON_DEV + cell_index % LON_DEV
    base_index = ((grid_row * lon_cells + grid_col) * var_count + variable).astype(jnp.int32)
    offsets = (0, var_count, lon_cells * var_count, (lon_cells + 1) * var_count)
    flat_tan = tangent_field.reshape(-1)
    at_obs = obs_weights[:, 0] * flat_tan[base_index + offsets[0]]
    for corner in range(1, 4):
        at_obs = at_obs + obs_weights[:, corner] * flat_tan[base_index + offsets[corner]]
    weighted = obs_precision * at_obs
    gathered_adj = jnp.zeros_like(flat_tan)
    for corner in range(4):
        gathered_adj = gathered_adj.at[base_index + offsets[corner]].add(obs_weights[:, corner] * weighted)
    adjoint_field = gathered_adj.reshape(lat_cells, lon_cells, var_count)
    change_ct = adjoint_field.astype(jnp.bfloat16)
    settled_ct = jax.vjp(decoding, settled)[1](change_ct)[0]
    block_ct = forward_roll(settled_ct)

    def adjoint_band(members):
        return jax.vjp(lambda values_in: attending(values_in, members[1]), members[0])[1](members[2])[0]
    rolled_ct = banded(adjoint_band, (rolled, wrapped, block_ct))
    hidden_ct = backward_roll(rolled_ct)
    state_ct = jax.vjp(embedding, background)[1](hidden_ct)[0]
    return (adjoint_field + state_ct, at_obs)
```

```python
import jax
import jax.numpy as jnp
from jax import lax
from jax.experimental import pallas as pl
from jax.experimental.pallas import tpu as pltpu
from jax.sharding import PartitionSpec as P

HEADS = 16
WLAT = 8
WLON = 16
CELLS = WLAT * WLON
HALF_LAT = WLAT // 2
HALF_LON = WLON // 2
QUARTER = HALF_LAT * HALF_LON
SLOTS = 8
PIECES = 3

eps_norm = 1e-05
eps_head = 1e-06

f32 = jnp.float32
bf16 = jnp.bfloat16

NN = ((1,), (0,))
NT = ((1,), (1,))
TN = ((0,), (0,))

VMEM = pl.BlockSpec(memory_space=pltpu.VMEM)
SMEM = pl.BlockSpec(memory_space=pltpu.SMEM)
ANY = pl.BlockSpec(memory_space=pl.ANY)


def product(left, right, dims):
    return lax.dot_general(left, right, (dims, ((), ())), preferred_element_type=f32)


def parts_of(value, count):
    parts = []
    for _ in range(count):
        part = value.astype(bf16)
        parts.append(part)
        value = value - part.astype(f32)
    return parts


def quadrants(own, lat_piece, lon_piece, far_piece):
    rows = []
    for left, right in ((own, lon_piece), (lat_piece, far_piece)):
        for i in range(HALF_LAT):
            rows.append(left[i * HALF_LON : (i + 1) * HALF_LON])
            rows.append(right[i * HALF_LON : (i + 1) * HALF_LON])
    return jnp.concatenate(rows, axis=0)


def quadrant_of(cells, row, col):
    return jnp.concatenate(
        [cells[(row + i) * WLON + col : (row + i) * WLON + col + HALF_LON] for i in range(HALF_LAT)], axis=0
    )


def centred_rows(values):
    centred = values - jnp.mean(values, axis=-1, keepdims=True)
    scale = lax.rsqrt(jnp.mean(centred * centred, axis=-1, keepdims=True) + eps_norm)
    return centred * scale, scale


def norm_tangent(unit, scale, tangent):
    moved = tangent - jnp.mean(tangent, axis=-1, keepdims=True)
    return scale * (moved - unit * jnp.mean(unit * moved, axis=-1, keepdims=True))


def strips_kernel(background_ref, direction_ref, lat_ref, lon_ref, far_ref):
    for out_ref, row, col in ((lat_ref, 0, HALF_LON), (lon_ref, HALF_LAT, 0), (far_ref, 0, 0)):
        pieces = []
        for source in (background_ref, direction_ref):
            for i in range(HALF_LAT):
                pieces.append(source[row + i, col : col + HALF_LON, :])
        out_ref[...] = jnp.concatenate(pieces, axis=0).astype(bf16)


def slots_of(owners, rows, devices):
    owner_hot = (lax.broadcasted_iota(jnp.int32, (devices, rows), 0) == owners).astype(f32)
    upper = (
        lax.broadcasted_iota(jnp.int32, (rows, rows), 0) <= lax.broadcasted_iota(jnp.int32, (rows, rows), 1)
    ).astype(bf16)
    counted = product(owner_hot.astype(bf16), upper, NN)
    slots = jnp.sum(counted * owner_hot, axis=0, keepdims=True) - 1.0
    return owner_hot, slots


def pack_kernel(owner_ref, site_ref, weights_ref, precision_ref, out_ref, slots_ref):
    rows = owner_ref.shape[1]
    devices = out_ref.shape[0]
    owner_hot, slots = slots_of(owner_ref[...], rows, devices)
    slots_ref[...] = slots
    payload = jnp.concatenate(
        [weights_ref[...], precision_ref[...], site_ref[...].astype(f32), jnp.zeros((2, rows), f32)], axis=0
    )
    owner_hot = owner_hot.astype(bf16)
    spread = jnp.concatenate([jnp.where(slots == float(k), payload, 0.0) for k in range(SLOTS)], axis=0)
    out = jnp.zeros((devices, SLOTS * 8), f32)
    for part in parts_of(spread, PIECES):
        out = out + product(owner_hot, part, NT)
    out_ref[...] = out


def unpack_kernel(owner_ref, slots_ref, returned_ref, out_ref):
    rows = owner_ref.shape[1]
    devices = returned_ref.shape[0]
    owner_hot = (lax.broadcasted_iota(jnp.int32, (devices, rows), 0) == owner_ref[...]).astype(bf16)
    picked = jnp.zeros((SLOTS, rows), f32)
    for part in parts_of(returned_ref[...], PIECES):
        picked = picked + product(part, owner_hot, TN)
    slot_hot = lax.broadcasted_iota(jnp.int32, (SLOTS, rows), 0).astype(f32) == slots_ref[...]
    out_ref[...] = jnp.sum(jnp.where(slot_hot, picked, 0.0), axis=0, keepdims=True)


def forward_kernel(
    lat_ref,
    logit_ref,
    background_ref,
    direction_ref,
    lat_piece,
    lon_piece,
    far_piece,
    embed_ref,
    gain_ref,
    decode_gain_ref,
    decode_ref,
    qkv_hbm,
    outw_hbm,
    lat_out,
    lon_out,
    far_out,
    own_out,
    hidden_out,
    block_out,
    unit_q_out,
    unit_k_out,
    scale_q_out,
    scale_k_out,
    value_out,
    probs_out,
    qkv_ref,
    outw_ref,
    packed_ref,
    mixed_ref,
    sems,
):
    width = embed_ref.shape[1]
    chunk = 512
    copies = []
    chunks = []
    for group in range(width // chunk):
        for third in range(3):
            columns = pl.ds(third * width + group * chunk, chunk)
            chunks.append(columns)
            copies.append(
                pltpu.make_async_copy(qkv_hbm.at[:, columns], qkv_ref.at[:, columns], sems.at[len(copies)])
            )
    copies.append(pltpu.make_async_copy(outw_hbm, outw_ref, sems.at[len(copies)]))
    for copy in copies:
        copy.start()

    states = []
    for number, source in enumerate((background_ref, direction_ref)):
        own = jnp.concatenate([source[HALF_LAT + i, HALF_LON:, :] for i in range(HALF_LAT)], axis=0)
        part = slice(number * QUARTER, (number + 1) * QUARTER)
        received = [piece[part, :].astype(f32) for piece in (lat_piece, lon_piece, far_piece)]
        states.append(quadrants(own, *received))
    states = jnp.concatenate(states, axis=0).astype(bf16)
    hidden = product(states, embed_ref[...], NN).astype(bf16)
    hidden_out[...] = hidden[:CELLS]
    hidden = hidden.astype(f32)
    unit, scale = centred_rows(hidden[:CELLS])
    moved = norm_tangent(unit, scale, hidden[CELLS:])
    gain = gain_ref[...]
    normed = jnp.concatenate([unit * gain, moved * gain], axis=0).astype(bf16)

    lane = lax.broadcasted_iota(jnp.int32, (1, 128), 1)
    first = lane < 64
    same_head = (
        (lax.broadcasted_iota(jnp.int32, (128, 128), 0) < 64) == (lax.broadcasted_iota(jnp.int32, (128, 128), 1) < 64)
    ).astype(bf16)
    low_q = lax.broadcasted_iota(jnp.int32, (CELLS, CELLS), 0) < CELLS // 2
    low_k = lax.broadcasted_iota(jnp.int32, (CELLS, CELLS), 1) < CELLS // 2
    allowed = jnp.logical_or(low_q == low_k, lat_ref[0] == 0).astype(f32)

    for group in range(width // chunk):
        for third in range(3):
            number = group * 3 + third
            copies[number].wait()
            packed_ref[:, chunks[number]] = product(normed, qkv_ref[:, chunks[number]], NN)
        for pair in range(group * chunk // 128, (group + 1) * chunk // 128):
            here = pl.ds(pair * 128, 128)
            units = []
            for third, unit_out, scale_out in ((0, unit_q_out, scale_q_out), (1, unit_k_out, scale_k_out)):
                both = packed_ref[:, pl.ds(third * width + pair * 128, 128)]
                raw, raw_tan = both[:CELLS], both[CELLS:]
                head_scale = lax.rsqrt(product((raw * raw).astype(bf16), same_head, NN) + eps_head)
                unit = raw * head_scale
                along = product((unit * raw_tan).astype(bf16), same_head, NN)
                unit_tan = head_scale * (raw_tan - unit * along)
                scale_out[:, here] = head_scale
                unit = unit.astype(bf16)
                unit_out[:, here] = unit
                units.append((unit, unit_tan.astype(bf16)))
            (query, query_tan), (key, key_tan) = units
            both = packed_ref[:, pl.ds(2 * width + pair * 128, 128)].astype(bf16)
            value, value_tan = both[:CELLS], both[CELLS:]
            value_out[:, here] = value
            stacked = jnp.concatenate([value, value_tan], axis=0)
            crossed = jnp.concatenate([key_tan, key], axis=1)
            results = []
            for side in range(2):
                head = pair * 2 + side
                mine = first if side == 0 else jnp.logical_not(first)
                zero = jnp.zeros((), bf16)
                query_here = jnp.where(mine, query, zero)
                query_tan_here = jnp.where(mine, query_tan, zero)
                logit = logit_ref[head]
                scores = product(query_here, key, NT)
                scores_tan = product(jnp.concatenate([query_here, query_tan_here], axis=1), crossed, NT) * logit
                weights = jnp.exp(scores * logit) * allowed
                probs = weights * (1.0 / jnp.sum(weights, axis=-1, keepdims=True))
                probs_tan = probs * (scores_tan - jnp.sum(probs * scores_tan, axis=-1, keepdims=True))
                probs = probs.astype(bf16)
                probs_out[head] = probs
                results.append(
                    (
                        product(probs, value, NN),
                        product(jnp.concatenate([probs_tan.astype(bf16), probs], axis=1), stacked, NN),
                    )
                )
            for number, rows in ((0, pl.ds(0, CELLS)), (1, pl.ds(CELLS, CELLS))):
                mixed_ref[rows, here] = jnp.where(first, results[0][number], results[1][number]).astype(bf16)

    copies[-1].wait()
    update = product(mixed_ref[...], outw_ref[...], NN)
    block = (hidden + update).astype(bf16)
    block_out[...] = block[:CELLS]
    block = block.astype(f32)
    unit, scale = centred_rows(block[:CELLS])
    moved = norm_tangent(unit, scale, block[CELLS:])
    change = product((moved * decode_gain_ref[...]).astype(bf16), decode_ref[...], NT)
    lat_out[...] = quadrant_of(change, HALF_LAT, 0).astype(bf16)
    lon_out[...] = quadrant_of(change, 0, HALF_LON).astype(bf16)
    far_out[...] = quadrant_of(change, HALF_LAT, HALF_LON).astype(bf16)
    own_out[...] = quadrant_of(change, 0, 0).astype(bf16)


def observe_kernel(
    direction_ref,
    own_piece,
    lat_piece,
    lon_piece,
    far_piece,
    arrived_ref,
    at_obs_out,
    adjoint_out,
    own_out,
    lat_out,
    lon_out,
    far_out,
):
    var_count = direction_ref.shape[2]
    devices = arrived_ref.shape[0]
    pieces = [piece[...].astype(f32) for piece in (far_piece, lon_piece, lat_piece, own_piece)]
    moved = quadrants(*pieces)
    tangent = jnp.concatenate([direction_ref[i] for i in range(WLAT)], axis=0) + moved
    arrived = jnp.transpose(arrived_ref[...])
    cell_ids = lax.broadcasted_iota(jnp.int32, (CELLS, devices), 0).astype(f32)
    var_ids = lax.broadcasted_iota(jnp.int32, (var_count, devices), 0).astype(f32)
    selectors, var_hots, precisions = [], [], []
    for k in range(SLOTS):
        row = arrived[k * 8 : (k + 1) * 8]
        site = row[5:6]
        cell = jnp.floor((site + 0.5) * (1.0 / var_count))
        variable = site - cell * var_count
        selector = jnp.zeros((CELLS, devices), f32)
        for corner, offset in enumerate((0, 1, WLON, WLON + 1)):
            selector = selector + jnp.where(cell_ids == cell + float(offset), row[corner : corner + 1], 0.0)
        selectors.append(selector)
        var_hots.append((var_ids == variable).astype(f32))
        precisions.append(row[4:5])
    selector = jnp.concatenate(selectors, axis=1)
    var_hot = jnp.concatenate(var_hots, axis=1)
    precision = jnp.concatenate(precisions, axis=1)
    selector_parts = parts_of(selector, 2)
    tangent_parts = parts_of(tangent, 3)
    picked = product(tangent_parts[0], selector_parts[0], TN)
    for left, right in ((1, 0), (0, 1), (2, 0)):
        picked = picked + product(tangent_parts[left], selector_parts[right], TN)
    at_obs = jnp.sum(picked * var_hot, axis=0, keepdims=True)
    at_obs_out[...] = jnp.transpose(
        jnp.concatenate([at_obs[:, k * devices : (k + 1) * devices] for k in range(SLOTS)], axis=0)
    )
    spread_parts = parts_of(var_hot * (at_obs * precision), 2)
    adjoint = product(selector_parts[0], spread_parts[0], NT)
    for left, right in ((1, 0), (0, 1)):
        adjoint = adjoint + product(selector_parts[left], spread_parts[right], NT)
    for i in range(WLAT):
        adjoint_out[i] = adjoint[i * WLON : (i + 1) * WLON]
    own_out[...] = quadrant_of(adjoint, HALF_LAT, HALF_LON).astype(bf16)
    lat_out[...] = quadrant_of(adjoint, 0, HALF_LON).astype(bf16)
    lon_out[...] = quadrant_of(adjoint, HALF_LAT, 0).astype(bf16)
    far_out[...] = quadrant_of(adjoint, 0, 0).astype(bf16)


def adjoint_kernel(
    logit_ref,
    own_piece,
    lat_piece,
    lon_piece,
    far_piece,
    embed_ref,
    gain_ref,
    decode_gain_ref,
    decode_ref,
    hidden_ref,
    block_ref,
    unit_q_ref,
    unit_k_ref,
    scale_q_ref,
    scale_k_ref,
    value_ref,
    probs_ref,
    qkv_hbm,
    outw_hbm,
    own_out,
    lat_out,
    lon_out,
    far_out,
    qkv_ref,
    outw_ref,
    packed_ref,
    sems,
):
    width = embed_ref.shape[1]
    out_copy = pltpu.make_async_copy(outw_hbm, outw_ref, sems.at[0])
    qkv_copy = pltpu.make_async_copy(qkv_hbm, qkv_ref, sems.at[1])
    out_copy.start()
    qkv_copy.start()

    change = quadrants(*[piece[...].astype(f32) for piece in (own_piece, lat_piece, lon_piece, far_piece)])
    unit, scale = centred_rows(block_ref[...].astype(f32))
    normed_ct = product(change.astype(bf16), decode_ref[...], NN).astype(bf16).astype(f32) * decode_gain_ref[...]
    block_ct = norm_tangent(unit, scale, normed_ct).astype(bf16)
    out_copy.wait()
    mixed_ct = product(block_ct, outw_ref[...], NT).astype(bf16)

    lane = lax.broadcasted_iota(jnp.int32, (1, 128), 1)
    first = lane < 64
    same_head = (
        (lax.broadcasted_iota(jnp.int32, (128, 128), 0) < 64) == (lax.broadcasted_iota(jnp.int32, (128, 128), 1) < 64)
    ).astype(bf16)
    for pair in range(width // 128):
        here = pl.ds(pair * 128, 128)
        query, key, value = unit_q_ref[:, here], unit_k_ref[:, here], value_ref[:, here]
        mixed_here = mixed_ct[:, pair * 128 : (pair + 1) * 128]
        results = []
        for side in range(2):
            head = pair * 2 + side
            mine = first if side == 0 else jnp.logical_not(first)
            probs = probs_ref[head]
            probs_ct = product(jnp.where(mine, mixed_here, jnp.zeros((), bf16)), value, NT)
            probs_wide = probs.astype(f32)
            scores_ct = probs_wide * (probs_ct - jnp.sum(probs_wide * probs_ct, axis=-1, keepdims=True))
            scores_ct = (scores_ct * logit_ref[head]).astype(bf16)
            results.append(
                (product(scores_ct, key, NN), product(scores_ct, query, TN), product(probs, mixed_here, TN))
            )
        for third, unit_ref, scale_ref in ((0, unit_q_ref, scale_q_ref), (1, unit_k_ref, scale_k_ref)):
            unit_ct = jnp.where(first, results[0][third], results[1][third])
            unit_here = unit_ref[:, here].astype(f32)
            along = product((unit_here * unit_ct).astype(bf16), same_head, NN)
            packed_ref[:, pl.ds(third * width + pair * 128, 128)] = (
                scale_ref[:, here] * (unit_ct - unit_here * along)
            ).astype(bf16)
        packed_ref[:, pl.ds(2 * width + pair * 128, 128)] = jnp.where(first, results[0][2], results[1][2]).astype(bf16)

    qkv_copy.wait()
    normed_ct = product(packed_ref[...], qkv_ref[...], NT).astype(bf16).astype(f32) * gain_ref[...]
    unit, scale = centred_rows(hidden_ref[...].astype(f32))
    hidden_ct = (norm_tangent(unit, scale, normed_ct) + block_ct.astype(f32)).astype(bf16)
    state = product(hidden_ct, embed_ref[...], NT)
    lat_out[...] = quadrant_of(state, HALF_LAT, 0).astype(bf16)
    lon_out[...] = quadrant_of(state, 0, HALF_LON).astype(bf16)
    far_out[...] = quadrant_of(state, HALF_LAT, HALF_LON).astype(bf16)
    own_out[...] = quadrant_of(state, 0, 0).astype(bf16)


def finish_kernel(adjoint_ref, own_piece, lat_piece, lon_piece, far_piece, out_ref):
    pieces = [piece[...].astype(f32) for piece in (far_piece, lon_piece, lat_piece, own_piece)]
    moved = quadrants(*pieces)
    for i in range(WLAT):
        out_ref[i] = adjoint_ref[i] + moved[i * WLON : (i + 1) * WLON]


def shape(dims, dtype):
    return jax.ShapeDtypeStruct(dims, dtype)


def exchanged(lat_piece, lon_piece, far_piece, steps):
    lat_count, lon_count = lax.axis_size("lat"), lax.axis_size("lon")
    lat_piece = lax.ppermute(lat_piece, "lat", [(i, (i + steps) % lat_count) for i in range(lat_count)])
    lon_piece = lax.ppermute(lon_piece, "lon", [(i, (i + steps) % lon_count) for i in range(lon_count)])
    pairs = [
        (i * lat_count + j, ((i + steps) % lon_count) * lat_count + (j + steps) % lat_count)
        for i in range(lon_count)
        for j in range(lat_count)
    ]
    far_piece = lax.ppermute(far_piece, ("lon", "lat"), pairs)
    return lat_piece, lon_piece, far_piece


def per_device(
    background,
    direction,
    obs_owner,
    obs_site,
    obs_weights,
    obs_precision,
    embed_weight,
    attn_gain,
    qkv_weight,
    logit_scale,
    out_weight,
    decode_gain,
    decode_weight,
):
    var_count = background.shape[2]
    width = embed_weight.shape[1]
    devices = lax.axis_size("lat") * lax.axis_size("lon")
    obs_rows = obs_site.shape[0]
    last_band = (lax.axis_index("lat") == lax.axis_size("lat") - 1).astype(jnp.int32).reshape(1)
    gain = attn_gain.reshape(1, width)
    decode_gain = decode_gain.reshape(1, width)
    decode_rows = decode_weight.T
    params = pltpu.CompilerParams(vmem_limit_bytes=40 * 1024 * 1024)
    quarter = shape((QUARTER, var_count), bf16)

    strips = pl.pallas_call(
        strips_kernel,
        out_shape=[shape((2 * QUARTER, var_count), bf16)] * 3,
        in_specs=[VMEM] * 2,
        out_specs=[VMEM] * 3,
        name="strips",
    )(background, direction)
    strips = exchanged(*strips, -1)

    owners = obs_owner.reshape(1, obs_rows)
    outgoing, slots = pl.pallas_call(
        pack_kernel,
        out_shape=[shape((devices, SLOTS * 8), f32), shape((1, obs_rows), f32)],
        in_specs=[VMEM] * 4,
        out_specs=[VMEM] * 2,
        name="pack",
    )(owners, obs_site.reshape(1, obs_rows), obs_weights.T, obs_precision.reshape(1, obs_rows))
    arrived = lax.all_to_all(outgoing, ("lon", "lat"), split_axis=0, concat_axis=0, tiled=True)

    wide = shape((CELLS, width), bf16)
    wide_long = shape((CELLS, width), f32)
    lat_piece, lon_piece, far_piece, own_piece, *kept = pl.pallas_call(
        forward_kernel,
        out_shape=[quarter] * 4
        + [wide, wide, wide, wide, wide_long, wide_long, wide, shape((HEADS, CELLS, CELLS), bf16)],
        in_specs=[SMEM] * 2 + [VMEM] * 9 + [ANY] * 2,
        out_specs=[VMEM] * 12,
        scratch_shapes=[
            pltpu.VMEM((width, 3 * width), bf16),
            pltpu.VMEM((width, width), bf16),
            pltpu.VMEM((2 * CELLS, 3 * width), f32),
            pltpu.VMEM((2 * CELLS, width), bf16),
            pltpu.SemaphoreType.DMA((3 * (width // 512) + 1,)),
        ],
        compiler_params=params,
        cost_estimate=pl.CostEstimate(flops=2_500_000_000, bytes_accessed=10_000_000, transcendentals=300_000),
        name="forward",
    )(
        last_band,
        logit_scale,
        background,
        direction,
        *strips,
        embed_weight,
        gain,
        decode_gain,
        decode_rows,
        qkv_weight,
        out_weight,
    )
    lat_piece, lon_piece, far_piece = exchanged(lat_piece, lon_piece, far_piece, 1)

    at_obs, adjoint_field, own_piece, lat_piece, lon_piece, far_piece = pl.pallas_call(
        observe_kernel,
        out_shape=[shape((devices, SLOTS), f32), shape(background.shape, f32)] + [quarter] * 4,
        in_specs=[VMEM] * 6,
        out_specs=[VMEM] * 6,
        name="observe",
    )(direction, own_piece, lat_piece, lon_piece, far_piece, arrived)
    lat_piece, lon_piece, far_piece = exchanged(lat_piece, lon_piece, far_piece, -1)
    returned = lax.all_to_all(at_obs, ("lon", "lat"), split_axis=0, concat_axis=0, tiled=True)

    own_piece, lat_piece, lon_piece, far_piece = pl.pallas_call(
        adjoint_kernel,
        out_shape=[quarter] * 4,
        in_specs=[SMEM] + [VMEM] * 16 + [ANY] * 2,
        out_specs=[VMEM] * 4,
        scratch_shapes=[
            pltpu.VMEM((width, 3 * width), bf16),
            pltpu.VMEM((width, width), bf16),
            pltpu.VMEM((CELLS, 3 * width), bf16),
            pltpu.SemaphoreType.DMA((2,)),
        ],
        compiler_params=params,
        cost_estimate=pl.CostEstimate(flops=1_500_000_000, bytes_accessed=10_000_000, transcendentals=300_000),
        name="adjoint",
    )(
        logit_scale,
        own_piece,
        lat_piece,
        lon_piece,
        far_piece,
        embed_weight,
        gain,
        decode_gain,
        decode_rows,
        *kept,
        qkv_weight,
        out_weight,
    )
    lat_piece, lon_piece, far_piece = exchanged(lat_piece, lon_piece, far_piece, 1)

    hvp = pl.pallas_call(
        finish_kernel,
        out_shape=shape(background.shape, f32),
        in_specs=[VMEM] * 5,
        out_specs=VMEM,
        name="finish",
    )(adjoint_field, own_piece, lat_piece, lon_piece, far_piece)
    obs_increment = pl.pallas_call(
        unpack_kernel,
        out_shape=shape((1, obs_rows), f32),
        in_specs=[VMEM] * 3,
        out_specs=VMEM,
        name="unpack",
    )(owners, slots, returned)
    return (hvp, obs_increment.reshape(obs_rows))


def solution(mesh):
    in_specs = (
        P("lat", "lon", None),
        P("lat", "lon", None),
        P(("lon", "lat"), None),
        P(("lon", "lat")),
        P(("lon", "lat"), None),
        P(("lon", "lat")),
        P(),
        P(),
        P(),
        P(),
        P(),
        P(),
        P(),
    )
    out_specs = (P("lat", "lon", None), P(("lon", "lat")))
    return jax.shard_map(
        per_device, mesh=mesh, in_specs=in_specs, out_specs=out_specs, check_vma=False
    )
```

```python
import jax
import jax.numpy as jnp
from jax import lax
from jax.experimental import pallas as pl
from jax.experimental.pallas import tpu as pltpu
from jax.sharding import PartitionSpec as P

HEADS = 16
WLAT = 8
WLON = 16
CELLS = WLAT * WLON
HALF_LAT = WLAT // 2
HALF_LON = WLON // 2
QUARTER = HALF_LAT * HALF_LON
SLOTS = 8
PIECES = 3

eps_norm = 1e-05
eps_head = 1e-06

f32 = jnp.float32
bf16 = jnp.bfloat16

NN = ((1,), (0,))
NT = ((1,), (1,))
TN = ((0,), (0,))

VMEM = pl.BlockSpec(memory_space=pltpu.VMEM)
SMEM = pl.BlockSpec(memory_space=pltpu.SMEM)
ANY = pl.BlockSpec(memory_space=pl.ANY)


def product(left, right, dims):
    return lax.dot_general(left, right, (dims, ((), ())), preferred_element_type=f32)


def parts_of(value, count):
    parts = []
    for _ in range(count):
        part = value.astype(bf16)
        parts.append(part)
        value = value - part.astype(f32)
    return parts


def quadrants(own, lat_piece, lon_piece, far_piece):
    rows = []
    for left, right in ((own, lon_piece), (lat_piece, far_piece)):
        for i in range(HALF_LAT):
            rows.append(left[i * HALF_LON : (i + 1) * HALF_LON])
            rows.append(right[i * HALF_LON : (i + 1) * HALF_LON])
    return jnp.concatenate(rows, axis=0)


def quadrant_of(cells, row, col):
    return jnp.concatenate(
        [cells[(row + i) * WLON + col : (row + i) * WLON + col + HALF_LON] for i in range(HALF_LAT)], axis=0
    )


def centred_rows(values):
    centred = values - jnp.mean(values, axis=-1, keepdims=True)
    scale = lax.rsqrt(jnp.mean(centred * centred, axis=-1, keepdims=True) + eps_norm)
    return centred * scale, scale


def norm_tangent(unit, scale, tangent):
    moved = tangent - jnp.mean(tangent, axis=-1, keepdims=True)
    return scale * (moved - unit * jnp.mean(unit * moved, axis=-1, keepdims=True))


def strips_kernel(background_ref, direction_ref, lat_ref, lon_ref, far_ref):
    for out_ref, row, col in ((lat_ref, 0, HALF_LON), (lon_ref, HALF_LAT, 0), (far_ref, 0, 0)):
        pieces = []
        for source in (background_ref, direction_ref):
            for i in range(HALF_LAT):
                pieces.append(source[row + i, col : col + HALF_LON, :])
        out_ref[...] = jnp.concatenate(pieces, axis=0).astype(bf16)


def slots_of(owners, rows, devices):
    owner_hot = (lax.broadcasted_iota(jnp.int32, (devices, rows), 0) == owners).astype(f32)
    upper = (
        lax.broadcasted_iota(jnp.int32, (rows, rows), 0) <= lax.broadcasted_iota(jnp.int32, (rows, rows), 1)
    ).astype(bf16)
    counted = product(owner_hot.astype(bf16), upper, NN)
    slots = jnp.sum(counted * owner_hot, axis=0, keepdims=True) - 1.0
    return owner_hot, slots


def pack_kernel(owner_ref, site_ref, weights_ref, precision_ref, out_ref, slots_ref):
    rows = owner_ref.shape[1]
    devices = out_ref.shape[0]
    owner_hot, slots = slots_of(owner_ref[...], rows, devices)
    slots_ref[...] = slots
    payload = jnp.concatenate(
        [weights_ref[...], precision_ref[...], site_ref[...].astype(f32), jnp.zeros((2, rows), f32)], axis=0
    )
    owner_hot = owner_hot.astype(bf16)
    spread = jnp.concatenate([jnp.where(slots == float(k), payload, 0.0) for k in range(SLOTS)], axis=0)
    out = jnp.zeros((devices, SLOTS * 8), f32)
    for part in parts_of(spread, PIECES):
        out = out + product(owner_hot, part, NT)
    out_ref[...] = out


def unpack_kernel(owner_ref, slots_ref, returned_ref, out_ref):
    rows = owner_ref.shape[1]
    devices = returned_ref.shape[0]
    owner_hot = (lax.broadcasted_iota(jnp.int32, (devices, rows), 0) == owner_ref[...]).astype(bf16)
    picked = jnp.zeros((SLOTS, rows), f32)
    for part in parts_of(returned_ref[...], PIECES):
        picked = picked + product(part, owner_hot, TN)
    slot_hot = lax.broadcasted_iota(jnp.int32, (SLOTS, rows), 0).astype(f32) == slots_ref[...]
    out_ref[...] = jnp.sum(jnp.where(slot_hot, picked, 0.0), axis=0, keepdims=True)


def forward_kernel(
    lat_ref,
    logit_ref,
    background_ref,
    direction_ref,
    lat_piece,
    lon_piece,
    far_piece,
    embed_ref,
    gain_ref,
    decode_gain_ref,
    decode_ref,
    qkv_hbm,
    outw_hbm,
    lat_out,
    lon_out,
    far_out,
    own_out,
    hidden_out,
    block_out,
    unit_q_out,
    unit_k_out,
    scale_q_out,
    scale_k_out,
    value_out,
    probs_out,
    qkv_ref,
    outw_ref,
    packed_ref,
    mixed_ref,
    sems,
):
    width = embed_ref.shape[1]
    chunk = 512
    copies = []
    chunks = []
    for group in range(width // chunk):
        for third in range(3):
            columns = pl.ds(third * width + group * chunk, chunk)
            chunks.append(columns)
            copies.append(
                pltpu.make_async_copy(qkv_hbm.at[:, columns], qkv_ref.at[:, columns], sems.at[len(copies)])
            )
    copies.append(pltpu.make_async_copy(outw_hbm, outw_ref, sems.at[len(copies)]))
    for copy in copies:
        copy.start()

    states = []
    for number, source in enumerate((background_ref, direction_ref)):
        own = jnp.concatenate([source[HALF_LAT + i, HALF_LON:, :] for i in range(HALF_LAT)], axis=0)
        part = slice(number * QUARTER, (number + 1) * QUARTER)
        received = [piece[part, :].astype(f32) for piece in (lat_piece, lon_piece, far_piece)]
        states.append(quadrants(own, *received))
    states = jnp.concatenate(states, axis=0).astype(bf16)
    hidden = product(states, embed_ref[...], NN).astype(bf16)
    hidden_out[...] = hidden[:CELLS]
    hidden = hidden.astype(f32)
    unit, scale = centred_rows(hidden[:CELLS])
    moved = norm_tangent(unit, scale, hidden[CELLS:])
    gain = gain_ref[...]
    normed = jnp.concatenate([unit * gain, moved * gain], axis=0).astype(bf16)

    lane = lax.broadcasted_iota(jnp.int32, (1, 128), 1)
    first = lane < 64
    same_head = (
        (lax.broadcasted_iota(jnp.int32, (128, 128), 0) < 64) == (lax.broadcasted_iota(jnp.int32, (128, 128), 1) < 64)
    ).astype(bf16)
    low_q = lax.broadcasted_iota(jnp.int32, (CELLS, CELLS), 0) < CELLS // 2
    low_k = lax.broadcasted_iota(jnp.int32, (CELLS, CELLS), 1) < CELLS // 2
    allowed = jnp.logical_or(low_q == low_k, lat_ref[0] == 0).astype(f32)

    for group in range(width // chunk):
        for third in range(3):
            number = group * 3 + third
            copies[number].wait()
            packed_ref[:, chunks[number]] = product(normed, qkv_ref[:, chunks[number]], NN)
        for pair in range(group * chunk // 128, (group + 1) * chunk // 128):
            here = pl.ds(pair * 128, 128)
            units = []
            for third, unit_out, scale_out in ((0, unit_q_out, scale_q_out), (1, unit_k_out, scale_k_out)):
                both = packed_ref[:, pl.ds(third * width + pair * 128, 128)]
                raw, raw_tan = both[:CELLS], both[CELLS:]
                head_scale = lax.rsqrt(product((raw * raw).astype(bf16), same_head, NN) + eps_head)
                unit = raw * head_scale
                along = product((unit * raw_tan).astype(bf16), same_head, NN)
                unit_tan = head_scale * (raw_tan - unit * along)
                scale_out[:, here] = head_scale
                unit = unit.astype(bf16)
                unit_out[:, here] = unit
                units.append((unit, unit_tan.astype(bf16)))
            (query, query_tan), (key, key_tan) = units
            both = packed_ref[:, pl.ds(2 * width + pair * 128, 128)].astype(bf16)
            value, value_tan = both[:CELLS], both[CELLS:]
            value_out[:, here] = value
            stacked = jnp.concatenate([value, value_tan], axis=0)
            crossed = jnp.concatenate([key_tan, key], axis=1)
            results = []
            for side in range(2):
                head = pair * 2 + side
                mine = first if side == 0 else jnp.logical_not(first)
                zero = jnp.zeros((), bf16)
                query_here = jnp.where(mine, query, zero)
                query_tan_here = jnp.where(mine, query_tan, zero)
                logit = logit_ref[head]
                scores = product(query_here, key, NT)
                scores_tan = product(jnp.concatenate([query_here, query_tan_here], axis=1), crossed, NT) * logit
                weights = jnp.exp(scores * logit) * allowed
                probs = weights * (1.0 / jnp.sum(weights, axis=-1, keepdims=True))
                probs_tan = probs * (scores_tan - jnp.sum(probs * scores_tan, axis=-1, keepdims=True))
                probs = probs.astype(bf16)
                probs_out[head] = probs
                results.append(
                    (
                        product(probs, value, NN),
                        product(jnp.concatenate([probs_tan.astype(bf16), probs], axis=1), stacked, NN),
                    )
                )
            for number, rows in ((0, pl.ds(0, CELLS)), (1, pl.ds(CELLS, CELLS))):
                mixed_ref[rows, here] = jnp.where(first, results[0][number], results[1][number]).astype(bf16)

    copies[-1].wait()
    update = product(mixed_ref[...], outw_ref[...], NN)
    block = (hidden + update).astype(bf16)
    block_out[...] = block[:CELLS]
    block = block.astype(f32)
    unit, scale = centred_rows(block[:CELLS])
    moved = norm_tangent(unit, scale, block[CELLS:])
    change = product((moved * decode_gain_ref[...]).astype(bf16), decode_ref[...], NT)
    lat_out[...] = quadrant_of(change, HALF_LAT, 0).astype(bf16)
    lon_out[...] = quadrant_of(change, 0, HALF_LON).astype(bf16)
    far_out[...] = quadrant_of(change, HALF_LAT, HALF_LON).astype(bf16)
    own_out[...] = quadrant_of(change, 0, 0).astype(bf16)


def observe_kernel(
    direction_ref,
    own_piece,
    lat_piece,
    lon_piece,
    far_piece,
    arrived_ref,
    at_obs_out,
    adjoint_out,
    own_out,
    lat_out,
    lon_out,
    far_out,
):
    var_count = direction_ref.shape[2]
    devices = arrived_ref.shape[0]
    pieces = [piece[...].astype(f32) for piece in (far_piece, lon_piece, lat_piece, own_piece)]
    moved = quadrants(*pieces)
    tangent = jnp.concatenate([direction_ref[i] for i in range(WLAT)], axis=0) + moved
    arrived = jnp.transpose(arrived_ref[...])
    cell_ids = lax.broadcasted_iota(jnp.int32, (CELLS, devices), 0).astype(f32)
    var_ids = lax.broadcasted_iota(jnp.int32, (var_count, devices), 0).astype(f32)
    selectors, var_hots, precisions = [], [], []
    for k in range(SLOTS):
        row = arrived[k * 8 : (k + 1) * 8]
        site = row[5:6]
        cell = jnp.floor((site + 0.5) * (1.0 / var_count))
        variable = site - cell * var_count
        selector = jnp.zeros((CELLS, devices), f32)
        for corner, offset in enumerate((0, 1, WLON, WLON + 1)):
            selector = selector + jnp.where(cell_ids == cell + float(offset), row[corner : corner + 1], 0.0)
        selectors.append(selector)
        var_hots.append((var_ids == variable).astype(f32))
        precisions.append(row[4:5])
    selector = jnp.concatenate(selectors, axis=1)
    var_hot = jnp.concatenate(var_hots, axis=1)
    precision = jnp.concatenate(precisions, axis=1)
    selector_parts = parts_of(selector, 2)
    tangent_parts = parts_of(tangent, 3)
    picked = product(tangent_parts[0], selector_parts[0], TN)
    for left, right in ((1, 0), (0, 1), (2, 0)):
        picked = picked + product(tangent_parts[left], selector_parts[right], TN)
    at_obs = jnp.sum(picked * var_hot, axis=0, keepdims=True)
    at_obs_out[...] = jnp.transpose(
        jnp.concatenate([at_obs[:, k * devices : (k + 1) * devices] for k in range(SLOTS)], axis=0)
    )
    spread_parts = parts_of(var_hot * (at_obs * precision), 2)
    adjoint = product(selector_parts[0], spread_parts[0], NT)
    for left, right in ((1, 0), (0, 1)):
        adjoint = adjoint + product(selector_parts[left], spread_parts[right], NT)
    for i in range(WLAT):
        adjoint_out[i] = adjoint[i * WLON : (i + 1) * WLON]
    own_out[...] = quadrant_of(adjoint, HALF_LAT, HALF_LON).astype(bf16)
    lat_out[...] = quadrant_of(adjoint, 0, HALF_LON).astype(bf16)
    lon_out[...] = quadrant_of(adjoint, HALF_LAT, 0).astype(bf16)
    far_out[...] = quadrant_of(adjoint, 0, 0).astype(bf16)


def adjoint_kernel(
    logit_ref,
    own_piece,
    lat_piece,
    lon_piece,
    far_piece,
    embed_ref,
    gain_ref,
    decode_gain_ref,
    decode_ref,
    hidden_ref,
    block_ref,
    unit_q_ref,
    unit_k_ref,
    scale_q_ref,
    scale_k_ref,
    value_ref,
    probs_ref,
    qkv_hbm,
    outw_hbm,
    own_out,
    lat_out,
    lon_out,
    far_out,
    qkv_ref,
    outw_ref,
    packed_ref,
    sems,
):
    width = embed_ref.shape[1]
    out_copy = pltpu.make_async_copy(outw_hbm, outw_ref, sems.at[0])
    qkv_copy = pltpu.make_async_copy(qkv_hbm, qkv_ref, sems.at[1])
    out_copy.start()
    qkv_copy.start()

    change = quadrants(*[piece[...].astype(f32) for piece in (own_piece, lat_piece, lon_piece, far_piece)])
    unit, scale = centred_rows(block_ref[...].astype(f32))
    normed_ct = product(change.astype(bf16), decode_ref[...], NN).astype(bf16).astype(f32) * decode_gain_ref[...]
    block_ct = norm_tangent(unit, scale, normed_ct).astype(bf16)
    out_copy.wait()
    mixed_ct = product(block_ct, outw_ref[...], NT).astype(bf16)

    lane = lax.broadcasted_iota(jnp.int32, (1, 128), 1)
    first = lane < 64
    same_head = (
        (lax.broadcasted_iota(jnp.int32, (128, 128), 0) < 64) == (lax.broadcasted_iota(jnp.int32, (128, 128), 1) < 64)
    ).astype(bf16)
    for pair in range(width // 128):
        here = pl.ds(pair * 128, 128)
        query, key, value = unit_q_ref[:, here], unit_k_ref[:, here], value_ref[:, here]
        mixed_here = mixed_ct[:, pair * 128 : (pair + 1) * 128]
        results = []
        for side in range(2):
            head = pair * 2 + side
            mine = first if side == 0 else jnp.logical_not(first)
            probs = probs_ref[head]
            probs_ct = product(jnp.where(mine, mixed_here, jnp.zeros((), bf16)), value, NT)
            probs_wide = probs.astype(f32)
            scores_ct = probs_wide * (probs_ct - jnp.sum(probs_wide * probs_ct, axis=-1, keepdims=True))
            scores_ct = (scores_ct * logit_ref[head]).astype(bf16)
            results.append(
                (product(scores_ct, key, NN), product(scores_ct, query, TN), product(probs, mixed_here, TN))
            )
        for third, unit_ref, scale_ref in ((0, unit_q_ref, scale_q_ref), (1, unit_k_ref, scale_k_ref)):
            unit_ct = jnp.where(first, results[0][third], results[1][third])
            unit_here = unit_ref[:, here].astype(f32)
            along = product((unit_here * unit_ct).astype(bf16), same_head, NN)
            packed_ref[:, pl.ds(third * width + pair * 128, 128)] = (
                scale_ref[:, here] * (unit_ct - unit_here * along)
            ).astype(bf16)
        packed_ref[:, pl.ds(2 * width + pair * 128, 128)] = jnp.where(first, results[0][2], results[1][2]).astype(bf16)

    qkv_copy.wait()
    normed_ct = product(packed_ref[...], qkv_ref[...], NT).astype(bf16).astype(f32) * gain_ref[...]
    unit, scale = centred_rows(hidden_ref[...].astype(f32))
    hidden_ct = (norm_tangent(unit, scale, normed_ct) + block_ct.astype(f32)).astype(bf16)
    state = product(hidden_ct, embed_ref[...], NT)
    lat_out[...] = quadrant_of(state, HALF_LAT, 0).astype(bf16)
    lon_out[...] = quadrant_of(state, 0, HALF_LON).astype(bf16)
    far_out[...] = quadrant_of(state, HALF_LAT, HALF_LON).astype(bf16)
    own_out[...] = quadrant_of(state, 0, 0).astype(bf16)


def finish_kernel(adjoint_ref, own_piece, lat_piece, lon_piece, far_piece, out_ref):
    pieces = [piece[...].astype(f32) for piece in (far_piece, lon_piece, lat_piece, own_piece)]
    moved = quadrants(*pieces)
    for i in range(WLAT):
        out_ref[i] = adjoint_ref[i] + moved[i * WLON : (i + 1) * WLON]


def shape(dims, dtype):
    return jax.ShapeDtypeStruct(dims, dtype)


def exchanged(lat_piece, lon_piece, far_piece, steps):
    lat_count, lon_count = lax.axis_size("lat"), lax.axis_size("lon")
    lat_piece = lax.ppermute(lat_piece, "lat", [(i, (i + steps) % lat_count) for i in range(lat_count)])
    lon_piece = lax.ppermute(lon_piece, "lon", [(i, (i + steps) % lon_count) for i in range(lon_count)])
    pairs = [
        (i * lat_count + j, ((i + steps) % lon_count) * lat_count + (j + steps) % lat_count)
        for i in range(lon_count)
        for j in range(lat_count)
    ]
    far_piece = lax.ppermute(far_piece, ("lon", "lat"), pairs)
    return lat_piece, lon_piece, far_piece


def per_device(
    background,
    direction,
    obs_owner,
    obs_site,
    obs_weights,
    obs_precision,
    embed_weight,
    attn_gain,
    qkv_weight,
    logit_scale,
    out_weight,
    decode_gain,
    decode_weight,
):
    var_count = background.shape[2]
    width = embed_weight.shape[1]
    devices = lax.axis_size("lat") * lax.axis_size("lon")
    obs_rows = obs_site.shape[0]
    last_band = (lax.axis_index("lat") == lax.axis_size("lat") - 1).astype(jnp.int32).reshape(1)
    gain = attn_gain.reshape(1, width)
    decode_gain = decode_gain.reshape(1, width)
    decode_rows = decode_weight.T
    quarter = shape((QUARTER, var_count), bf16)

    strips = pl.pallas_call(
        strips_kernel,
        out_shape=[shape((2 * QUARTER, var_count), bf16)] * 3,
        in_specs=[VMEM] * 2,
        out_specs=[VMEM] * 3,
        name="strips",
    )(background, direction)
    strips = exchanged(*strips, -1)

    owners = obs_owner.reshape(1, obs_rows)
    outgoing, slots = pl.pallas_call(
        pack_kernel,
        out_shape=[shape((devices, SLOTS * 8), f32), shape((1, obs_rows), f32)],
        in_specs=[VMEM] * 4,
        out_specs=[VMEM] * 2,
        name="pack",
    )(owners, obs_site.reshape(1, obs_rows), obs_weights.T, obs_precision.reshape(1, obs_rows))
    arrived = lax.all_to_all(outgoing, ("lon", "lat"), split_axis=0, concat_axis=0, tiled=True)

    wide = shape((CELLS, width), bf16)
    wide_long = shape((CELLS, width), f32)
    lat_piece, lon_piece, far_piece, own_piece, *kept = pl.pallas_call(
        forward_kernel,
        out_shape=[quarter] * 4
        + [wide, wide, wide, wide, wide_long, wide_long, wide, shape((HEADS, CELLS, CELLS), bf16)],
        in_specs=[SMEM] * 2 + [VMEM] * 9 + [ANY] * 2,
        out_specs=[VMEM] * 12,
        scratch_shapes=[
            pltpu.VMEM((width, 3 * width), bf16),
            pltpu.VMEM((width, width), bf16),
            pltpu.VMEM((2 * CELLS, 3 * width), f32),
            pltpu.VMEM((2 * CELLS, width), bf16),
            pltpu.SemaphoreType.DMA((3 * (width // 512) + 1,)),
        ],
        cost_estimate=pl.CostEstimate(flops=2_500_000_000, bytes_accessed=10_000_000, transcendentals=300_000),
        name="forward",
    )(
        last_band,
        logit_scale,
        background,
        direction,
        *strips,
        embed_weight,
        gain,
        decode_gain,
        decode_rows,
        qkv_weight,
        out_weight,
    )
    lat_piece, lon_piece, far_piece = exchanged(lat_piece, lon_piece, far_piece, 1)

    at_obs, adjoint_field, own_piece, lat_piece, lon_piece, far_piece = pl.pallas_call(
        observe_kernel,
        out_shape=[shape((devices, SLOTS), f32), shape(background.shape, f32)] + [quarter] * 4,
        in_specs=[VMEM] * 6,
        out_specs=[VMEM] * 6,
        name="observe",
    )(direction, own_piece, lat_piece, lon_piece, far_piece, arrived)
    lat_piece, lon_piece, far_piece = exchanged(lat_piece, lon_piece, far_piece, -1)
    returned = lax.all_to_all(at_obs, ("lon", "lat"), split_axis=0, concat_axis=0, tiled=True)

    own_piece, lat_piece, lon_piece, far_piece = pl.pallas_call(
        adjoint_kernel,
        out_shape=[quarter] * 4,
        in_specs=[SMEM] + [VMEM] * 16 + [ANY] * 2,
        out_specs=[VMEM] * 4,
        scratch_shapes=[
            pltpu.VMEM((width, 3 * width), bf16),
            pltpu.VMEM((width, width), bf16),
            pltpu.VMEM((CELLS, 3 * width), bf16),
            pltpu.SemaphoreType.DMA((2,)),
        ],
        cost_estimate=pl.CostEstimate(flops=1_500_000_000, bytes_accessed=10_000_000, transcendentals=300_000),
        name="adjoint",
    )(
        logit_scale,
        own_piece,
        lat_piece,
        lon_piece,
        far_piece,
        embed_weight,
        gain,
        decode_gain,
        decode_rows,
        *kept,
        qkv_weight,
        out_weight,
    )
    lat_piece, lon_piece, far_piece, returned = lax.optimization_barrier((lat_piece, lon_piece, far_piece, returned))
    lat_piece, lon_piece, far_piece = exchanged(lat_piece, lon_piece, far_piece, 1)

    hvp = pl.pallas_call(
        finish_kernel,
        out_shape=shape(background.shape, f32),
        in_specs=[VMEM] * 5,
        out_specs=VMEM,
        name="finish",
    )(adjoint_field, own_piece, lat_piece, lon_piece, far_piece)
    obs_increment = pl.pallas_call(
        unpack_kernel,
        out_shape=shape((1, obs_rows), f32),
        in_specs=[VMEM] * 3,
        out_specs=VMEM,
        name="unpack",
    )(owners, slots, returned)
    return (hvp, obs_increment.reshape(obs_rows))


def solution(mesh):
    in_specs = (
        P("lat", "lon", None),
        P("lat", "lon", None),
        P(("lon", "lat"), None),
        P(("lon", "lat")),
        P(("lon", "lat"), None),
        P(("lon", "lat")),
        P(),
        P(),
        P(),
        P(),
        P(),
        P(),
        P(),
    )
    out_specs = (P("lat", "lon", None), P(("lon", "lat")))
    return jax.shard_map(
        per_device, mesh=mesh, in_specs=in_specs, out_specs=out_specs, check_vma=False
    )
```

```python
import jax
import jax.numpy as jnp
from jax import lax
from jax.experimental import pallas as pl
from jax.experimental.pallas import tpu as pltpu
from jax.sharding import PartitionSpec as P

HEADS = 16
WLAT = 8
WLON = 16
CELLS = WLAT * WLON
HALF_LAT = WLAT // 2
HALF_LON = WLON // 2
QUARTER = HALF_LAT * HALF_LON
SLOTS = 8
PIECES = 3
QUAD = 256

eps_norm = 1e-05
eps_head = 1e-06

f32 = jnp.float32
bf16 = jnp.bfloat16

NN = ((1,), (0,))
NT = ((1,), (1,))
TN = ((0,), (0,))

VMEM = pl.BlockSpec(memory_space=pltpu.VMEM)
SMEM = pl.BlockSpec(memory_space=pltpu.SMEM)
ANY = pl.BlockSpec(memory_space=pl.ANY)


def product(left, right, dims):
    return lax.dot_general(left, right, (dims, ((), ())), preferred_element_type=f32)


def parts_of(value, count):
    parts = []
    for _ in range(count):
        part = value.astype(bf16)
        parts.append(part)
        value = value - part.astype(f32)
    return parts


def quadrants(top_left, bottom_left, top_right, bottom_right):
    rows = []
    for left, right in ((top_left, top_right), (bottom_left, bottom_right)):
        for i in range(HALF_LAT):
            rows.append(left[i * HALF_LON : (i + 1) * HALF_LON])
            rows.append(right[i * HALF_LON : (i + 1) * HALF_LON])
    return jnp.concatenate(rows, axis=0)


def quadrant_of(cells, row, col):
    return jnp.concatenate(
        [cells[(row + i) * WLON + col : (row + i) * WLON + col + HALF_LON] for i in range(HALF_LAT)], axis=0
    )


def normed_rows(values):
    centred = values - jnp.mean(values, axis=-1, keepdims=True)
    scale = lax.rsqrt(jnp.mean(centred * centred, axis=-1, keepdims=True) + eps_norm)
    return centred * scale, scale


def norm_tangent(unit, scale, tangent):
    moved = tangent - jnp.mean(tangent, axis=-1, keepdims=True)
    return scale * (moved - unit * jnp.mean(unit * tangent, axis=-1, keepdims=True))


def normed_with_tangent(values, tangent):
    centred = values - jnp.mean(values, axis=-1, keepdims=True)
    moved = tangent - jnp.mean(tangent, axis=-1, keepdims=True)
    spread = jnp.mean(centred * centred, axis=-1, keepdims=True)
    along = jnp.mean(centred * moved, axis=-1, keepdims=True)
    scale = lax.rsqrt(spread + eps_norm)
    unit = centred * scale
    return unit, scale * (moved - unit * (scale * along))


def same_head_block():
    rows = lax.broadcasted_iota(jnp.int32, (QUAD, QUAD), 0) >> 6
    return (rows == lax.broadcasted_iota(jnp.int32, (QUAD, QUAD), 1) >> 6).astype(bf16)


def by_head(pair, first):
    zero = jnp.zeros((), pair.dtype)
    return jnp.concatenate([jnp.where(first, pair, zero), jnp.where(first, zero, pair)], axis=0)


def halves(value):
    return value[:, :CELLS], value[:, CELLS:]


def slots_of(owners, rows, devices):
    owner_hot = (lax.broadcasted_iota(jnp.int32, (devices, rows), 0) == owners).astype(f32)
    upper = (
        lax.broadcasted_iota(jnp.int32, (rows, rows), 0) <= lax.broadcasted_iota(jnp.int32, (rows, rows), 1)
    ).astype(bf16)
    counted = product(owner_hot.astype(bf16), upper, NN)
    slots = jnp.sum(counted * owner_hot, axis=0, keepdims=True) - 1.0
    return owner_hot, slots


def prepare_kernel(
    background_ref,
    direction_ref,
    owner_ref,
    site_ref,
    weights_ref,
    precision_ref,
    lat_out,
    lon_out,
    far_out,
    out_ref,
    slots_ref,
):
    for piece_out, row, col in ((lat_out, 0, HALF_LON), (lon_out, HALF_LAT, 0), (far_out, 0, 0)):
        pieces = []
        for source in (background_ref, direction_ref):
            for i in range(HALF_LAT):
                pieces.append(source[row + i, col : col + HALF_LON, :])
        piece_out[...] = jnp.concatenate(pieces, axis=0).astype(bf16)
    rows = owner_ref.shape[1]
    devices = out_ref.shape[0]
    owner_hot, slots = slots_of(owner_ref[...], rows, devices)
    slots_ref[...] = slots
    payload = jnp.concatenate(
        [weights_ref[...], precision_ref[...], site_ref[...].astype(f32), jnp.zeros((2, rows), f32)], axis=0
    )
    owner_hot = owner_hot.astype(bf16)
    spread = jnp.concatenate([jnp.where(slots == float(k), payload, 0.0) for k in range(SLOTS)], axis=0)
    out = jnp.zeros((devices, SLOTS * 8), f32)
    for part in parts_of(spread, PIECES):
        out = out + product(owner_hot, part, NT)
    out_ref[...] = out


def unpack_kernel(owner_ref, slots_ref, returned_ref, out_ref):
    rows = owner_ref.shape[1]
    devices = returned_ref.shape[0]
    owner_hot = (lax.broadcasted_iota(jnp.int32, (devices, rows), 0) == owner_ref[...]).astype(bf16)
    picked = jnp.zeros((SLOTS, rows), f32)
    for part in parts_of(returned_ref[...], PIECES):
        picked = picked + product(part, owner_hot, TN)
    slot_hot = lax.broadcasted_iota(jnp.int32, (SLOTS, rows), 0).astype(f32) == slots_ref[...]
    out_ref[...] = jnp.sum(jnp.where(slot_hot, picked, 0.0), axis=0, keepdims=True)


def forward_kernel(
    band_hbm,
    logit_hbm,
    background_hbm,
    direction_hbm,
    lat_hbm,
    lon_hbm,
    far_hbm,
    embed_hbm,
    gain_hbm,
    decode_gain_hbm,
    decode_hbm,
    qkv_hbm,
    outw_hbm,
    lat_out,
    lon_out,
    far_out,
    own_out,
    hidden_hbm,
    block_hbm,
    unit_q_hbm,
    unit_k_hbm,
    scale_q_hbm,
    scale_k_hbm,
    value_hbm,
    probs_hbm,
    band_ref,
    logit_ref,
    background_ref,
    direction_ref,
    lat_piece,
    lon_piece,
    far_piece,
    embed_ref,
    gain_ref,
    decode_gain_ref,
    decode_ref,
    qkv_ref,
    outw_ref,
    hidden_ref,
    block_ref,
    unit_q_ref,
    unit_k_ref,
    scale_q_ref,
    scale_k_ref,
    value_ref,
    probs_ref,
    mixed_ref,
    sems_in,
    sems_out,
):
    width = embed_ref.shape[1]
    quads = width // QUAD
    count = 0

    def fetch(source, target):
        nonlocal count
        copy = pltpu.make_async_copy(source, target, sems_in.at[count])
        copy.start()
        count += 1
        return copy

    first_needed = [
        fetch(*pair)
        for pair in (
            (lat_hbm, lat_piece),
            (lon_hbm, lon_piece),
            (far_hbm, far_piece),
            (background_hbm, background_ref),
            (direction_hbm, direction_ref),
            (embed_hbm, embed_ref),
            (gain_hbm, gain_ref),
            (band_hbm, band_ref),
            (logit_hbm, logit_ref),
        )
    ]
    fetched = []
    for quad in range(quads):
        for third in range(3):
            columns = pl.ds(third * width + quad * QUAD, QUAD)
            fetched.append(fetch(qkv_hbm.at[:, columns], qkv_ref.at[:, columns]))
    last_needed = [
        fetch(*pair) for pair in ((outw_hbm, outw_ref), (decode_gain_hbm, decode_gain_ref), (decode_hbm, decode_ref))
    ]
    kept = []

    def keep(source, target):
        copy = pltpu.make_async_copy(source, target, sems_out.at[len(kept)])
        copy.start()
        kept.append(copy)

    lane = lax.broadcasted_iota(jnp.int32, (1, 128), 1)
    first = lane < 64
    same_head = same_head_block()
    for copy in first_needed:
        copy.wait()
    low_q = lax.broadcasted_iota(jnp.int32, (CELLS, CELLS), 0) < CELLS // 2
    low_k = lax.broadcasted_iota(jnp.int32, (CELLS, CELLS), 1) < CELLS // 2
    allowed = jnp.where(low_q == low_k, 1.0, 1.0 - band_ref[...])
    logits = logit_ref[...]
    states = []
    for number, source in enumerate((background_ref, direction_ref)):
        own = jnp.concatenate([source[HALF_LAT + i, HALF_LON:, :] for i in range(HALF_LAT)], axis=0)
        part = slice(number * QUARTER, (number + 1) * QUARTER)
        received = [piece[part, :].astype(f32) for piece in (lat_piece, lon_piece, far_piece)]
        states.append(quadrants(own, *received))
    states = jnp.concatenate(states, axis=0).astype(bf16)
    hidden = product(states, embed_ref[...], NN).astype(bf16)
    hidden_ref[...] = hidden
    keep(hidden_ref.at[:CELLS], hidden_hbm)
    hidden = hidden.astype(f32)
    gain = gain_ref[...]
    normed = jnp.concatenate(
        [part * gain for part in normed_with_tangent(hidden[:CELLS], hidden[CELLS:])], axis=0
    ).astype(bf16)

    def project(quad):
        here = pl.ds(quad * QUAD, QUAD)
        packed = []
        for third in range(3):
            packed.append(product(normed, qkv_ref[:, pl.ds(third * width + quad * QUAD, QUAD)], NN))
        raw = jnp.concatenate([packed[0][:CELLS], packed[1][:CELLS]], axis=0)
        raw_tan = jnp.concatenate([packed[0][CELLS:], packed[1][CELLS:]], axis=0)
        scale = lax.rsqrt(product((raw * raw).astype(bf16), same_head, NN) + eps_head)
        unit = raw * scale
        along = product((unit * raw_tan).astype(bf16), same_head, NN)
        unit_tan = (scale * (raw_tan - unit * along)).astype(bf16)
        unit = unit.astype(bf16)
        value = packed[2].astype(bf16)
        scale_q_ref[:, here] = scale[:CELLS]
        scale_k_ref[:, here] = scale[CELLS:]
        unit_q_ref[:, here] = unit[:CELLS]
        unit_k_ref[:, here] = unit[CELLS:]
        value_ref[:, here] = value[:CELLS]
        for source, target in (
            (scale_q_ref, scale_q_hbm),
            (scale_k_ref, scale_k_hbm),
            (unit_q_ref, unit_q_hbm),
            (unit_k_ref, unit_k_hbm),
            (value_ref, value_hbm),
        ):
            keep(source.at[:, here], target.at[:, here])
        return unit, unit_tan, value

    def attend(quad, unit, unit_tan, value):
        for side in range(2):
            pair = quad * 2 + side
            lanes = slice(side * 128, (side + 1) * 128)
            query, key = unit[:CELLS, lanes], by_head(unit[CELLS:, lanes], first)
            query_tan, key_tan = unit_tan[:CELLS, lanes], by_head(unit_tan[CELLS:, lanes], first)
            values = jnp.concatenate(
                [by_head(value[:CELLS, lanes], first), by_head(value[CELLS:, lanes], first)], axis=1
            )
            scores = product(query, key, NT)
            scores_tan = product(
                jnp.concatenate([query, query_tan], axis=1), jnp.concatenate([key_tan, key], axis=1), NT
            )
            probs, probs_tan = [], []
            for half, (score, score_tan) in enumerate(zip(halves(scores), halves(scores_tan))):
                head = pair * 2 + half
                logit = logits[:, head : head + 1]
                weights = jnp.exp(score * logit) * allowed
                prob = weights * (1.0 / jnp.sum(weights, axis=-1, keepdims=True))
                score_tan = score_tan * logit
                prob_tan = prob * (score_tan - jnp.sum(prob * score_tan, axis=-1, keepdims=True))
                probs.append(prob.astype(bf16))
                probs_tan.append(prob_tan.astype(bf16))
            probs = jnp.concatenate(probs, axis=1)
            probs_ref[pair] = probs
            mixed, mixed_tan = halves(product(probs, values, NN))
            mixed_tan = mixed_tan + product(jnp.concatenate(probs_tan, axis=1), values[:, :128], NN)
            columns = pl.ds(pair * 128, 128)
            mixed_ref[:CELLS, columns] = mixed.astype(bf16)
            mixed_ref[CELLS:, columns] = mixed_tan.astype(bf16)
        pairs = pl.ds(quad * 2, 2)
        keep(probs_ref.at[pairs], probs_hbm.at[pairs])

    for copy in fetched[0:3]:
        copy.wait()
    vals0 = project(0)
    for copy in fetched[3:6]:
        copy.wait()
    vals1 = project(1)
    attend(0, *vals0)
    for copy in fetched[6:9]:
        copy.wait()
    vals2 = project(2)
    attend(1, *vals1)
    for copy in fetched[9:12]:
        copy.wait()
    vals3 = project(3)
    attend(2, *vals2)
    attend(3, *vals3)

    for copy in last_needed:
        copy.wait()
    block = (hidden_ref[...].astype(f32) + product(mixed_ref[...], outw_ref[...], NN)).astype(bf16)
    block_ref[...] = block
    keep(block_ref.at[:CELLS], block_hbm)
    block = block.astype(f32)
    moved = normed_with_tangent(block[:CELLS], block[CELLS:])[1]
    change = product((moved * decode_gain_ref[...]).astype(bf16), decode_ref[...], NT)
    lat_out[...] = quadrant_of(change, HALF_LAT, 0).astype(bf16)
    lon_out[...] = quadrant_of(change, 0, HALF_LON).astype(bf16)
    far_out[...] = quadrant_of(change, HALF_LAT, HALF_LON).astype(bf16)
    own_out[...] = quadrant_of(change, 0, 0).astype(bf16)
    for copy in kept:
        copy.wait()


def observe_kernel(
    direction_ref,
    own_piece,
    lat_piece,
    lon_piece,
    far_piece,
    arrived_ref,
    at_obs_out,
    adjoint_out,
    own_out,
    lat_out,
    lon_out,
    far_out,
):
    var_count = direction_ref.shape[2]
    devices = arrived_ref.shape[0]
    pieces = [piece[...].astype(f32) for piece in (far_piece, lon_piece, lat_piece, own_piece)]
    moved = quadrants(*pieces)
    tangent = jnp.concatenate([direction_ref[i] for i in range(WLAT)], axis=0) + moved
    arrived = jnp.transpose(arrived_ref[...])
    cell_ids = lax.broadcasted_iota(jnp.int32, (CELLS, devices), 0).astype(f32)
    var_ids = lax.broadcasted_iota(jnp.int32, (var_count, devices), 0).astype(f32)
    selectors, var_hots, precisions = [], [], []
    for k in range(SLOTS):
        row = arrived[k * 8 : (k + 1) * 8]
        site = row[5:6]
        cell = jnp.floor((site + 0.5) * (1.0 / var_count))
        variable = site - cell * var_count
        selector = jnp.zeros((CELLS, devices), f32)
        for corner, offset in enumerate((0, 1, WLON, WLON + 1)):
            selector = selector + jnp.where(cell_ids == cell + float(offset), row[corner : corner + 1], 0.0)
        selectors.append(selector)
        var_hots.append((var_ids == variable).astype(f32))
        precisions.append(row[4:5])
    selector = jnp.concatenate(selectors, axis=1)
    var_hot = jnp.concatenate(var_hots, axis=1)
    precision = jnp.concatenate(precisions, axis=1)
    selector_parts = parts_of(selector, 2)
    tangent_parts = parts_of(tangent, 3)
    picked = product(tangent_parts[0], selector_parts[0], TN)
    for left, right in ((1, 0), (0, 1), (2, 0)):
        picked = picked + product(tangent_parts[left], selector_parts[right], TN)
    at_obs = jnp.sum(picked * var_hot, axis=0, keepdims=True)
    at_obs_out[...] = jnp.transpose(
        jnp.concatenate([at_obs[:, k * devices : (k + 1) * devices] for k in range(SLOTS)], axis=0)
    )
    spread_parts = parts_of(var_hot * (at_obs * precision), 2)
    adjoint = product(selector_parts[0], spread_parts[0], NT)
    for left, right in ((1, 0), (0, 1)):
        adjoint = adjoint + product(selector_parts[left], spread_parts[right], NT)
    for i in range(WLAT):
        adjoint_out[i] = adjoint[i * WLON : (i + 1) * WLON]
    own_out[...] = quadrant_of(adjoint, HALF_LAT, HALF_LON).astype(bf16)
    lat_out[...] = quadrant_of(adjoint, 0, HALF_LON).astype(bf16)
    lon_out[...] = quadrant_of(adjoint, HALF_LAT, 0).astype(bf16)
    far_out[...] = quadrant_of(adjoint, 0, 0).astype(bf16)


def adjoint_kernel(
    logit_ref,
    own_piece,
    lat_piece,
    lon_piece,
    far_piece,
    decode_gain_ref,
    decode_ref,
    block_ref,
    embed_hbm,
    gain_hbm,
    hidden_hbm,
    unit_q_hbm,
    unit_k_hbm,
    scale_q_hbm,
    scale_k_hbm,
    value_hbm,
    probs_hbm,
    qkv_hbm,
    outw_hbm,
    own_out,
    lat_out,
    lon_out,
    far_out,
    embed_ref,
    gain_ref,
    hidden_ref,
    unit_q_ref,
    unit_k_ref,
    scale_q_ref,
    scale_k_ref,
    value_ref,
    probs_ref,
    qkv_ref,
    outw_ref,
    packed_ref,
    sems,
):
    width = embed_ref.shape[1]
    quads = width // QUAD
    fetched = []
    for source, target in (
        (outw_hbm, outw_ref),
        (value_hbm, value_ref),
        (probs_hbm, probs_ref),
        (unit_q_hbm, unit_q_ref),
        (unit_k_hbm, unit_k_ref),
        (scale_q_hbm, scale_q_ref),
        (scale_k_hbm, scale_k_ref),
        (qkv_hbm, qkv_ref),
        (gain_hbm, gain_ref),
        (hidden_hbm, hidden_ref),
        (embed_hbm, embed_ref),
    ):
        copy = pltpu.make_async_copy(source, target, sems.at[len(fetched)])
        copy.start()
        fetched.append(copy)

    change = quadrants(*[piece[...].astype(f32) for piece in (own_piece, lat_piece, lon_piece, far_piece)])
    unit, scale = normed_rows(block_ref[...].astype(f32))
    normed_ct = product(change.astype(bf16), decode_ref[...], NN).astype(bf16).astype(f32) * decode_gain_ref[...]
    block_ct = norm_tangent(unit, scale, normed_ct).astype(bf16)
    fetched[0].wait()
    mixed_ct = product(block_ct, outw_ref[...], NT).astype(bf16)

    lane = lax.broadcasted_iota(jnp.int32, (1, 128), 1)
    first = lane < 64
    same_head = same_head_block()
    logits = logit_ref[...]
    for copy in fetched[1:7]:
        copy.wait()
    for quad in range(quads):
        cotangents = []
        for side in range(2):
            pair = quad * 2 + side
            here = pl.ds(pair * 128, 128)
            query, key, value = unit_q_ref[:, here], unit_k_ref[:, here], value_ref[:, here]
            mixed_here = mixed_ct[:, pair * 128 : (pair + 1) * 128]
            probs = halves(probs_ref[pair])
            scores_ct = []
            for prob, prob_ct in zip(probs, halves(product(mixed_here, by_head(value, first), NT))):
                prob = prob.astype(f32)
                scores_ct.append((prob * (prob_ct - jnp.sum(prob * prob_ct, axis=-1, keepdims=True))).astype(bf16))
            head = pair * 2
            logit = jnp.where(first, logits[:, head : head + 1], logits[:, head + 1 : head + 2])
            query_ct = product(jnp.concatenate(scores_ct, axis=1), by_head(key, first), NN) * logit
            key_ct = product(jnp.concatenate(scores_ct, axis=0), by_head(query, first), TN) * logit
            value_ct = product(jnp.concatenate(probs, axis=0), by_head(mixed_here, first), TN)
            packed_ref[:, pl.ds(2 * width + pair * 128, 128)] = value_ct.astype(bf16)
            cotangents.append(jnp.concatenate([query_ct, key_ct], axis=0))
        unit_ct = jnp.concatenate(cotangents, axis=1)
        here = pl.ds(quad * QUAD, QUAD)
        units = jnp.concatenate([unit_q_ref[:, here], unit_k_ref[:, here]], axis=0).astype(f32)
        along = product((units * unit_ct).astype(bf16), same_head, NN)
        rest = unit_ct - units * along
        packed_ref[:, here] = (scale_q_ref[:, here] * rest[:CELLS]).astype(bf16)
        packed_ref[:, pl.ds(width + quad * QUAD, QUAD)] = (scale_k_ref[:, here] * rest[CELLS:]).astype(bf16)

    for copy in fetched[7:]:
        copy.wait()
    unit, scale = normed_rows(hidden_ref[...].astype(f32))
    normed_ct = product(packed_ref[...], qkv_ref[...], NT).astype(bf16).astype(f32) * gain_ref[...]
    hidden_ct = (norm_tangent(unit, scale, normed_ct) + block_ct.astype(f32)).astype(bf16)
    state = product(hidden_ct, embed_ref[...], NT)
    lat_out[...] = quadrant_of(state, HALF_LAT, 0).astype(bf16)
    lon_out[...] = quadrant_of(state, 0, HALF_LON).astype(bf16)
    far_out[...] = quadrant_of(state, HALF_LAT, HALF_LON).astype(bf16)
    own_out[...] = quadrant_of(state, 0, 0).astype(bf16)


def finish_kernel(adjoint_ref, own_piece, lat_piece, lon_piece, far_piece, out_ref):
    pieces = [piece[...].astype(f32) for piece in (far_piece, lon_piece, lat_piece, own_piece)]
    moved = quadrants(*pieces)
    for i in range(WLAT):
        out_ref[i] = adjoint_ref[i] + moved[i * WLON : (i + 1) * WLON]


def shape(dims, dtype):
    return jax.ShapeDtypeStruct(dims, dtype)


def exchanged(lat_piece, lon_piece, far_piece, steps):
    lat_count, lon_count = lax.axis_size("lat"), lax.axis_size("lon")
    lat_piece = lax.ppermute(lat_piece, "lat", [(i, (i + steps) % lat_count) for i in range(lat_count)])
    lon_piece = lax.ppermute(lon_piece, "lon", [(i, (i + steps) % lon_count) for i in range(lon_count)])
    pairs = [
        (i * lat_count + j, ((i + steps) % lon_count) * lat_count + (j + steps) % lat_count)
        for i in range(lon_count)
        for j in range(lat_count)
    ]
    far_piece = lax.ppermute(far_piece, ("lon", "lat"), pairs)
    return lat_piece, lon_piece, far_piece


def run_forward(
    last_band, logit_scale, background, direction, strips, embed_weight, gain, decode_gain, decode_rows, qkv_weight, out_weight
):
    width = embed_weight.shape[1]
    quarter = shape((QUARTER, background.shape[2]), bf16)
    wide = shape((CELLS, width), bf16)
    wide_long = shape((CELLS, width), f32)
    kept = [wide, wide, wide, wide, wide_long, wide_long, wide, shape((HEADS // 2, CELLS, 2 * CELLS), bf16)]
    inputs = (last_band, logit_scale, background, direction, *strips, embed_weight, gain, decode_gain, decode_rows, qkv_weight, out_weight)
    both = pltpu.VMEM((2 * CELLS, width), bf16)
    return pl.pallas_call(
        forward_kernel,
        out_shape=[quarter] * 4 + kept,
        in_specs=[ANY] * 13,
        out_specs=[VMEM] * 4 + [ANY] * 8,
        scratch_shapes=[pltpu.VMEM(item.shape, item.dtype) for item in inputs]
        + [both, both]
        + [pltpu.VMEM(item.shape, item.dtype) for item in kept[2:]]
        + [both, pltpu.SemaphoreType.DMA((12 + 3 * (width // QUAD),)), pltpu.SemaphoreType.DMA((2 + 6 * (width // QUAD),))],
        cost_estimate=pl.CostEstimate(flops=2_500_000_000, bytes_accessed=10_000_000, transcendentals=300_000),
        name="forward",
    )(*inputs)


def run_observe(direction, pieces, arrived):
    quarter = shape(pieces[0].shape, bf16)
    devices = arrived.shape[0]
    return pl.pallas_call(
        observe_kernel,
        out_shape=[shape((devices, SLOTS), f32), shape(direction.shape, f32)] + [quarter] * 4,
        in_specs=[VMEM] * 6,
        out_specs=[VMEM] * 6,
        name="observe",
    )(direction, *pieces, arrived)


def run_adjoint(logit_scale, pieces, embed_weight, gain, decode_gain, decode_rows, kept, qkv_weight, out_weight):
    hidden, block, *attention = kept
    width = embed_weight.shape[1]
    late = (embed_weight, gain, hidden, *attention, qkv_weight, out_weight)
    return pl.pallas_call(
        adjoint_kernel,
        out_shape=[shape(pieces[0].shape, bf16)] * 4,
        in_specs=[VMEM] * 8 + [ANY] * len(late),
        out_specs=[VMEM] * 4,
        scratch_shapes=[pltpu.VMEM(item.shape, item.dtype) for item in late]
        + [pltpu.VMEM((CELLS, 3 * width), bf16), pltpu.SemaphoreType.DMA((len(late),))],
        cost_estimate=pl.CostEstimate(flops=1_500_000_000, bytes_accessed=10_000_000, transcendentals=300_000),
        name="adjoint",
    )(logit_scale, *pieces, decode_gain, decode_rows, block, *late)


def per_device(
    background,
    direction,
    obs_owner,
    obs_site,
    obs_weights,
    obs_precision,
    embed_weight,
    attn_gain,
    qkv_weight,
    logit_scale,
    out_weight,
    decode_gain,
    decode_weight,
):
    var_count = background.shape[2]
    width = embed_weight.shape[1]
    devices = lax.axis_size("lat") * lax.axis_size("lon")
    obs_rows = obs_site.shape[0]
    last_band = (lax.axis_index("lat") == lax.axis_size("lat") - 1).astype(f32).reshape(1, 1)
    logit_scale = logit_scale.reshape(1, HEADS)
    gain = attn_gain.reshape(1, width)
    decode_gain = decode_gain.reshape(1, width)
    decode_rows = decode_weight.T

    owners = obs_owner.reshape(1, obs_rows)
    *strips, outgoing, slots = pl.pallas_call(
        prepare_kernel,
        out_shape=[shape((2 * QUARTER, var_count), bf16)] * 3
        + [shape((devices, SLOTS * 8), f32), shape((1, obs_rows), f32)],
        in_specs=[VMEM] * 6,
        out_specs=[VMEM] * 5,
        name="prepare",
    )(
        background,
        direction,
        owners,
        obs_site.reshape(1, obs_rows),
        obs_weights.T,
        obs_precision.reshape(1, obs_rows),
    )
    strips = exchanged(*strips, -1)
    arrived = lax.all_to_all(outgoing, ("lon", "lat"), split_axis=0, concat_axis=0, tiled=True)

    lat_piece, lon_piece, far_piece, own_piece, *kept = run_forward(
        last_band, logit_scale, background, direction, strips, embed_weight, gain, decode_gain, decode_rows, qkv_weight, out_weight
    )
    lat_piece, lon_piece, far_piece = exchanged(lat_piece, lon_piece, far_piece, 1)

    at_obs, adjoint_field, own_piece, lat_piece, lon_piece, far_piece = run_observe(
        direction, (own_piece, lat_piece, lon_piece, far_piece), arrived
    )
    lat_piece, lon_piece, far_piece = exchanged(lat_piece, lon_piece, far_piece, -1)
    returned = lax.all_to_all(at_obs, ("lon", "lat"), split_axis=0, concat_axis=0, tiled=True)

    own_piece, lat_piece, lon_piece, far_piece = run_adjoint(
        logit_scale, (own_piece, lat_piece, lon_piece, far_piece), embed_weight, gain, decode_gain, decode_rows, kept, qkv_weight, out_weight
    )
    lat_piece, lon_piece, far_piece, returned = lax.optimization_barrier((lat_piece, lon_piece, far_piece, returned))
    lat_piece, lon_piece, far_piece = exchanged(lat_piece, lon_piece, far_piece, 1)

    hvp = pl.pallas_call(
        finish_kernel,
        out_shape=shape(background.shape, f32),
        in_specs=[VMEM] * 5,
        out_specs=VMEM,
        name="finish",
    )(adjoint_field, own_piece, lat_piece, lon_piece, far_piece)
    obs_increment = pl.pallas_call(
        unpack_kernel,
        out_shape=shape((1, obs_rows), f32),
        in_specs=[VMEM] * 3,
        out_specs=VMEM,
        name="unpack",
    )(owners, slots, returned)
    return (hvp, obs_increment.reshape(obs_rows))


def solution(mesh):
    in_specs = (
        P("lat", "lon", None),
        P("lat", "lon", None),
        P(("lon", "lat"), None),
        P(("lon", "lat")),
        P(("lon", "lat"), None),
        P(("lon", "lat")),
        P(),
        P(),
        P(),
        P(),
        P(),
        P(),
        P(),
    )
    out_specs = (P("lat", "lon", None), P(("lon", "lat")))
    return jax.shard_map(
        per_device, mesh=mesh, in_specs=in_specs, out_specs=out_specs, check_vma=False
    )
```

```python
import jax
import jax.numpy as jnp
from jax import lax
from jax.experimental import pallas as pl
from jax.experimental.pallas import tpu as pltpu
from jax.sharding import PartitionSpec as P

HEADS = 16
WLAT = 8
WLON = 16
CELLS = WLAT * WLON
HALF_LAT = WLAT // 2
HALF_LON = WLON // 2
QUARTER = HALF_LAT * HALF_LON
SLOTS = 8
PIECES = 3
QUAD = 256

eps_norm = 1e-05
eps_head = 1e-06

f32 = jnp.float32
bf16 = jnp.bfloat16

NN = ((1,), (0,))
NT = ((1,), (1,))
TN = ((0,), (0,))

VMEM = pl.BlockSpec(memory_space=pltpu.VMEM)
SMEM = pl.BlockSpec(memory_space=pltpu.SMEM)
ANY = pl.BlockSpec(memory_space=pl.ANY)


def product(left, right, dims):
    return lax.dot_general(left, right, (dims, ((), ())), preferred_element_type=f32)


def parts_of(value, count):
    parts = []
    for _ in range(count):
        part = value.astype(bf16)
        parts.append(part)
        value = value - part.astype(f32)
    return parts


def quadrants(top_left, bottom_left, top_right, bottom_right):
    rows = []
    for left, right in ((top_left, top_right), (bottom_left, bottom_right)):
        for i in range(HALF_LAT):
            rows.append(left[i * HALF_LON : (i + 1) * HALF_LON])
            rows.append(right[i * HALF_LON : (i + 1) * HALF_LON])
    return jnp.concatenate(rows, axis=0)


def quadrant_of(cells, row, col):
    return jnp.concatenate(
        [cells[(row + i) * WLON + col : (row + i) * WLON + col + HALF_LON] for i in range(HALF_LAT)], axis=0
    )


def normed_rows(values):
    centred = values - jnp.mean(values, axis=-1, keepdims=True)
    scale = lax.rsqrt(jnp.mean(centred * centred, axis=-1, keepdims=True) + eps_norm)
    return centred * scale, scale


def norm_tangent(unit, scale, tangent):
    moved = tangent - jnp.mean(tangent, axis=-1, keepdims=True)
    return scale * (moved - unit * jnp.mean(unit * tangent, axis=-1, keepdims=True))


def normed_with_tangent(values, tangent):
    centred = values - jnp.mean(values, axis=-1, keepdims=True)
    moved = tangent - jnp.mean(tangent, axis=-1, keepdims=True)
    spread = jnp.mean(centred * centred, axis=-1, keepdims=True)
    along = jnp.mean(centred * moved, axis=-1, keepdims=True)
    scale = lax.rsqrt(spread + eps_norm)
    unit = centred * scale
    return unit, scale * (moved - unit * (scale * along))


def same_head_block():
    rows = lax.broadcasted_iota(jnp.int32, (QUAD, QUAD), 0) >> 6
    return (rows == lax.broadcasted_iota(jnp.int32, (QUAD, QUAD), 1) >> 6).astype(bf16)


def by_head(pair, first):
    zero = jnp.zeros((), pair.dtype)
    return jnp.concatenate([jnp.where(first, pair, zero), jnp.where(first, zero, pair)], axis=0)


def halves(value):
    return value[:, :CELLS], value[:, CELLS:]


def slots_of(owners, rows, devices):
    owner_hot = (lax.broadcasted_iota(jnp.int32, (devices, rows), 0) == owners).astype(f32)
    upper = (
        lax.broadcasted_iota(jnp.int32, (rows, rows), 0) <= lax.broadcasted_iota(jnp.int32, (rows, rows), 1)
    ).astype(bf16)
    counted = product(owner_hot.astype(bf16), upper, NN)
    slots = jnp.sum(counted * owner_hot, axis=0, keepdims=True) - 1.0
    return owner_hot, slots


def prepare_kernel(
    background_ref,
    direction_ref,
    owner_ref,
    site_ref,
    weights_ref,
    precision_ref,
    lat_out,
    lon_out,
    far_out,
    out_ref,
    slots_ref,
):
    for piece_out, row, col in ((lat_out, 0, HALF_LON), (lon_out, HALF_LAT, 0), (far_out, 0, 0)):
        pieces = []
        for source in (background_ref, direction_ref):
            for i in range(HALF_LAT):
                pieces.append(source[row + i, col : col + HALF_LON, :])
        piece_out[...] = jnp.concatenate(pieces, axis=0).astype(bf16)
    rows = owner_ref.shape[1]
    devices = out_ref.shape[0]
    owner_hot, slots = slots_of(owner_ref[...], rows, devices)
    slots_ref[...] = slots
    payload = jnp.concatenate(
        [weights_ref[...], precision_ref[...], site_ref[...].astype(f32), jnp.zeros((2, rows), f32)], axis=0
    )
    owner_hot = owner_hot.astype(bf16)
    spread = jnp.concatenate([jnp.where(slots == float(k), payload, 0.0) for k in range(SLOTS)], axis=0)
    out = jnp.zeros((devices, SLOTS * 8), f32)
    for part in parts_of(spread, PIECES):
        out = out + product(owner_hot, part, NT)
    out_ref[...] = out


def unpack_kernel(owner_ref, slots_ref, returned_ref, out_ref):
    rows = owner_ref.shape[1]
    devices = returned_ref.shape[0]
    owner_hot = (lax.broadcasted_iota(jnp.int32, (devices, rows), 0) == owner_ref[...]).astype(bf16)
    picked = jnp.zeros((SLOTS, rows), f32)
    for part in parts_of(returned_ref[...], PIECES):
        picked = picked + product(part, owner_hot, TN)
    slot_hot = lax.broadcasted_iota(jnp.int32, (SLOTS, rows), 0).astype(f32) == slots_ref[...]
    out_ref[...] = jnp.sum(jnp.where(slot_hot, picked, 0.0), axis=0, keepdims=True)


def forward_kernel(
    band_hbm,
    logit_hbm,
    background_hbm,
    direction_hbm,
    lon_hbm,
    far_hbm,
    lat_hbm,
    embed_hbm,
    gain_hbm,
    decode_gain_hbm,
    decode_hbm,
    qkv_hbm,
    outw_hbm,
    lat_out,
    lon_out,
    far_out,
    own_out,
    hidden_hbm,
    block_hbm,
    units_hbm,
    scales_hbm,
    probs_hbm,
    band_ref,
    logit_ref,
    background_ref,
    direction_ref,
    lon_piece,
    far_piece,
    lat_piece,
    embed_ref,
    gain_ref,
    decode_gain_ref,
    decode_ref,
    qkv_ref,
    outw_ref,
    hidden_ref,
    block_ref,
    units_ref,
    scales_ref,
    probs_ref,
    mixed_ref,
    sems_in,
    sems_out,
):
    width = embed_ref.shape[1]
    quads = width // QUAD
    count = 0

    def fetch(source, target):
        nonlocal count
        copy = pltpu.make_async_copy(source, target, sems_in.at[count])
        copy.start()
        count += 1
        return copy

    first_needed = [
        fetch(*pair)
        for pair in (
            (lat_hbm, lat_piece),
            (lon_hbm, lon_piece),
            (far_hbm, far_piece),
            (background_hbm, background_ref),
            (direction_hbm, direction_ref),
            (embed_hbm, embed_ref),
            (gain_hbm, gain_ref),
            (band_hbm, band_ref),
            (logit_hbm, logit_ref),
        )
    ]
    fetched = []
    for half in range(2):
        for third in range(3):
            columns = pl.ds(third * width + half * (width // 2), width // 2)
            fetched.append(fetch(qkv_hbm.at[:, columns], qkv_ref.at[:, columns]))
    last_needed = [
        fetch(*pair) for pair in ((outw_hbm, outw_ref), (decode_gain_hbm, decode_gain_ref), (decode_hbm, decode_ref))
    ]
    kept = []

    def keep(source, target):
        copy = pltpu.make_async_copy(source, target, sems_out.at[len(kept)])
        copy.start()
        kept.append(copy)

    lane = lax.broadcasted_iota(jnp.int32, (1, 128), 1)
    first = lane < 64
    same_head = same_head_block()
    for copy in first_needed:
        copy.wait()
    low_q = lax.broadcasted_iota(jnp.int32, (CELLS, CELLS), 0) < CELLS // 2
    low_k = lax.broadcasted_iota(jnp.int32, (CELLS, CELLS), 1) < CELLS // 2
    allowed = jnp.where(low_q == low_k, 1.0, 1.0 - band_ref[...])
    logits = logit_ref[...]
    states = []
    for number, source in enumerate((background_ref, direction_ref)):
        own = jnp.concatenate([source[HALF_LAT + i, HALF_LON:, :] for i in range(HALF_LAT)], axis=0)
        part = slice(number * QUARTER, (number + 1) * QUARTER)
        received = [piece[part, :].astype(f32) for piece in (lat_piece, lon_piece, far_piece)]
        states.append(quadrants(own, *received))
    states = jnp.concatenate(states, axis=0).astype(bf16)
    hidden = product(states, embed_ref[...], NN).astype(bf16)
    hidden_ref[...] = hidden
    keep(hidden_ref.at[:CELLS], hidden_hbm)
    hidden = hidden.astype(f32)
    gain = gain_ref[...]
    normed = jnp.concatenate(
        [part * gain for part in normed_with_tangent(hidden[:CELLS], hidden[CELLS:])], axis=0
    ).astype(bf16)

    def project(quad):
        here = pl.ds(quad * QUAD, QUAD)
        packed = []
        for third in range(3):
            packed.append(product(normed, qkv_ref[:, pl.ds(third * width + quad * QUAD, QUAD)], NN))
        raw = jnp.concatenate([packed[0][:CELLS], packed[1][:CELLS]], axis=0)
        raw_tan = jnp.concatenate([packed[0][CELLS:], packed[1][CELLS:]], axis=0)
        scale = lax.rsqrt(product((raw * raw).astype(bf16), same_head, NN) + eps_head)
        unit = raw * scale
        along = product((unit * raw_tan).astype(bf16), same_head, NN)
        unit_tan = (scale * (raw_tan - unit * along)).astype(bf16)
        unit = unit.astype(bf16)
        value = packed[2].astype(bf16)
        scales_ref[:, here] = scale
        units_ref[: 2 * CELLS, here] = unit
        units_ref[2 * CELLS :, here] = value[:CELLS]
        return unit, unit_tan, value

    def attend(quad, unit, unit_tan, value):
        for side in range(2):
            pair = quad * 2 + side
            lanes = slice(side * 128, (side + 1) * 128)
            query, key = unit[:CELLS, lanes], by_head(unit[CELLS:, lanes], first)
            query_tan, key_tan = unit_tan[:CELLS, lanes], by_head(unit_tan[CELLS:, lanes], first)
            values = jnp.concatenate(
                [by_head(value[:CELLS, lanes], first), by_head(value[CELLS:, lanes], first)], axis=1
            )
            scores = product(query, key, NT)
            scores_tan = product(
                jnp.concatenate([query, query_tan], axis=1), jnp.concatenate([key_tan, key], axis=1), NT
            )
            probs, probs_tan = [], []
            for half, (score, score_tan) in enumerate(zip(halves(scores), halves(scores_tan))):
                head = pair * 2 + half
                logit = logits[:, head : head + 1]
                weights = jnp.exp(score * logit) * allowed
                prob = weights * (1.0 / jnp.sum(weights, axis=-1, keepdims=True))
                score_tan = score_tan * logit
                prob_tan = prob * (score_tan - jnp.sum(prob * score_tan, axis=-1, keepdims=True))
                probs.append(prob.astype(bf16))
                probs_tan.append(prob_tan.astype(bf16))
            probs = jnp.concatenate(probs, axis=1)
            probs_ref[pair] = probs
            mixed, mixed_tan = halves(product(probs, values, NN))
            mixed_tan = mixed_tan + product(jnp.concatenate(probs_tan, axis=1), values[:, :128], NN)
            columns = pl.ds(pair * 128, 128)
            mixed_ref[:CELLS, columns] = mixed.astype(bf16)
            mixed_ref[CELLS:, columns] = mixed_tan.astype(bf16)

    for copy in fetched[0:3]:
        copy.wait()
    vals0 = project(0)
    vals1 = project(1)
    for copy in fetched[3:6]:
        copy.wait()
    vals2 = project(2)
    vals3 = project(3)
    attend(0, *vals0)
    attend(1, *vals1)
    attend(2, *vals2)
    attend(3, *vals3)

    keep(units_ref, units_hbm)
    keep(scales_ref, scales_hbm)
    keep(probs_ref, probs_hbm)
    for copy in last_needed:
        copy.wait()
    block = (hidden_ref[...].astype(f32) + product(mixed_ref[...], outw_ref[...], NN)).astype(bf16)
    block_ref[...] = block
    keep(block_ref.at[:CELLS], block_hbm)
    block = block.astype(f32)
    moved = normed_with_tangent(block[:CELLS], block[CELLS:])[1]
    change = product((moved * decode_gain_ref[...]).astype(bf16), decode_ref[...], NT)
    lat_out[...] = quadrant_of(change, HALF_LAT, 0).astype(bf16)
    lon_out[...] = quadrant_of(change, 0, HALF_LON).astype(bf16)
    far_out[...] = quadrant_of(change, HALF_LAT, HALF_LON).astype(bf16)
    own_out[...] = quadrant_of(change, 0, 0).astype(bf16)
    for copy in kept:
        copy.wait()


def observe_kernel(
    direction_ref,
    own_piece,
    lon_piece,
    far_piece,
    lat_piece,
    arrived_ref,
    at_obs_out,
    adjoint_out,
    own_out,
    lat_out,
    lon_out,
    far_out,
):
    var_count = direction_ref.shape[2]
    devices = arrived_ref.shape[0]
    pieces = [piece[...].astype(f32) for piece in (far_piece, lon_piece, lat_piece, own_piece)]
    moved = quadrants(*pieces)
    tangent = jnp.concatenate([direction_ref[i] for i in range(WLAT)], axis=0) + moved
    arrived = jnp.transpose(arrived_ref[...])
    cell_ids = lax.broadcasted_iota(jnp.int32, (CELLS, devices), 0).astype(f32)
    var_ids = lax.broadcasted_iota(jnp.int32, (var_count, devices), 0).astype(f32)
    selectors, var_hots, precisions = [], [], []
    for k in range(SLOTS):
        row = arrived[k * 8 : (k + 1) * 8]
        site = row[5:6]
        cell = jnp.floor((site + 0.5) * (1.0 / var_count))
        variable = site - cell * var_count
        selector = jnp.zeros((CELLS, devices), f32)
        for corner, offset in enumerate((0, 1, WLON, WLON + 1)):
            selector = selector + jnp.where(cell_ids == cell + float(offset), row[corner : corner + 1], 0.0)
        selectors.append(selector)
        var_hots.append((var_ids == variable).astype(f32))
        precisions.append(row[4:5])
    selector = jnp.concatenate(selectors, axis=1)
    var_hot = jnp.concatenate(var_hots, axis=1)
    precision = jnp.concatenate(precisions, axis=1)
    selector_parts = parts_of(selector, 2)
    tangent_parts = parts_of(tangent, 3)
    picked = product(tangent_parts[0], selector_parts[0], TN)
    for left, right in ((1, 0), (0, 1), (2, 0)):
        picked = picked + product(tangent_parts[left], selector_parts[right], TN)
    at_obs = jnp.sum(picked * var_hot, axis=0, keepdims=True)
    at_obs_out[...] = jnp.transpose(
        jnp.concatenate([at_obs[:, k * devices : (k + 1) * devices] for k in range(SLOTS)], axis=0)
    )
    spread_parts = parts_of(var_hot * (at_obs * precision), 2)
    adjoint = product(selector_parts[0], spread_parts[0], NT)
    for left, right in ((1, 0), (0, 1)):
        adjoint = adjoint + product(selector_parts[left], spread_parts[right], NT)
    for i in range(WLAT):
        adjoint_out[i] = adjoint[i * WLON : (i + 1) * WLON]
    own_out[...] = quadrant_of(adjoint, HALF_LAT, HALF_LON).astype(bf16)
    lat_out[...] = quadrant_of(adjoint, 0, HALF_LON).astype(bf16)
    lon_out[...] = quadrant_of(adjoint, HALF_LAT, 0).astype(bf16)
    far_out[...] = quadrant_of(adjoint, 0, 0).astype(bf16)


def adjoint_kernel(
    logit_ref,
    own_piece,
    lon_piece,
    far_piece,
    lat_piece,
    decode_gain_ref,
    decode_ref,
    block_ref,
    embed_hbm,
    gain_hbm,
    hidden_hbm,
    units_hbm,
    scales_hbm,
    probs_hbm,
    qkv_hbm,
    outw_hbm,
    own_out,
    lat_out,
    lon_out,
    far_out,
    embed_ref,
    gain_ref,
    hidden_ref,
    units_ref,
    scales_ref,
    probs_ref,
    qkv_ref,
    outw_ref,
    packed_ref,
    sems,
):
    width = embed_ref.shape[1]
    quads = width // QUAD
    fetched = []
    for source, target in (
        (outw_hbm, outw_ref),
        (units_hbm, units_ref),
        (probs_hbm, probs_ref),
        (scales_hbm, scales_ref),
        (qkv_hbm, qkv_ref),
        (gain_hbm, gain_ref),
        (hidden_hbm, hidden_ref),
        (embed_hbm, embed_ref),
    ):
        copy = pltpu.make_async_copy(source, target, sems.at[len(fetched)])
        copy.start()
        fetched.append(copy)

    change = quadrants(*[piece[...].astype(f32) for piece in (own_piece, lat_piece, lon_piece, far_piece)])
    unit, scale = normed_rows(block_ref[...].astype(f32))
    normed_ct = product(change.astype(bf16), decode_ref[...], NN).astype(bf16).astype(f32) * decode_gain_ref[...]
    block_ct = norm_tangent(unit, scale, normed_ct).astype(bf16)
    fetched[0].wait()
    mixed_ct = product(block_ct, outw_ref[...], NT).astype(bf16)

    lane = lax.broadcasted_iota(jnp.int32, (1, 128), 1)
    first = lane < 64
    same_head = same_head_block()
    logits = logit_ref[...]
    for copy in fetched[1:4]:
        copy.wait()
    for quad in range(quads):
        cotangents = []
        for side in range(2):
            pair = quad * 2 + side
            here = pl.ds(pair * 128, 128)
            query, key, value = (units_ref[i * CELLS : (i + 1) * CELLS, here] for i in range(3))
            mixed_here = mixed_ct[:, pair * 128 : (pair + 1) * 128]
            probs = halves(probs_ref[pair])
            scores_ct = []
            for prob, prob_ct in zip(probs, halves(product(mixed_here, by_head(value, first), NT))):
                prob = prob.astype(f32)
                scores_ct.append((prob * (prob_ct - jnp.sum(prob * prob_ct, axis=-1, keepdims=True))).astype(bf16))
            head = pair * 2
            logit = jnp.where(first, logits[:, head : head + 1], logits[:, head + 1 : head + 2])
            query_ct = product(jnp.concatenate(scores_ct, axis=1), by_head(key, first), NN) * logit
            key_ct = product(jnp.concatenate(scores_ct, axis=0), by_head(query, first), TN) * logit
            value_ct = product(jnp.concatenate(probs, axis=0), by_head(mixed_here, first), TN)
            packed_ref[:, pl.ds(2 * width + pair * 128, 128)] = value_ct.astype(bf16)
            cotangents.append(jnp.concatenate([query_ct, key_ct], axis=0))
        unit_ct = jnp.concatenate(cotangents, axis=1)
        here = pl.ds(quad * QUAD, QUAD)
        units = units_ref[: 2 * CELLS, here].astype(f32)
        along = product((units * unit_ct).astype(bf16), same_head, NN)
        raw_ct = (scales_ref[:, here] * (unit_ct - units * along)).astype(bf16)
        packed_ref[:, here] = raw_ct[:CELLS]
        packed_ref[:, pl.ds(width + quad * QUAD, QUAD)] = raw_ct[CELLS:]

    for copy in fetched[4:]:
        copy.wait()
    unit, scale = normed_rows(hidden_ref[...].astype(f32))
    normed_ct = product(packed_ref[...], qkv_ref[...], NT).astype(bf16).astype(f32) * gain_ref[...]
    hidden_ct = (norm_tangent(unit, scale, normed_ct) + block_ct.astype(f32)).astype(bf16)
    state = product(hidden_ct, embed_ref[...], NT)
    lat_out[...] = quadrant_of(state, HALF_LAT, 0).astype(bf16)
    lon_out[...] = quadrant_of(state, 0, HALF_LON).astype(bf16)
    far_out[...] = quadrant_of(state, HALF_LAT, HALF_LON).astype(bf16)
    own_out[...] = quadrant_of(state, 0, 0).astype(bf16)


def shape(dims, dtype):
    return jax.ShapeDtypeStruct(dims, dtype)


def exchanged(lat_piece, lon_piece, far_piece, steps):
    lat_count, lon_count = lax.axis_size("lat"), lax.axis_size("lon")
    lat_piece = lax.ppermute(lat_piece, "lat", [(i, (i + steps) % lat_count) for i in range(lat_count)])
    lon_piece = lax.ppermute(lon_piece, "lon", [(i, (i + steps) % lon_count) for i in range(lon_count)])
    pairs = [
        (i * lat_count + j, ((i + steps) % lon_count) * lat_count + (j + steps) % lat_count)
        for i in range(lon_count)
        for j in range(lat_count)
    ]
    far_piece = lax.ppermute(far_piece, ("lon", "lat"), pairs)
    return lat_piece, lon_piece, far_piece


def run_forward(
    last_band, logit_scale, background, direction, strips, embed_weight, gain, decode_gain, decode_rows, qkv_weight, out_weight
):
    width = embed_weight.shape[1]
    quarter = shape((QUARTER, background.shape[2]), bf16)
    wide = shape((CELLS, width), bf16)
    kept = [
        wide,
        wide,
        shape((3 * CELLS, width), bf16),
        shape((2 * CELLS, width), f32),
        shape((HEADS // 2, CELLS, 2 * CELLS), bf16),
    ]
    inputs = (last_band, logit_scale, background, direction, strips[1], strips[2], strips[0], embed_weight, gain, decode_gain, decode_rows, qkv_weight, out_weight)
    both = pltpu.VMEM((2 * CELLS, width), bf16)
    return pl.pallas_call(
        forward_kernel,
        out_shape=[quarter] * 4 + kept,
        in_specs=[ANY] * 13,
        out_specs=[VMEM] * 4 + [ANY] * 5,
        scratch_shapes=[pltpu.VMEM(item.shape, item.dtype) for item in inputs]
        + [both, both]
        + [pltpu.VMEM(item.shape, item.dtype) for item in kept[2:]]
        + [both, pltpu.SemaphoreType.DMA((18,)), pltpu.SemaphoreType.DMA((5,))],
        cost_estimate=pl.CostEstimate(flops=2_500_000_000, bytes_accessed=10_000_000, transcendentals=300_000),
        name="forward",
    )(*inputs)


def run_observe(direction, pieces, arrived):
    quarter = shape(pieces[0].shape, bf16)
    devices = arrived.shape[0]
    return pl.pallas_call(
        observe_kernel,
        out_shape=[shape((devices, SLOTS), f32), shape(direction.shape, f32)] + [quarter] * 4,
        in_specs=[VMEM] * 6,
        out_specs=[VMEM] * 6,
        name="observe",
    )(direction, *pieces, arrived)


def run_adjoint(logit_scale, pieces, embed_weight, gain, decode_gain, decode_rows, kept, qkv_weight, out_weight):
    hidden, block, *attention = kept
    width = embed_weight.shape[1]
    late = (embed_weight, gain, hidden, *attention, qkv_weight, out_weight)
    return pl.pallas_call(
        adjoint_kernel,
        out_shape=[shape(pieces[0].shape, bf16)] * 4,
        in_specs=[VMEM] * 8 + [ANY] * len(late),
        out_specs=[VMEM] * 4,
        scratch_shapes=[pltpu.VMEM(item.shape, item.dtype) for item in late]
        + [pltpu.VMEM((CELLS, 3 * width), bf16), pltpu.SemaphoreType.DMA((len(late),))],
        cost_estimate=pl.CostEstimate(flops=1_500_000_000, bytes_accessed=10_000_000, transcendentals=300_000),
        name="adjoint",
    )(logit_scale, *pieces, decode_gain, decode_rows, block, *late)


def per_device(
    background,
    direction,
    obs_owner,
    obs_site,
    obs_weights,
    obs_precision,
    embed_weight,
    attn_gain,
    qkv_weight,
    logit_scale,
    out_weight,
    decode_gain,
    decode_weight,
):
    var_count = background.shape[2]
    width = embed_weight.shape[1]
    devices = lax.axis_size("lat") * lax.axis_size("lon")
    obs_rows = obs_site.shape[0]
    last_band = (lax.axis_index("lat") == lax.axis_size("lat") - 1).astype(f32).reshape(1, 1)
    logit_scale = logit_scale.reshape(1, HEADS)
    gain = attn_gain.reshape(1, width)
    decode_gain = decode_gain.reshape(1, width)
    decode_rows = decode_weight.T

    owners = obs_owner.reshape(1, obs_rows)
    *strips, outgoing, slots = pl.pallas_call(
        prepare_kernel,
        out_shape=[shape((2 * QUARTER, var_count), bf16)] * 3
        + [shape((devices, SLOTS * 8), f32), shape((1, obs_rows), f32)],
        in_specs=[VMEM] * 6,
        out_specs=[VMEM] * 5,
        name="prepare",
    )(
        background,
        direction,
        owners,
        obs_site.reshape(1, obs_rows),
        obs_weights.T,
        obs_precision.reshape(1, obs_rows),
    )
    strips = exchanged(*strips, -1)
    arrived = lax.all_to_all(outgoing, ("lon", "lat"), split_axis=0, concat_axis=0, tiled=True)

    lat_piece, lon_piece, far_piece, own_piece, *kept = run_forward(
        last_band, logit_scale, background, direction, strips, embed_weight, gain, decode_gain, decode_rows, qkv_weight, out_weight
    )
    lat_piece, lon_piece, far_piece = exchanged(lat_piece, lon_piece, far_piece, 1)

    at_obs, adjoint_field, own_piece, lat_piece, lon_piece, far_piece = run_observe(
        direction, (own_piece, lon_piece, far_piece, lat_piece), arrived
    )
    lat_piece, lon_piece, far_piece = exchanged(lat_piece, lon_piece, far_piece, -1)
    returned = lax.all_to_all(at_obs, ("lon", "lat"), split_axis=0, concat_axis=0, tiled=True)

    own_piece, lat_piece, lon_piece, far_piece = run_adjoint(
        logit_scale, (own_piece, lon_piece, far_piece, lat_piece), embed_weight, gain, decode_gain, decode_rows, kept, qkv_weight, out_weight
    )
    lat_piece, lon_piece, far_piece, returned = lax.optimization_barrier((lat_piece, lon_piece, far_piece, returned))
    lat_piece, lon_piece, far_piece = exchanged(lat_piece, lon_piece, far_piece, 1)

    hvp = adjoint_field
    for piece, row, col in (
        (lon_piece, HALF_LAT, 0),
        (far_piece, 0, 0),
        (lat_piece, 0, HALF_LON),
        (own_piece, HALF_LAT, HALF_LON),
    ):
        piece = piece.reshape(HALF_LAT, HALF_LON, var_count).astype(f32)
        around = ((row, HALF_LAT - row, 0), (col, HALF_LON - col, 0), (0, 0, 0))
        hvp = hvp + lax.pad(piece, jnp.zeros((), f32), around)
    obs_increment = pl.pallas_call(
        unpack_kernel,
        out_shape=shape((1, obs_rows), f32),
        in_specs=[VMEM] * 3,
        out_specs=VMEM,
        name="unpack",
    )(owners, slots, returned)
    return (hvp, obs_increment.reshape(obs_rows))


def solution(mesh):
    in_specs = (
        P("lat", "lon", None),
        P("lat", "lon", None),
        P(("lon", "lat"), None),
        P(("lon", "lat")),
        P(("lon", "lat"), None),
        P(("lon", "lat")),
        P(),
        P(),
        P(),
        P(),
        P(),
        P(),
        P(),
    )
    out_specs = (P("lat", "lon", None), P(("lon", "lat")))
    return jax.shard_map(
        per_device, mesh=mesh, in_specs=in_specs, out_specs=out_specs, check_vma=False
    )
```

```python
import jax
import jax.numpy as jnp
from jax import lax
from jax.experimental import pallas as pl
from jax.experimental.pallas import tpu as pltpu
from jax.sharding import PartitionSpec as P

HEADS = 16
WLAT = 8
WLON = 16
CELLS = WLAT * WLON
HALF_LAT = WLAT // 2
HALF_LON = WLON // 2
QUARTER = HALF_LAT * HALF_LON
SLOTS = 8
PIECES = 2
QUAD = 256

eps_norm = 1e-05
eps_head = 1e-06

f32 = jnp.float32
bf16 = jnp.bfloat16

NN = ((1,), (0,))
NT = ((1,), (1,))
TN = ((0,), (0,))

VMEM = pl.BlockSpec(memory_space=pltpu.VMEM)
SMEM = pl.BlockSpec(memory_space=pltpu.SMEM)
ANY = pl.BlockSpec(memory_space=pl.ANY)


def product(left, right, dims):
    return lax.dot_general(left, right, (dims, ((), ())), preferred_element_type=f32)


def parts_of(value, count):
    parts = []
    for _ in range(count):
        part = value.astype(bf16)
        parts.append(part)
        value = value - part.astype(f32)
    return parts


def quadrants(top_left, bottom_left, top_right, bottom_right):
    rows = []
    for left, right in ((top_left, top_right), (bottom_left, bottom_right)):
        for i in range(HALF_LAT):
            rows.append(left[i * HALF_LON : (i + 1) * HALF_LON])
            rows.append(right[i * HALF_LON : (i + 1) * HALF_LON])
    return jnp.concatenate(rows, axis=0)


def quadrant_of(cells, row, col):
    return jnp.concatenate(
        [cells[(row + i) * WLON + col : (row + i) * WLON + col + HALF_LON] for i in range(HALF_LAT)], axis=0
    )


def normed_rows(values):
    centred = values - jnp.mean(values, axis=-1, keepdims=True)
    scale = lax.rsqrt(jnp.mean(centred * centred, axis=-1, keepdims=True) + eps_norm)
    return centred * scale, scale


def norm_tangent(unit, scale, tangent):
    moved = tangent - jnp.mean(tangent, axis=-1, keepdims=True)
    return scale * (moved - unit * jnp.mean(unit * tangent, axis=-1, keepdims=True))


def normed_with_tangent(values, tangent):
    centred = values - jnp.mean(values, axis=-1, keepdims=True)
    moved = tangent - jnp.mean(tangent, axis=-1, keepdims=True)
    spread = jnp.mean(centred * centred, axis=-1, keepdims=True)
    along = jnp.mean(centred * moved, axis=-1, keepdims=True)
    scale = lax.rsqrt(spread + eps_norm)
    unit = centred * scale
    return unit, scale * (moved - unit * (scale * along))


def same_head_block():
    rows = lax.broadcasted_iota(jnp.int32, (QUAD, QUAD), 0) >> 6
    return (rows == lax.broadcasted_iota(jnp.int32, (QUAD, QUAD), 1) >> 6).astype(bf16)


def by_head(pair, first):
    zero = jnp.zeros((), pair.dtype)
    return jnp.concatenate([jnp.where(first, pair, zero), jnp.where(first, zero, pair)], axis=0)


def halves(value):
    return value[:, :CELLS], value[:, CELLS:]


def slots_of(owners, rows, devices):
    owner_hot = (lax.broadcasted_iota(jnp.int32, (devices, rows), 0) == owners).astype(f32)
    upper = (
        lax.broadcasted_iota(jnp.int32, (rows, rows), 0) <= lax.broadcasted_iota(jnp.int32, (rows, rows), 1)
    ).astype(bf16)
    counted = product(owner_hot.astype(bf16), upper, NN)
    slots = jnp.sum(counted * owner_hot, axis=0, keepdims=True) - 1.0
    return owner_hot, slots


def prepare_kernel(
    background_ref,
    direction_ref,
    owner_ref,
    site_ref,
    weights_ref,
    precision_ref,
    lat_out,
    lon_out,
    far_out,
    out_ref,
    slots_ref,
):
    for piece_out, row, col in ((lat_out, 0, HALF_LON), (lon_out, HALF_LAT, 0), (far_out, 0, 0)):
        pieces = []
        for source in (background_ref, direction_ref):
            for i in range(HALF_LAT):
                pieces.append(source[row + i, col : col + HALF_LON, :])
        piece_out[...] = jnp.concatenate(pieces, axis=0).astype(bf16)
    rows = owner_ref.shape[1]
    devices = out_ref.shape[0]
    owner_hot, slots = slots_of(owner_ref[...], rows, devices)
    slots_ref[...] = slots
    payload = jnp.concatenate(
        [weights_ref[...], precision_ref[...], site_ref[...].astype(f32), jnp.zeros((2, rows), f32)], axis=0
    )
    owner_hot = owner_hot.astype(bf16)
    spread = jnp.concatenate([jnp.where(slots == float(k), payload, 0.0) for k in range(SLOTS)], axis=0)
    out = jnp.zeros((devices, SLOTS * 8), f32)
    for part in parts_of(spread, PIECES):
        out = out + product(owner_hot, part, NT)
    out_ref[...] = out


def unpack_kernel(owner_ref, slots_ref, returned_ref, out_ref):
    rows = owner_ref.shape[1]
    devices = returned_ref.shape[0]
    owner_hot = (lax.broadcasted_iota(jnp.int32, (devices, rows), 0) == owner_ref[...]).astype(bf16)
    picked = jnp.zeros((SLOTS, rows), f32)
    for part in parts_of(returned_ref[...], PIECES):
        picked = picked + product(part, owner_hot, TN)
    slot_hot = lax.broadcasted_iota(jnp.int32, (SLOTS, rows), 0).astype(f32) == slots_ref[...]
    out_ref[...] = jnp.sum(jnp.where(slot_hot, picked, 0.0), axis=0, keepdims=True)


def forward_kernel(
    band_hbm,
    logit_hbm,
    background_hbm,
    direction_hbm,
    lon_hbm,
    far_hbm,
    lat_hbm,
    embed_hbm,
    gain_hbm,
    decode_gain_hbm,
    decode_hbm,
    qkv_hbm,
    outw_hbm,
    lat_out,
    lon_out,
    far_out,
    own_out,
    hidden_hbm,
    block_hbm,
    units_hbm,
    scales_hbm,
    probs_hbm,
    band_ref,
    logit_ref,
    background_ref,
    direction_ref,
    lon_piece,
    far_piece,
    lat_piece,
    embed_ref,
    gain_ref,
    decode_gain_ref,
    decode_ref,
    qkv_ref,
    outw_ref,
    hidden_ref,
    block_ref,
    units_ref,
    scales_ref,
    probs_ref,
    mixed_ref,
    sems_in,
    sems_out,
):
    width = embed_ref.shape[1]
    quads = width // QUAD
    count = 0

    def fetch(source, target):
        nonlocal count
        copy = pltpu.make_async_copy(source, target, sems_in.at[count])
        copy.start()
        count += 1
        return copy

    first_needed = [
        fetch(*pair)
        for pair in (
            (lat_hbm, lat_piece),
            (lon_hbm, lon_piece),
            (far_hbm, far_piece),
            (background_hbm, background_ref),
            (direction_hbm, direction_ref),
            (embed_hbm, embed_ref),
            (gain_hbm, gain_ref),
            (band_hbm, band_ref),
            (logit_hbm, logit_ref),
        )
    ]
    fetched = []
    for half in range(2):
        for third in range(3):
            columns = pl.ds(third * width + half * (width // 2), width // 2)
            fetched.append(fetch(qkv_hbm.at[:, columns], qkv_ref.at[:, columns]))
    last_needed = [
        fetch(*pair) for pair in ((outw_hbm, outw_ref), (decode_gain_hbm, decode_gain_ref), (decode_hbm, decode_ref))
    ]
    kept = []

    def keep(source, target):
        copy = pltpu.make_async_copy(source, target, sems_out.at[len(kept)])
        copy.start()
        kept.append(copy)

    lane = lax.broadcasted_iota(jnp.int32, (1, 128), 1)
    first = lane < 64
    same_head = same_head_block()
    for copy in first_needed:
        copy.wait()
    low_q = lax.broadcasted_iota(jnp.int32, (CELLS, CELLS), 0) < CELLS // 2
    low_k = lax.broadcasted_iota(jnp.int32, (CELLS, CELLS), 1) < CELLS // 2
    allowed = jnp.where(low_q == low_k, 1.0, 1.0 - band_ref[...])
    logits = logit_ref[...]
    states = []
    for number, source in enumerate((background_ref, direction_ref)):
        own = jnp.concatenate([source[HALF_LAT + i, HALF_LON:, :] for i in range(HALF_LAT)], axis=0)
        part = slice(number * QUARTER, (number + 1) * QUARTER)
        received = [piece[part, :].astype(f32) for piece in (lat_piece, lon_piece, far_piece)]
        states.append(quadrants(own, *received))
    states = jnp.concatenate(states, axis=0).astype(bf16)
    hidden = product(states, embed_ref[...], NN).astype(bf16)
    hidden_ref[...] = hidden
    keep(hidden_ref.at[:CELLS], hidden_hbm)
    hidden = hidden.astype(f32)
    gain = gain_ref[...]
    normed = jnp.concatenate(
        [part * gain for part in normed_with_tangent(hidden[:CELLS], hidden[CELLS:])], axis=0
    ).astype(bf16)

    def project(quad):
        here = pl.ds(quad * QUAD, QUAD)
        packed = []
        for third in range(3):
            packed.append(product(normed, qkv_ref[:, pl.ds(third * width + quad * QUAD, QUAD)], NN))
        raw = jnp.concatenate([packed[0][:CELLS], packed[1][:CELLS]], axis=0)
        raw_tan = jnp.concatenate([packed[0][CELLS:], packed[1][CELLS:]], axis=0)
        scale = lax.rsqrt(product((raw * raw).astype(bf16), same_head, NN) + eps_head)
        unit = raw * scale
        along = product((unit * raw_tan).astype(bf16), same_head, NN)
        unit_tan = (scale * (raw_tan - unit * along)).astype(bf16)
        unit = unit.astype(bf16)
        value = packed[2].astype(bf16)
        scales_ref[:, here] = scale
        units_ref[: 2 * CELLS, here] = unit
        units_ref[2 * CELLS :, here] = value[:CELLS]
        return unit, unit_tan, value

    def attend(quad, unit, unit_tan, value):
        for side in range(2):
            pair = quad * 2 + side
            lanes = slice(side * 128, (side + 1) * 128)
            query, key = unit[:CELLS, lanes], by_head(unit[CELLS:, lanes], first)
            query_tan, key_tan = unit_tan[:CELLS, lanes], by_head(unit_tan[CELLS:, lanes], first)
            values = jnp.concatenate(
                [by_head(value[:CELLS, lanes], first), by_head(value[CELLS:, lanes], first)], axis=1
            )
            scores = product(query, key, NT)
            scores_tan = product(
                jnp.concatenate([query, query_tan], axis=1), jnp.concatenate([key_tan, key], axis=1), NT
            )
            probs, probs_tan = [], []
            for half, (score, score_tan) in enumerate(zip(halves(scores), halves(scores_tan))):
                head = pair * 2 + half
                logit = logits[:, head : head + 1]
                weights = jnp.exp(score * logit) * allowed
                prob = weights * (1.0 / jnp.sum(weights, axis=-1, keepdims=True))
                score_tan = score_tan * logit
                prob_tan = prob * (score_tan - jnp.sum(prob * score_tan, axis=-1, keepdims=True))
                probs.append(prob.astype(bf16))
                probs_tan.append(prob_tan.astype(bf16))
            probs = jnp.concatenate(probs, axis=1)
            probs_ref[pair] = probs
            mixed, mixed_tan = halves(product(probs, values, NN))
            mixed_tan = mixed_tan + product(jnp.concatenate(probs_tan, axis=1), values[:, :128], NN)
            columns = pl.ds(pair * 128, 128)
            mixed_ref[:CELLS, columns] = mixed.astype(bf16)
            mixed_ref[CELLS:, columns] = mixed_tan.astype(bf16)

    for copy in fetched[0:3]:
        copy.wait()
    vals0 = project(0)
    vals1 = project(1)
    for copy in fetched[3:6]:
        copy.wait()
    vals2 = project(2)
    vals3 = project(3)
    attend(0, *vals0)
    attend(1, *vals1)
    attend(2, *vals2)
    attend(3, *vals3)

    keep(units_ref, units_hbm)
    keep(scales_ref, scales_hbm)
    keep(probs_ref, probs_hbm)
    for copy in last_needed:
        copy.wait()
    block = (hidden_ref[...].astype(f32) + product(mixed_ref[...], outw_ref[...], NN)).astype(bf16)
    block_ref[...] = block
    keep(block_ref.at[:CELLS], block_hbm)
    block = block.astype(f32)
    moved = normed_with_tangent(block[:CELLS], block[CELLS:])[1]
    change = product((moved * decode_gain_ref[...]).astype(bf16), decode_ref[...], NT)
    lat_out[...] = quadrant_of(change, HALF_LAT, 0).astype(bf16)
    lon_out[...] = quadrant_of(change, 0, HALF_LON).astype(bf16)
    far_out[...] = quadrant_of(change, HALF_LAT, HALF_LON).astype(bf16)
    own_out[...] = quadrant_of(change, 0, 0).astype(bf16)
    for copy in kept:
        copy.wait()


def observe_kernel(
    direction_ref,
    own_piece,
    lon_piece,
    far_piece,
    lat_piece,
    arrived_ref,
    at_obs_out,
    adjoint_out,
    own_out,
    lat_out,
    lon_out,
    far_out,
):
    var_count = direction_ref.shape[2]
    devices = arrived_ref.shape[0]
    pieces = [piece[...].astype(f32) for piece in (far_piece, lon_piece, lat_piece, own_piece)]
    moved = quadrants(*pieces)
    tangent = jnp.concatenate([direction_ref[i] for i in range(WLAT)], axis=0) + moved
    arrived = jnp.transpose(arrived_ref[...])
    cell_ids = lax.broadcasted_iota(jnp.int32, (CELLS, devices), 0).astype(f32)
    var_ids = lax.broadcasted_iota(jnp.int32, (var_count, devices), 0).astype(f32)
    selectors, var_hots, precisions = [], [], []
    for k in range(SLOTS):
        row = arrived[k * 8 : (k + 1) * 8]
        site = row[5:6]
        cell = jnp.floor((site + 0.5) * (1.0 / var_count))
        variable = site - cell * var_count
        selector = jnp.zeros((CELLS, devices), f32)
        for corner, offset in enumerate((0, 1, WLON, WLON + 1)):
            selector = selector + jnp.where(cell_ids == cell + float(offset), row[corner : corner + 1], 0.0)
        selectors.append(selector)
        var_hots.append((var_ids == variable).astype(f32))
        precisions.append(row[4:5])
    selector = jnp.concatenate(selectors, axis=1)
    var_hot = jnp.concatenate(var_hots, axis=1)
    precision = jnp.concatenate(precisions, axis=1)
    selector_parts = parts_of(selector, 2)
    tangent_parts = parts_of(tangent, 3)
    picked = product(tangent_parts[0], selector_parts[0], TN)
    for left, right in ((1, 0), (0, 1), (2, 0)):
        picked = picked + product(tangent_parts[left], selector_parts[right], TN)
    at_obs = jnp.sum(picked * var_hot, axis=0, keepdims=True)
    at_obs_out[...] = jnp.transpose(
        jnp.concatenate([at_obs[:, k * devices : (k + 1) * devices] for k in range(SLOTS)], axis=0)
    )
    spread_parts = parts_of(var_hot * (at_obs * precision), 2)
    adjoint = product(selector_parts[0], spread_parts[0], NT)
    for left, right in ((1, 0), (0, 1)):
        adjoint = adjoint + product(selector_parts[left], spread_parts[right], NT)
    for i in range(WLAT):
        adjoint_out[i] = adjoint[i * WLON : (i + 1) * WLON]
    own_out[...] = quadrant_of(adjoint, HALF_LAT, HALF_LON).astype(bf16)
    lat_out[...] = quadrant_of(adjoint, 0, HALF_LON).astype(bf16)
    lon_out[...] = quadrant_of(adjoint, HALF_LAT, 0).astype(bf16)
    far_out[...] = quadrant_of(adjoint, 0, 0).astype(bf16)


def adjoint_kernel(
    own_hbm,
    lon_hbm,
    far_hbm,
    lat_hbm,
    block_hbm,
    decode_hbm,
    decode_gain_hbm,
    logit_hbm,
    outw_hbm,
    units_hbm,
    probs_hbm,
    scales_hbm,
    hidden_hbm,
    gain_hbm,
    embed_hbm,
    qkv_hbm,
    own_out,
    lat_out,
    lon_out,
    far_out,
    own_piece,
    lon_piece,
    far_piece,
    lat_piece,
    block_ref,
    decode_ref,
    decode_gain_ref,
    logit_ref,
    outw_ref,
    units_ref,
    probs_ref,
    scales_ref,
    hidden_ref,
    gain_ref,
    embed_ref,
    qkv_ref,
    packed_ref,
    sems,
):
    width = embed_ref.shape[1]
    quads = width // QUAD
    fetched = []

    def fetch(source, target):
        copy = pltpu.make_async_copy(source, target, sems.at[len(fetched)])
        copy.start()
        fetched.append(copy)

    for source, target in (
        (own_hbm, own_piece),
        (lon_hbm, lon_piece),
        (far_hbm, far_piece),
        (lat_hbm, lat_piece),
        (block_hbm, block_ref),
        (decode_hbm, decode_ref),
        (decode_gain_hbm, decode_gain_ref),
        (logit_hbm, logit_ref),
        (outw_hbm, outw_ref),
        (units_hbm, units_ref),
        (probs_hbm, probs_ref),
        (scales_hbm, scales_ref),
        (hidden_hbm, hidden_ref),
        (gain_hbm, gain_ref),
        (embed_hbm, embed_ref),
        (qkv_hbm, qkv_ref),
    ):
        fetch(source, target)

    def wait(start, stop):
        for copy in fetched[start:stop]:
            copy.wait()

    wait(0, 8)
    change = quadrants(*[piece[...].astype(f32) for piece in (own_piece, lat_piece, lon_piece, far_piece)])
    unit, scale = normed_rows(block_ref[...].astype(f32))
    normed_ct = product(change.astype(bf16), decode_ref[...], NN).astype(bf16).astype(f32) * decode_gain_ref[...]
    block_ct = norm_tangent(unit, scale, normed_ct).astype(bf16)
    wait(8, 9)
    mixed_ct = product(block_ct, outw_ref[...], NT).astype(bf16)

    lane = lax.broadcasted_iota(jnp.int32, (1, 128), 1)
    first = lane < 64
    same_head = same_head_block()
    logits = logit_ref[...]
    wait(9, 15)
    for quad in range(quads):
        cotangents = []
        for side in range(2):
            pair = quad * 2 + side
            here = pl.ds(pair * 128, 128)
            query, key, value = (units_ref[i * CELLS : (i + 1) * CELLS, here] for i in range(3))
            mixed_here = mixed_ct[:, pair * 128 : (pair + 1) * 128]
            probs = halves(probs_ref[pair])
            scores_ct = []
            for prob, prob_ct in zip(probs, halves(product(mixed_here, by_head(value, first), NT))):
                prob = prob.astype(f32)
                scores_ct.append((prob * (prob_ct - jnp.sum(prob * prob_ct, axis=-1, keepdims=True))).astype(bf16))
            head = pair * 2
            logit = jnp.where(first, logits[:, head : head + 1], logits[:, head + 1 : head + 2])
            query_ct = product(jnp.concatenate(scores_ct, axis=1), by_head(key, first), NN) * logit
            key_ct = product(jnp.concatenate(scores_ct, axis=0), by_head(query, first), TN) * logit
            value_ct = product(jnp.concatenate(probs, axis=0), by_head(mixed_here, first), TN)
            packed_ref[:, pl.ds(2 * width + pair * 128, 128)] = value_ct.astype(bf16)
            cotangents.append(jnp.concatenate([query_ct, key_ct], axis=0))
        unit_ct = jnp.concatenate(cotangents, axis=1)
        here = pl.ds(quad * QUAD, QUAD)
        units = units_ref[: 2 * CELLS, here].astype(f32)
        along = product((units * unit_ct).astype(bf16), same_head, NN)
        raw_ct = (scales_ref[:, here] * (unit_ct - units * along)).astype(bf16)
        packed_ref[:, here] = raw_ct[:CELLS]
        packed_ref[:, pl.ds(width + quad * QUAD, QUAD)] = raw_ct[CELLS:]

    unit, scale = normed_rows(hidden_ref[...].astype(f32))
    wait(15, 16)
    normed_ct = product(packed_ref[...], qkv_ref[...], NT).astype(bf16).astype(f32) * gain_ref[...]
    hidden_ct = (norm_tangent(unit, scale, normed_ct) + block_ct.astype(f32)).astype(bf16)
    state = product(hidden_ct, embed_ref[...], NT)
    lat_out[...] = quadrant_of(state, HALF_LAT, 0).astype(bf16)
    lon_out[...] = quadrant_of(state, 0, HALF_LON).astype(bf16)
    far_out[...] = quadrant_of(state, HALF_LAT, HALF_LON).astype(bf16)
    own_out[...] = quadrant_of(state, 0, 0).astype(bf16)


def shape(dims, dtype):
    return jax.ShapeDtypeStruct(dims, dtype)


def exchanged(lat_piece, lon_piece, far_piece, steps):
    lat_count, lon_count = lax.axis_size("lat"), lax.axis_size("lon")
    lat_piece = lax.ppermute(lat_piece, "lat", [(i, (i + steps) % lat_count) for i in range(lat_count)])
    lon_piece = lax.ppermute(lon_piece, "lon", [(i, (i + steps) % lon_count) for i in range(lon_count)])
    pairs = [
        (i * lat_count + j, ((i + steps) % lon_count) * lat_count + (j + steps) % lat_count)
        for i in range(lon_count)
        for j in range(lat_count)
    ]
    far_piece = lax.ppermute(far_piece, ("lon", "lat"), pairs)
    return lat_piece, lon_piece, far_piece


def run_forward(
    last_band, logit_scale, background, direction, strips, embed_weight, gain, decode_gain, decode_rows, qkv_weight, out_weight
):
    width = embed_weight.shape[1]
    quarter = shape((QUARTER, background.shape[2]), bf16)
    wide = shape((CELLS, width), bf16)
    kept = [
        wide,
        wide,
        shape((3 * CELLS, width), bf16),
        shape((2 * CELLS, width), f32),
        shape((HEADS // 2, CELLS, 2 * CELLS), bf16),
    ]
    inputs = (last_band, logit_scale, background, direction, strips[1], strips[2], strips[0], embed_weight, gain, decode_gain, decode_rows, qkv_weight, out_weight)
    both = pltpu.VMEM((2 * CELLS, width), bf16)
    return pl.pallas_call(
        forward_kernel,
        out_shape=[quarter] * 4 + kept,
        in_specs=[ANY] * 13,
        out_specs=[VMEM] * 4 + [ANY] * 5,
        scratch_shapes=[pltpu.VMEM(item.shape, item.dtype) for item in inputs]
        + [both, both]
        + [pltpu.VMEM(item.shape, item.dtype) for item in kept[2:]]
        + [both, pltpu.SemaphoreType.DMA((18,)), pltpu.SemaphoreType.DMA((5,))],
        cost_estimate=pl.CostEstimate(flops=2_500_000_000, bytes_accessed=10_000_000, transcendentals=300_000),
        name="forward",
    )(*inputs)


def run_observe(direction, pieces, arrived):
    quarter = shape(pieces[0].shape, bf16)
    devices = arrived.shape[0]
    return pl.pallas_call(
        observe_kernel,
        out_shape=[shape((devices, SLOTS), f32), shape(direction.shape, f32)] + [quarter] * 4,
        in_specs=[VMEM] * 6,
        out_specs=[VMEM] * 6,
        name="observe",
    )(direction, *pieces, arrived)


def run_adjoint(logit_scale, pieces, embed_weight, gain, decode_gain, decode_rows, kept, qkv_weight, out_weight):
    hidden, block, units, scales, probs = kept
    width = embed_weight.shape[1]
    inputs = (*pieces, block, decode_rows, decode_gain, logit_scale, out_weight, units, probs, scales)
    inputs = (*inputs, hidden, gain, embed_weight, qkv_weight)
    return pl.pallas_call(
        adjoint_kernel,
        out_shape=[shape(pieces[0].shape, bf16)] * 4,
        in_specs=[ANY] * len(inputs),
        out_specs=[VMEM] * 4,
        scratch_shapes=[pltpu.VMEM(item.shape, item.dtype) for item in inputs]
        + [pltpu.VMEM((CELLS, 3 * width), bf16), pltpu.SemaphoreType.DMA((len(inputs),))],
        cost_estimate=pl.CostEstimate(flops=1_500_000_000, bytes_accessed=10_000_000, transcendentals=300_000),
        name="adjoint",
    )(*inputs)


def per_device(
    background,
    direction,
    obs_owner,
    obs_site,
    obs_weights,
    obs_precision,
    embed_weight,
    attn_gain,
    qkv_weight,
    logit_scale,
    out_weight,
    decode_gain,
    decode_weight,
):
    var_count = background.shape[2]
    width = embed_weight.shape[1]
    devices = lax.axis_size("lat") * lax.axis_size("lon")
    obs_rows = obs_site.shape[0]
    last_band = (lax.axis_index("lat") == lax.axis_size("lat") - 1).astype(f32).reshape(1, 1)
    logit_scale = logit_scale.reshape(1, HEADS)
    gain = attn_gain.reshape(1, width)
    decode_gain = decode_gain.reshape(1, width)
    decode_rows = decode_weight.T

    owners = obs_owner.reshape(1, obs_rows)
    *strips, outgoing, slots = pl.pallas_call(
        prepare_kernel,
        out_shape=[shape((2 * QUARTER, var_count), bf16)] * 3
        + [shape((devices, SLOTS * 8), f32), shape((1, obs_rows), f32)],
        in_specs=[VMEM] * 6,
        out_specs=[VMEM] * 5,
        name="prepare",
    )(
        background,
        direction,
        owners,
        obs_site.reshape(1, obs_rows),
        obs_weights.T,
        obs_precision.reshape(1, obs_rows),
    )
    strips = exchanged(*strips, -1)
    arrived = lax.all_to_all(outgoing, ("lon", "lat"), split_axis=0, concat_axis=0, tiled=True)

    lat_piece, lon_piece, far_piece, own_piece, *kept = run_forward(
        last_band, logit_scale, background, direction, strips, embed_weight, gain, decode_gain, decode_rows, qkv_weight, out_weight
    )
    lat_piece, lon_piece, far_piece = exchanged(lat_piece, lon_piece, far_piece, 1)

    at_obs, adjoint_field, own_piece, lat_piece, lon_piece, far_piece = run_observe(
        direction, (own_piece, lon_piece, far_piece, lat_piece), arrived
    )
    lat_piece, lon_piece, far_piece = exchanged(lat_piece, lon_piece, far_piece, -1)
    returned = lax.all_to_all(at_obs, ("lon", "lat"), split_axis=0, concat_axis=0, tiled=True)

    own_piece, lat_piece, lon_piece, far_piece = run_adjoint(
        logit_scale, (own_piece, lon_piece, far_piece, lat_piece), embed_weight, gain, decode_gain, decode_rows, kept, qkv_weight, out_weight
    )
    lat_piece, lon_piece, far_piece, returned = lax.optimization_barrier((lat_piece, lon_piece, far_piece, returned))
    lat_piece, lon_piece, far_piece = exchanged(lat_piece, lon_piece, far_piece, 1)

    hvp = adjoint_field
    for piece, row, col in (
        (lon_piece, HALF_LAT, 0),
        (far_piece, 0, 0),
        (lat_piece, 0, HALF_LON),
        (own_piece, HALF_LAT, HALF_LON),
    ):
        piece = piece.reshape(HALF_LAT, HALF_LON, var_count).astype(f32)
        around = ((row, HALF_LAT - row, 0), (col, HALF_LON - col, 0), (0, 0, 0))
        hvp = hvp + lax.pad(piece, jnp.zeros((), f32), around)
    obs_increment = pl.pallas_call(
        unpack_kernel,
        out_shape=shape((1, obs_rows), f32),
        in_specs=[VMEM] * 3,
        out_specs=VMEM,
        name="unpack",
    )(owners, slots, returned)
    return (hvp, obs_increment.reshape(obs_rows))


def solution(mesh):
    in_specs = (
        P("lat", "lon", None),
        P("lat", "lon", None),
        P(("lon", "lat"), None),
        P(("lon", "lat")),
        P(("lon", "lat"), None),
        P(("lon", "lat")),
        P(),
        P(),
        P(),
        P(),
        P(),
        P(),
        P(),
    )
    out_specs = (P("lat", "lon", None), P(("lon", "lat")))
    return jax.shard_map(
        per_device, mesh=mesh, in_specs=in_specs, out_specs=out_specs, check_vma=False
    )
```

```python
import jax
import jax.numpy as jnp
from jax import lax
from jax.experimental import pallas as pl
from jax.experimental.pallas import tpu as pltpu
from jax.sharding import PartitionSpec as P

HEADS = 16
WLAT = 8
WLON = 16
CELLS = WLAT * WLON
HALF_LAT = WLAT // 2
HALF_LON = WLON // 2
QUARTER = HALF_LAT * HALF_LON
SLOTS = 8
PIECES = 2
QUAD = 256

eps_norm = 1e-05
eps_head = 1e-06

f32 = jnp.float32
bf16 = jnp.bfloat16

NN = ((1,), (0,))
NT = ((1,), (1,))
TN = ((0,), (0,))

VMEM = pl.BlockSpec(memory_space=pltpu.VMEM)
SMEM = pl.BlockSpec(memory_space=pltpu.SMEM)
ANY = pl.BlockSpec(memory_space=pl.ANY)


def product(left, right, dims):
    return lax.dot_general(left, right, (dims, ((), ())), preferred_element_type=f32)


def parts_of(value, count):
    parts = []
    for _ in range(count):
        part = value.astype(bf16)
        parts.append(part)
        value = value - part.astype(f32)
    return parts


def quadrants(top_left, bottom_left, top_right, bottom_right):
    rows = []
    for left, right in ((top_left, top_right), (bottom_left, bottom_right)):
        for i in range(HALF_LAT):
            rows.append(left[i * HALF_LON : (i + 1) * HALF_LON])
            rows.append(right[i * HALF_LON : (i + 1) * HALF_LON])
    return jnp.concatenate(rows, axis=0)


def quadrant_of(cells, row, col):
    return jnp.concatenate(
        [cells[(row + i) * WLON + col : (row + i) * WLON + col + HALF_LON] for i in range(HALF_LAT)], axis=0
    )


def normed_rows(values):
    centred = values - jnp.mean(values, axis=-1, keepdims=True)
    scale = lax.rsqrt(jnp.mean(centred * centred, axis=-1, keepdims=True) + eps_norm)
    return centred * scale, scale


def norm_tangent(unit, scale, tangent):
    moved = tangent - jnp.mean(tangent, axis=-1, keepdims=True)
    return scale * (moved - unit * jnp.mean(unit * tangent, axis=-1, keepdims=True))


def normed_with_tangent(values, tangent):
    centred = values - jnp.mean(values, axis=-1, keepdims=True)
    moved = tangent - jnp.mean(tangent, axis=-1, keepdims=True)
    spread = jnp.mean(centred * centred, axis=-1, keepdims=True)
    along = jnp.mean(centred * moved, axis=-1, keepdims=True)
    scale = lax.rsqrt(spread + eps_norm)
    unit = centred * scale
    return unit, scale * (moved - unit * (scale * along))


def same_head_block():
    rows = lax.broadcasted_iota(jnp.int32, (QUAD, QUAD), 0) >> 6
    return (rows == lax.broadcasted_iota(jnp.int32, (QUAD, QUAD), 1) >> 6).astype(bf16)


def by_head(pair, first):
    zero = jnp.zeros((), pair.dtype)
    return jnp.concatenate([jnp.where(first, pair, zero), jnp.where(first, zero, pair)], axis=0)


def halves(value):
    return value[:, :CELLS], value[:, CELLS:]


def slots_of(owners, rows, devices):
    owner_hot = (lax.broadcasted_iota(jnp.int32, (devices, rows), 0) == owners).astype(f32)
    upper = (
        lax.broadcasted_iota(jnp.int32, (rows, rows), 0) <= lax.broadcasted_iota(jnp.int32, (rows, rows), 1)
    ).astype(bf16)
    counted = product(owner_hot.astype(bf16), upper, NN)
    slots = jnp.sum(counted * owner_hot, axis=0, keepdims=True) - 1.0
    return owner_hot, slots


def prepare_kernel(
    background_ref,
    direction_ref,
    owner_ref,
    site_ref,
    weights_ref,
    precision_ref,
    lat_out,
    lon_out,
    far_out,
    out_ref,
    slots_ref,
):
    for piece_out, row, col in ((lat_out, 0, HALF_LON), (lon_out, HALF_LAT, 0), (far_out, 0, 0)):
        pieces = []
        for source in (background_ref, direction_ref):
            for i in range(HALF_LAT):
                pieces.append(source[row + i, col : col + HALF_LON, :])
        piece_out[...] = jnp.concatenate(pieces, axis=0).astype(bf16)
    rows = owner_ref.shape[1]
    devices = out_ref.shape[0]
    owner_hot, slots = slots_of(owner_ref[...], rows, devices)
    slots_ref[...] = slots
    payload = jnp.concatenate(
        [weights_ref[...], precision_ref[...], site_ref[...].astype(f32), jnp.zeros((2, rows), f32)], axis=0
    )
    owner_hot = owner_hot.astype(bf16)
    spread = jnp.concatenate([jnp.where(slots == float(k), payload, 0.0) for k in range(SLOTS)], axis=0)
    out = jnp.zeros((devices, SLOTS * 8), f32)
    for part in parts_of(spread, PIECES):
        out = out + product(owner_hot, part, NT)
    out_ref[...] = out


def unpack_kernel(owner_ref, slots_ref, returned_ref, out_ref):
    rows = owner_ref.shape[1]
    devices = returned_ref.shape[0]
    owner_hot = (lax.broadcasted_iota(jnp.int32, (devices, rows), 0) == owner_ref[...]).astype(bf16)
    picked = jnp.zeros((SLOTS, rows), f32)
    for part in parts_of(returned_ref[...], PIECES):
        picked = picked + product(part, owner_hot, TN)
    slot_hot = lax.broadcasted_iota(jnp.int32, (SLOTS, rows), 0).astype(f32) == slots_ref[...]
    out_ref[...] = jnp.sum(jnp.where(slot_hot, picked, 0.0), axis=0, keepdims=True)


def forward_kernel(
    band_hbm,
    logit_hbm,
    background_hbm,
    direction_hbm,
    lon_hbm,
    far_hbm,
    lat_hbm,
    embed_hbm,
    gain_hbm,
    decode_gain_hbm,
    decode_hbm,
    qkv_hbm,
    outw_hbm,
    lat_out,
    lon_out,
    far_out,
    own_out,
    hidden_hbm,
    block_hbm,
    units_hbm,
    scales_hbm,
    probs_hbm,
    band_ref,
    logit_ref,
    background_ref,
    direction_ref,
    lon_piece,
    far_piece,
    lat_piece,
    embed_ref,
    gain_ref,
    decode_gain_ref,
    decode_ref,
    qkv_ref,
    outw_ref,
    hidden_ref,
    block_ref,
    units_ref,
    scales_ref,
    probs_ref,
    mixed_ref,
    sems_in,
    sems_out,
):
    width = embed_ref.shape[1]
    quads = width // QUAD
    count = 0

    def fetch(source, target):
        nonlocal count
        copy = pltpu.make_async_copy(source, target, sems_in.at[count])
        copy.start()
        count += 1
        return copy

    first_needed = [
        fetch(*pair)
        for pair in (
            (lat_hbm, lat_piece),
            (lon_hbm, lon_piece),
            (far_hbm, far_piece),
            (background_hbm, background_ref),
            (direction_hbm, direction_ref),
            (embed_hbm, embed_ref),
            (gain_hbm, gain_ref),
            (band_hbm, band_ref),
            (logit_hbm, logit_ref),
        )
    ]
    fetched = []
    for half in range(2):
        for third in range(3):
            columns = pl.ds(third * width + half * (width // 2), width // 2)
            fetched.append(fetch(qkv_hbm.at[:, columns], qkv_ref.at[:, columns]))
    last_needed = [
        fetch(*pair) for pair in ((outw_hbm, outw_ref), (decode_gain_hbm, decode_gain_ref), (decode_hbm, decode_ref))
    ]
    kept = []

    def keep(source, target):
        copy = pltpu.make_async_copy(source, target, sems_out.at[len(kept)])
        copy.start()
        kept.append(copy)

    lane = lax.broadcasted_iota(jnp.int32, (1, 128), 1)
    first = lane < 64
    same_head = same_head_block()
    for copy in first_needed:
        copy.wait()
    low_q = lax.broadcasted_iota(jnp.int32, (CELLS, CELLS), 0) < CELLS // 2
    low_k = lax.broadcasted_iota(jnp.int32, (CELLS, CELLS), 1) < CELLS // 2
    allowed = jnp.where(low_q == low_k, 1.0, 1.0 - band_ref[...])
    logits = logit_ref[...]
    states = []
    for number, source in enumerate((background_ref, direction_ref)):
        own = jnp.concatenate([source[HALF_LAT + i, HALF_LON:, :] for i in range(HALF_LAT)], axis=0)
        part = slice(number * QUARTER, (number + 1) * QUARTER)
        received = [piece[part, :].astype(f32) for piece in (lat_piece, lon_piece, far_piece)]
        states.append(quadrants(own, *received))
    states = jnp.concatenate(states, axis=0).astype(bf16)
    hidden = product(states, embed_ref[...], NN).astype(bf16)
    hidden_ref[...] = hidden
    keep(hidden_ref.at[:CELLS], hidden_hbm)
    hidden = hidden.astype(f32)
    gain = gain_ref[...]
    normed = jnp.concatenate(
        [part * gain for part in normed_with_tangent(hidden[:CELLS], hidden[CELLS:])], axis=0
    ).astype(bf16)

    def project(quad):
        here = pl.ds(quad * QUAD, QUAD)
        packed = []
        for third in range(3):
            packed.append(product(normed, qkv_ref[:, pl.ds(third * width + quad * QUAD, QUAD)], NN))
        raw = jnp.concatenate([packed[0][:CELLS], packed[1][:CELLS]], axis=0)
        raw_tan = jnp.concatenate([packed[0][CELLS:], packed[1][CELLS:]], axis=0)
        scale = lax.rsqrt(product((raw * raw).astype(bf16), same_head, NN) + eps_head)
        unit = raw * scale
        along = product((unit * raw_tan).astype(bf16), same_head, NN)
        unit_tan = (scale * (raw_tan - unit * along)).astype(bf16)
        unit = unit.astype(bf16)
        value = packed[2].astype(bf16)
        scales_ref[:, here] = scale
        units_ref[: 2 * CELLS, here] = unit
        units_ref[2 * CELLS :, here] = value[:CELLS]
        return unit, unit_tan, value

    def attend(quad, unit, unit_tan, value):
        for side in range(2):
            pair = quad * 2 + side
            lanes = slice(side * 128, (side + 1) * 128)
            query, key = unit[:CELLS, lanes], by_head(unit[CELLS:, lanes], first)
            query_tan, key_tan = unit_tan[:CELLS, lanes], by_head(unit_tan[CELLS:, lanes], first)
            values = jnp.concatenate(
                [by_head(value[:CELLS, lanes], first), by_head(value[CELLS:, lanes], first)], axis=1
            )
            scores = product(query, key, NT)
            scores_tan = product(
                jnp.concatenate([query, query_tan], axis=1), jnp.concatenate([key_tan, key], axis=1), NT
            )
            probs, probs_tan = [], []
            for half, (score, score_tan) in enumerate(zip(halves(scores), halves(scores_tan))):
                head = pair * 2 + half
                logit = logits[:, head : head + 1]
                weights = jnp.exp(score * logit) * allowed
                prob = weights * (1.0 / jnp.sum(weights, axis=-1, keepdims=True))
                score_tan = score_tan * logit
                prob_tan = prob * (score_tan - jnp.sum(prob * score_tan, axis=-1, keepdims=True))
                probs.append(prob.astype(bf16))
                probs_tan.append(prob_tan.astype(bf16))
            probs = jnp.concatenate(probs, axis=1)
            probs_ref[pair] = probs
            mixed, mixed_tan = halves(product(probs, values, NN))
            mixed_tan = mixed_tan + product(jnp.concatenate(probs_tan, axis=1), values[:, :128], NN)
            columns = pl.ds(pair * 128, 128)
            mixed_ref[:CELLS, columns] = mixed.astype(bf16)
            mixed_ref[CELLS:, columns] = mixed_tan.astype(bf16)

    for copy in fetched[0:3]:
        copy.wait()
    vals0 = project(0)
    vals1 = project(1)
    for copy in fetched[3:6]:
        copy.wait()
    vals2 = project(2)
    vals3 = project(3)
    attend(0, *vals0)
    attend(1, *vals1)
    attend(2, *vals2)
    attend(3, *vals3)

    keep(units_ref, units_hbm)
    keep(scales_ref, scales_hbm)
    keep(probs_ref, probs_hbm)
    for copy in last_needed:
        copy.wait()
    block = (hidden_ref[...].astype(f32) + product(mixed_ref[...], outw_ref[...], NN)).astype(bf16)
    block_ref[...] = block
    keep(block_ref.at[:CELLS], block_hbm)
    block = block.astype(f32)
    moved = normed_with_tangent(block[:CELLS], block[CELLS:])[1]
    change = product((moved * decode_gain_ref[...]).astype(bf16), decode_ref[...], NT)
    lat_out[...] = quadrant_of(change, HALF_LAT, 0).astype(bf16)
    lon_out[...] = quadrant_of(change, 0, HALF_LON).astype(bf16)
    far_out[...] = quadrant_of(change, HALF_LAT, HALF_LON).astype(bf16)
    own_out[...] = quadrant_of(change, 0, 0).astype(bf16)
    for copy in kept:
        copy.wait()


def observe_kernel(
    direction_ref,
    own_piece,
    lon_piece,
    far_piece,
    lat_piece,
    arrived_ref,
    at_obs_out,
    adjoint_out,
    own_out,
    lat_out,
    lon_out,
    far_out,
):
    var_count = direction_ref.shape[2]
    devices = arrived_ref.shape[0]
    pieces = [piece[...].astype(f32) for piece in (far_piece, lon_piece, lat_piece, own_piece)]
    moved = quadrants(*pieces)
    tangent = jnp.concatenate([direction_ref[i] for i in range(WLAT)], axis=0) + moved
    arrived = jnp.transpose(arrived_ref[...])
    cell_ids = lax.broadcasted_iota(jnp.int32, (CELLS, devices), 0).astype(f32)
    var_ids = lax.broadcasted_iota(jnp.int32, (var_count, devices), 0).astype(f32)
    selectors, var_hots, precisions = [], [], []
    for k in range(SLOTS):
        row = arrived[k * 8 : (k + 1) * 8]
        site = row[5:6]
        cell = jnp.floor((site + 0.5) * (1.0 / var_count))
        variable = site - cell * var_count
        selector = jnp.zeros((CELLS, devices), f32)
        for corner, offset in enumerate((0, 1, WLON, WLON + 1)):
            selector = selector + jnp.where(cell_ids == cell + float(offset), row[corner : corner + 1], 0.0)
        selectors.append(selector)
        var_hots.append((var_ids == variable).astype(f32))
        precisions.append(row[4:5])
    selector = jnp.concatenate(selectors, axis=1)
    var_hot = jnp.concatenate(var_hots, axis=1)
    precision = jnp.concatenate(precisions, axis=1)
    selector_parts = parts_of(selector, 2)
    tangent_parts = parts_of(tangent, 3)
    picked = product(tangent_parts[0], selector_parts[0], TN)
    for left, right in ((1, 0), (0, 1), (2, 0)):
        picked = picked + product(tangent_parts[left], selector_parts[right], TN)
    at_obs = jnp.sum(picked * var_hot, axis=0, keepdims=True)
    at_obs_out[...] = jnp.transpose(
        jnp.concatenate([at_obs[:, k * devices : (k + 1) * devices] for k in range(SLOTS)], axis=0)
    )
    spread_parts = parts_of(var_hot * (at_obs * precision), 2)
    adjoint = product(selector_parts[0], spread_parts[0], NT)
    for left, right in ((1, 0), (0, 1)):
        adjoint = adjoint + product(selector_parts[left], spread_parts[right], NT)
    for i in range(WLAT):
        adjoint_out[i] = adjoint[i * WLON : (i + 1) * WLON]
    own_out[...] = quadrant_of(adjoint, HALF_LAT, HALF_LON).astype(bf16)
    lat_out[...] = quadrant_of(adjoint, 0, HALF_LON).astype(bf16)
    lon_out[...] = quadrant_of(adjoint, HALF_LAT, 0).astype(bf16)
    far_out[...] = quadrant_of(adjoint, 0, 0).astype(bf16)


def adjoint_kernel(
    own_hbm,
    lon_hbm,
    far_hbm,
    lat_hbm,
    block_hbm,
    decode_hbm,
    decode_gain_hbm,
    logit_hbm,
    outw_hbm,
    units_hbm,
    probs_hbm,
    scales_hbm,
    hidden_hbm,
    gain_hbm,
    embed_hbm,
    qkv_hbm,
    own_out,
    lat_out,
    lon_out,
    far_out,
    own_piece,
    lon_piece,
    far_piece,
    lat_piece,
    block_ref,
    decode_ref,
    decode_gain_ref,
    logit_ref,
    outw_ref,
    units_ref,
    probs_ref,
    scales_ref,
    hidden_ref,
    gain_ref,
    embed_ref,
    qkv_ref,
    packed_ref,
    sems,
):
    width = embed_ref.shape[1]
    quads = width // QUAD
    fetched = []

    def fetch(source, target):
        copy = pltpu.make_async_copy(source, target, sems.at[len(fetched)])
        copy.start()
        fetched.append(copy)

    for source, target in (
        (own_hbm, own_piece),
        (lon_hbm, lon_piece),
        (far_hbm, far_piece),
        (lat_hbm, lat_piece),
        (block_hbm, block_ref),
        (decode_hbm, decode_ref),
        (decode_gain_hbm, decode_gain_ref),
        (logit_hbm, logit_ref),
        (outw_hbm, outw_ref),
        (units_hbm, units_ref),
        (probs_hbm, probs_ref),
        (scales_hbm, scales_ref),
        (hidden_hbm, hidden_ref),
        (gain_hbm, gain_ref),
        (embed_hbm, embed_ref),
        (qkv_hbm, qkv_ref),
    ):
        fetch(source, target)

    def wait(start, stop):
        for copy in fetched[start:stop]:
            copy.wait()

    wait(0, 8)
    change = quadrants(*[piece[...].astype(f32) for piece in (own_piece, lat_piece, lon_piece, far_piece)])
    unit, scale = normed_rows(block_ref[...].astype(f32))
    normed_ct = product(change.astype(bf16), decode_ref[...], NN).astype(bf16).astype(f32) * decode_gain_ref[...]
    block_ct = norm_tangent(unit, scale, normed_ct).astype(bf16)
    wait(8, 9)
    mixed_ct = product(block_ct, outw_ref[...], NT).astype(bf16)

    lane = lax.broadcasted_iota(jnp.int32, (1, 128), 1)
    first = lane < 64
    same_head = same_head_block()
    logits = logit_ref[...]
    wait(9, 15)
    for quad in range(quads):
        cotangents = []
        for side in range(2):
            pair = quad * 2 + side
            here = pl.ds(pair * 128, 128)
            query, key, value = (units_ref[i * CELLS : (i + 1) * CELLS, here] for i in range(3))
            mixed_here = mixed_ct[:, pair * 128 : (pair + 1) * 128]
            probs = halves(probs_ref[pair])
            scores_ct = []
            for prob, prob_ct in zip(probs, halves(product(mixed_here, by_head(value, first), NT))):
                prob = prob.astype(f32)
                scores_ct.append((prob * (prob_ct - jnp.sum(prob * prob_ct, axis=-1, keepdims=True))).astype(bf16))
            head = pair * 2
            logit = jnp.where(first, logits[:, head : head + 1], logits[:, head + 1 : head + 2])
            query_ct = product(jnp.concatenate(scores_ct, axis=1), by_head(key, first), NN) * logit
            key_ct = product(jnp.concatenate(scores_ct, axis=0), by_head(query, first), TN) * logit
            value_ct = product(jnp.concatenate(probs, axis=0), by_head(mixed_here, first), TN)
            packed_ref[:, pl.ds(2 * width + pair * 128, 128)] = value_ct.astype(bf16)
            cotangents.append(jnp.concatenate([query_ct, key_ct], axis=0))
        unit_ct = jnp.concatenate(cotangents, axis=1)
        here = pl.ds(quad * QUAD, QUAD)
        units = units_ref[: 2 * CELLS, here].astype(f32)
        along = product((units * unit_ct).astype(bf16), same_head, NN)
        raw_ct = (scales_ref[:, here] * (unit_ct - units * along)).astype(bf16)
        packed_ref[:, here] = raw_ct[:CELLS]
        packed_ref[:, pl.ds(width + quad * QUAD, QUAD)] = raw_ct[CELLS:]

    unit, scale = normed_rows(hidden_ref[...].astype(f32))
    wait(15, 16)
    normed_ct = product(packed_ref[...], qkv_ref[...], NT).astype(bf16).astype(f32) * gain_ref[...]
    hidden_ct = (norm_tangent(unit, scale, normed_ct) + block_ct.astype(f32)).astype(bf16)
    state = product(hidden_ct, embed_ref[...], NT)
    lat_out[...] = quadrant_of(state, HALF_LAT, 0).astype(bf16)
    lon_out[...] = quadrant_of(state, 0, HALF_LON).astype(bf16)
    far_out[...] = quadrant_of(state, HALF_LAT, HALF_LON).astype(bf16)
    own_out[...] = quadrant_of(state, 0, 0).astype(bf16)


def shape(dims, dtype):
    return jax.ShapeDtypeStruct(dims, dtype)


def exchanged(lat_piece, lon_piece, far_piece, steps):
    lat_count, lon_count = lax.axis_size("lat"), lax.axis_size("lon")
    lat_piece = lax.ppermute(lat_piece, "lat", [(i, (i + steps) % lat_count) for i in range(lat_count)])
    lon_piece = lax.ppermute(lon_piece, "lon", [(i, (i + steps) % lon_count) for i in range(lon_count)])
    pairs = [
        (i * lat_count + j, ((i + steps) % lon_count) * lat_count + (j + steps) % lat_count)
        for i in range(lon_count)
        for j in range(lat_count)
    ]
    far_piece = lax.ppermute(far_piece, ("lon", "lat"), pairs)
    return lat_piece, lon_piece, far_piece


def run_forward(
    last_band, logit_scale, background, direction, strips, embed_weight, gain, decode_gain, decode_rows, qkv_weight, out_weight
):
    width = embed_weight.shape[1]
    quarter = shape((QUARTER, background.shape[2]), bf16)
    wide = shape((CELLS, width), bf16)
    kept = [
        wide,
        wide,
        shape((3 * CELLS, width), bf16),
        shape((2 * CELLS, width), f32),
        shape((HEADS // 2, CELLS, 2 * CELLS), bf16),
    ]
    inputs = (last_band, logit_scale, background, direction, strips[1], strips[2], strips[0], embed_weight, gain, decode_gain, decode_rows, qkv_weight, out_weight)
    both = pltpu.VMEM((2 * CELLS, width), bf16)
    return pl.pallas_call(
        forward_kernel,
        out_shape=[quarter] * 4 + kept,
        in_specs=[ANY] * 13,
        out_specs=[VMEM] * 4 + [ANY] * 5,
        scratch_shapes=[pltpu.VMEM(item.shape, item.dtype) for item in inputs]
        + [both, both]
        + [pltpu.VMEM(item.shape, item.dtype) for item in kept[2:]]
        + [both, pltpu.SemaphoreType.DMA((18,)), pltpu.SemaphoreType.DMA((5,))],
        cost_estimate=pl.CostEstimate(flops=2_500_000_000, bytes_accessed=10_000_000, transcendentals=300_000),
        name="forward",
    )(*inputs)


def run_observe(direction, pieces, arrived):
    quarter = shape(pieces[0].shape, bf16)
    devices = arrived.shape[0]
    return pl.pallas_call(
        observe_kernel,
        out_shape=[shape((devices, SLOTS), f32), shape(direction.shape, f32)] + [quarter] * 4,
        in_specs=[VMEM] * 6,
        out_specs=[VMEM] * 6,
        name="observe",
    )(direction, *pieces, arrived)


def run_adjoint(logit_scale, pieces, embed_weight, gain, decode_gain, decode_rows, kept, qkv_weight, out_weight):
    hidden, block, units, scales, probs = kept
    width = embed_weight.shape[1]
    inputs = (*pieces, block, decode_rows, decode_gain, logit_scale, out_weight, units, probs, scales)
    inputs = (*inputs, hidden, gain, embed_weight, qkv_weight)
    return pl.pallas_call(
        adjoint_kernel,
        out_shape=[shape(pieces[0].shape, bf16)] * 4,
        in_specs=[ANY] * len(inputs),
        out_specs=[VMEM] * 4,
        scratch_shapes=[pltpu.VMEM(item.shape, item.dtype) for item in inputs]
        + [pltpu.VMEM((CELLS, 3 * width), bf16), pltpu.SemaphoreType.DMA((len(inputs),))],
        cost_estimate=pl.CostEstimate(flops=1_500_000_000, bytes_accessed=10_000_000, transcendentals=300_000),
        name="adjoint",
    )(*inputs)


def per_device(
    background,
    direction,
    obs_owner,
    obs_site,
    obs_weights,
    obs_precision,
    embed_weight,
    attn_gain,
    qkv_weight,
    logit_scale,
    out_weight,
    decode_gain,
    decode_weight,
):
    var_count = background.shape[2]
    width = embed_weight.shape[1]
    devices = lax.axis_size("lat") * lax.axis_size("lon")
    obs_rows = obs_site.shape[0]
    last_band = (lax.axis_index("lat") == lax.axis_size("lat") - 1).astype(f32).reshape(1, 1)
    logit_scale = logit_scale.reshape(1, HEADS)
    gain = attn_gain.reshape(1, width)
    decode_gain = decode_gain.reshape(1, width)
    decode_rows = decode_weight.T

    owners = obs_owner.reshape(1, obs_rows)
    *strips, outgoing, slots = pl.pallas_call(
        prepare_kernel,
        out_shape=[shape((2 * QUARTER, var_count), bf16)] * 3
        + [shape((devices, SLOTS * 8), f32), shape((1, obs_rows), f32)],
        in_specs=[VMEM] * 6,
        out_specs=[VMEM] * 5,
        name="prepare",
    )(
        background,
        direction,
        owners,
        obs_site.reshape(1, obs_rows),
        obs_weights.T,
        obs_precision.reshape(1, obs_rows),
    )
    strips = exchanged(*strips, -1)
    arrived = lax.all_to_all(outgoing, ("lon", "lat"), split_axis=0, concat_axis=0, tiled=True)

    lat_piece, lon_piece, far_piece, own_piece, *kept = run_forward(
        last_band, logit_scale, background, direction, strips, embed_weight, gain, decode_gain, decode_rows, qkv_weight, out_weight
    )
    lat_piece, lon_piece, far_piece = exchanged(lat_piece, lon_piece, far_piece, 1)

    at_obs, adjoint_field, own_piece, lat_piece, lon_piece, far_piece = run_observe(
        direction, (own_piece, lon_piece, far_piece, lat_piece), arrived
    )
    lat_piece, lon_piece, far_piece = exchanged(lat_piece, lon_piece, far_piece, -1)
    returned = lax.all_to_all(at_obs, ("lon", "lat"), split_axis=0, concat_axis=0, tiled=True)

    own_piece, lat_piece, lon_piece, far_piece = run_adjoint(
        logit_scale, (own_piece, lon_piece, far_piece, lat_piece), embed_weight, gain, decode_gain, decode_rows, kept, qkv_weight, out_weight
    )
    own_piece, returned = lax.optimization_barrier((own_piece, returned))
    lat_piece, lon_piece, far_piece = exchanged(lat_piece, lon_piece, far_piece, 1)

    hvp = adjoint_field
    for piece, row, col in (
        (lon_piece, HALF_LAT, 0),
        (far_piece, 0, 0),
        (lat_piece, 0, HALF_LON),
        (own_piece, HALF_LAT, HALF_LON),
    ):
        piece = piece.reshape(HALF_LAT, HALF_LON, var_count).astype(f32)
        around = ((row, HALF_LAT - row, 0), (col, HALF_LON - col, 0), (0, 0, 0))
        hvp = hvp + lax.pad(piece, jnp.zeros((), f32), around)
    obs_increment = pl.pallas_call(
        unpack_kernel,
        out_shape=shape((1, obs_rows), f32),
        in_specs=[VMEM] * 3,
        out_specs=VMEM,
        name="unpack",
    )(owners, slots, returned)
    return (hvp, obs_increment.reshape(obs_rows))


def solution(mesh):
    in_specs = (
        P("lat", "lon", None),
        P("lat", "lon", None),
        P(("lon", "lat"), None),
        P(("lon", "lat")),
        P(("lon", "lat"), None),
        P(("lon", "lat")),
        P(),
        P(),
        P(),
        P(),
        P(),
        P(),
        P(),
    )
    out_specs = (P("lat", "lon", None), P(("lon", "lat")))
    return jax.shard_map(
        per_device, mesh=mesh, in_specs=in_specs, out_specs=out_specs, check_vma=False
    )
```

```python
import jax
import jax.numpy as jnp
from jax import lax
from jax.experimental import pallas as pl
from jax.experimental.pallas import tpu as pltpu
from jax.sharding import PartitionSpec as P

HEADS = 16
WLAT = 8
WLON = 16
CELLS = WLAT * WLON
HALF_LAT = WLAT // 2
HALF_LON = WLON // 2
QUARTER = HALF_LAT * HALF_LON
SLOTS = 8
PIECES = 2
QUAD = 256

eps_norm = 1e-05
eps_head = 1e-06

f32 = jnp.float32
bf16 = jnp.bfloat16

NN = ((1,), (0,))
NT = ((1,), (1,))
TN = ((0,), (0,))

VMEM = pl.BlockSpec(memory_space=pltpu.VMEM)
SMEM = pl.BlockSpec(memory_space=pltpu.SMEM)
ANY = pl.BlockSpec(memory_space=pl.ANY)


def product(left, right, dims):
    return lax.dot_general(left, right, (dims, ((), ())), preferred_element_type=f32)


def parts_of(value, count):
    parts = []
    for _ in range(count):
        part = value.astype(bf16)
        parts.append(part)
        value = value - part.astype(f32)
    return parts


def quadrants(top_left, bottom_left, top_right, bottom_right):
    rows = []
    for left, right in ((top_left, top_right), (bottom_left, bottom_right)):
        for i in range(HALF_LAT):
            rows.append(left[i * HALF_LON : (i + 1) * HALF_LON])
            rows.append(right[i * HALF_LON : (i + 1) * HALF_LON])
    return jnp.concatenate(rows, axis=0)


def quadrant_of(cells, row, col):
    return jnp.concatenate(
        [cells[(row + i) * WLON + col : (row + i) * WLON + col + HALF_LON] for i in range(HALF_LAT)], axis=0
    )


def normed_rows(values):
    centred = values - jnp.mean(values, axis=-1, keepdims=True)
    scale = lax.rsqrt(jnp.mean(centred * centred, axis=-1, keepdims=True) + eps_norm)
    return centred * scale, scale


def norm_tangent(unit, scale, tangent):
    moved = tangent - jnp.mean(tangent, axis=-1, keepdims=True)
    return scale * (moved - unit * jnp.mean(unit * tangent, axis=-1, keepdims=True))


def normed_with_tangent(values, tangent):
    centred = values - jnp.mean(values, axis=-1, keepdims=True)
    moved = tangent - jnp.mean(tangent, axis=-1, keepdims=True)
    spread = jnp.mean(centred * centred, axis=-1, keepdims=True)
    along = jnp.mean(centred * moved, axis=-1, keepdims=True)
    scale = lax.rsqrt(spread + eps_norm)
    unit = centred * scale
    return unit, scale * (moved - unit * (scale * along))


def same_head_block():
    rows = lax.broadcasted_iota(jnp.int32, (QUAD, QUAD), 0) >> 6
    return (rows == lax.broadcasted_iota(jnp.int32, (QUAD, QUAD), 1) >> 6).astype(bf16)


def by_head(pair, first):
    zero = jnp.zeros((), pair.dtype)
    return jnp.concatenate([jnp.where(first, pair, zero), jnp.where(first, zero, pair)], axis=0)


def halves(value):
    return value[:, :CELLS], value[:, CELLS:]


def slots_of(owners, rows, devices):
    owner_hot = (lax.broadcasted_iota(jnp.int32, (devices, rows), 0) == owners).astype(f32)
    upper = (
        lax.broadcasted_iota(jnp.int32, (rows, rows), 0) <= lax.broadcasted_iota(jnp.int32, (rows, rows), 1)
    ).astype(bf16)
    counted = product(owner_hot.astype(bf16), upper, NN)
    slots = jnp.sum(counted * owner_hot, axis=0, keepdims=True) - 1.0
    return owner_hot, slots


def prepare_kernel(
    background_ref,
    direction_ref,
    owner_ref,
    site_ref,
    weights_ref,
    precision_ref,
    lat_out,
    lon_out,
    far_out,
    out_ref,
    slots_ref,
):
    for piece_out, row, col in ((lat_out, 0, HALF_LON), (lon_out, HALF_LAT, 0), (far_out, 0, 0)):
        pieces = []
        for source in (background_ref, direction_ref):
            for i in range(HALF_LAT):
                pieces.append(source[row + i, col : col + HALF_LON, :])
        piece_out[...] = jnp.concatenate(pieces, axis=0).astype(bf16)
    rows = owner_ref.shape[1]
    devices = out_ref.shape[0]
    owner_hot, slots = slots_of(owner_ref[...], rows, devices)
    slots_ref[...] = slots
    payload = jnp.concatenate(
        [weights_ref[...], precision_ref[...], site_ref[...].astype(f32), jnp.zeros((2, rows), f32)], axis=0
    )
    owner_hot = owner_hot.astype(bf16)
    spread = jnp.concatenate([jnp.where(slots == float(k), payload, 0.0) for k in range(SLOTS)], axis=0)
    out = jnp.zeros((devices, SLOTS * 8), f32)
    for part in parts_of(spread, PIECES):
        out = out + product(owner_hot, part, NT)
    out_ref[...] = out


def unpack_kernel(owner_ref, slots_ref, returned_ref, out_ref):
    rows = owner_ref.shape[1]
    devices = returned_ref.shape[0]
    owner_hot = (lax.broadcasted_iota(jnp.int32, (devices, rows), 0) == owner_ref[...]).astype(bf16)
    picked = jnp.zeros((SLOTS, rows), f32)
    for part in parts_of(returned_ref[...], PIECES):
        picked = picked + product(part, owner_hot, TN)
    slot_hot = lax.broadcasted_iota(jnp.int32, (SLOTS, rows), 0).astype(f32) == slots_ref[...]
    out_ref[...] = jnp.sum(jnp.where(slot_hot, picked, 0.0), axis=0, keepdims=True)


def forward_kernel(
    band_hbm,
    logit_hbm,
    background_hbm,
    direction_hbm,
    lon_hbm,
    far_hbm,
    lat_hbm,
    embed_hbm,
    gain_hbm,
    decode_gain_hbm,
    decode_hbm,
    qkv_hbm,
    outw_hbm,
    lat_out,
    lon_out,
    far_out,
    own_out,
    hidden_hbm,
    block_hbm,
    units_hbm,
    scales_hbm,
    probs_hbm,
    band_ref,
    logit_ref,
    background_ref,
    direction_ref,
    lon_piece,
    far_piece,
    lat_piece,
    embed_ref,
    gain_ref,
    decode_gain_ref,
    decode_ref,
    qkv_ref,
    outw_ref,
    hidden_ref,
    block_ref,
    units_ref,
    scales_ref,
    probs_ref,
    mixed_ref,
    sems_in,
    sems_out,
):
    width = embed_ref.shape[1]
    quads = width // QUAD
    count = 0

    def fetch(source, target):
        nonlocal count
        copy = pltpu.make_async_copy(source, target, sems_in.at[count])
        copy.start()
        count += 1
        return copy

    first_needed = [
        fetch(*pair)
        for pair in (
            (lat_hbm, lat_piece),
            (lon_hbm, lon_piece),
            (far_hbm, far_piece),
            (background_hbm, background_ref),
            (direction_hbm, direction_ref),
            (embed_hbm, embed_ref),
            (gain_hbm, gain_ref),
            (band_hbm, band_ref),
            (logit_hbm, logit_ref),
        )
    ]
    fetched = []
    for half in range(2):
        for third in range(3):
            columns = pl.ds(third * width + half * (width // 2), width // 2)
            fetched.append(fetch(qkv_hbm.at[:, columns], qkv_ref.at[:, columns]))
    last_needed = [
        fetch(*pair) for pair in ((outw_hbm, outw_ref), (decode_gain_hbm, decode_gain_ref), (decode_hbm, decode_ref))
    ]
    kept = []

    def keep(source, target):
        copy = pltpu.make_async_copy(source, target, sems_out.at[len(kept)])
        copy.start()
        kept.append(copy)

    lane = lax.broadcasted_iota(jnp.int32, (1, 128), 1)
    first = lane < 64
    same_head = same_head_block()
    for copy in first_needed:
        copy.wait()
    low_q = lax.broadcasted_iota(jnp.int32, (CELLS, CELLS), 0) < CELLS // 2
    low_k = lax.broadcasted_iota(jnp.int32, (CELLS, CELLS), 1) < CELLS // 2
    allowed = jnp.where(low_q == low_k, 1.0, 1.0 - band_ref[...])
    logits = logit_ref[...]
    states = []
    for number, source in enumerate((background_ref, direction_ref)):
        own = jnp.concatenate([source[HALF_LAT + i, HALF_LON:, :] for i in range(HALF_LAT)], axis=0)
        part = slice(number * QUARTER, (number + 1) * QUARTER)
        received = [piece[part, :].astype(f32) for piece in (lat_piece, lon_piece, far_piece)]
        states.append(quadrants(own, *received))
    states = jnp.concatenate(states, axis=0).astype(bf16)
    hidden = product(states, embed_ref[...], NN).astype(bf16)
    hidden_ref[...] = hidden
    keep(hidden_ref.at[:CELLS], hidden_hbm)
    hidden = hidden.astype(f32)
    gain = gain_ref[...]
    normed = jnp.concatenate(
        [part * gain for part in normed_with_tangent(hidden[:CELLS], hidden[CELLS:])], axis=0
    ).astype(bf16)

    def project(quad):
        here = pl.ds(quad * QUAD, QUAD)
        packed = []
        for third in range(3):
            packed.append(product(normed, qkv_ref[:, pl.ds(third * width + quad * QUAD, QUAD)], NN))
        raw = jnp.concatenate([packed[0][:CELLS], packed[1][:CELLS]], axis=0)
        raw_tan = jnp.concatenate([packed[0][CELLS:], packed[1][CELLS:]], axis=0)
        scale = lax.rsqrt(product((raw * raw).astype(bf16), same_head, NN) + eps_head)
        unit = raw * scale
        along = product((unit * raw_tan).astype(bf16), same_head, NN)
        unit_tan = (scale * (raw_tan - unit * along)).astype(bf16)
        unit = unit.astype(bf16)
        value = packed[2].astype(bf16)
        scales_ref[:, here] = scale
        units_ref[: 2 * CELLS, here] = unit
        units_ref[2 * CELLS :, here] = value[:CELLS]
        return unit, unit_tan, value

    def attend(quad, unit, unit_tan, value):
        for side in range(2):
            pair = quad * 2 + side
            lanes = slice(side * 128, (side + 1) * 128)
            query, key = unit[:CELLS, lanes], by_head(unit[CELLS:, lanes], first)
            query_tan, key_tan = unit_tan[:CELLS, lanes], by_head(unit_tan[CELLS:, lanes], first)
            values = jnp.concatenate(
                [by_head(value[:CELLS, lanes], first), by_head(value[CELLS:, lanes], first)], axis=1
            )
            scores = product(query, key, NT)
            scores_tan = product(
                jnp.concatenate([query, query_tan], axis=1), jnp.concatenate([key_tan, key], axis=1), NT
            )
            probs, probs_tan = [], []
            for half, (score, score_tan) in enumerate(zip(halves(scores), halves(scores_tan))):
                head = pair * 2 + half
                logit = logits[:, head : head + 1]
                weights = jnp.exp(score * logit) * allowed
                prob = weights * (1.0 / jnp.sum(weights, axis=-1, keepdims=True))
                score_tan = score_tan * logit
                prob_tan = prob * (score_tan - jnp.sum(prob * score_tan, axis=-1, keepdims=True))
                probs.append(prob.astype(bf16))
                probs_tan.append(prob_tan.astype(bf16))
            probs = jnp.concatenate(probs, axis=1)
            probs_ref[pair] = probs
            mixed, mixed_tan = halves(product(probs, values, NN))
            mixed_tan = mixed_tan + product(jnp.concatenate(probs_tan, axis=1), values[:, :128], NN)
            columns = pl.ds(pair * 128, 128)
            mixed_ref[:CELLS, columns] = mixed.astype(bf16)
            mixed_ref[CELLS:, columns] = mixed_tan.astype(bf16)

    for copy in fetched[0:3]:
        copy.wait()
    vals0 = project(0)
    vals1 = project(1)
    for copy in fetched[3:6]:
        copy.wait()
    vals2 = project(2)
    vals3 = project(3)
    attend(0, *vals0)
    attend(1, *vals1)
    attend(2, *vals2)
    attend(3, *vals3)

    keep(units_ref, units_hbm)
    keep(scales_ref, scales_hbm)
    keep(probs_ref, probs_hbm)
    for copy in last_needed:
        copy.wait()
    block = (hidden_ref[...].astype(f32) + product(mixed_ref[...], outw_ref[...], NN)).astype(bf16)
    block_ref[...] = block
    keep(block_ref.at[:CELLS], block_hbm)
    block = block.astype(f32)
    moved = normed_with_tangent(block[:CELLS], block[CELLS:])[1]
    change = product((moved * decode_gain_ref[...]).astype(bf16), decode_ref[...], NT)
    lat_out[...] = quadrant_of(change, HALF_LAT, 0).astype(bf16)
    lon_out[...] = quadrant_of(change, 0, HALF_LON).astype(bf16)
    far_out[...] = quadrant_of(change, HALF_LAT, HALF_LON).astype(bf16)
    own_out[...] = quadrant_of(change, 0, 0).astype(bf16)
    for copy in kept:
        copy.wait()


def observe_kernel(
    direction_ref,
    own_piece,
    lon_piece,
    far_piece,
    lat_piece,
    arrived_ref,
    at_obs_out,
    adjoint_out,
    own_out,
    lat_out,
    lon_out,
    far_out,
):
    var_count = direction_ref.shape[2]
    devices = arrived_ref.shape[0]
    pieces = [piece[...].astype(f32) for piece in (far_piece, lon_piece, lat_piece, own_piece)]
    moved = quadrants(*pieces)
    tangent = jnp.concatenate([direction_ref[i] for i in range(WLAT)], axis=0) + moved
    arrived = jnp.transpose(arrived_ref[...])
    cell_ids = lax.broadcasted_iota(jnp.int32, (CELLS, devices), 0).astype(f32)
    var_ids = lax.broadcasted_iota(jnp.int32, (var_count, devices), 0).astype(f32)
    selectors, var_hots, precisions = [], [], []
    for k in range(SLOTS):
        row = arrived[k * 8 : (k + 1) * 8]
        site = row[5:6]
        cell = jnp.floor((site + 0.5) * (1.0 / var_count))
        variable = site - cell * var_count
        selector = jnp.zeros((CELLS, devices), f32)
        for corner, offset in enumerate((0, 1, WLON, WLON + 1)):
            selector = selector + jnp.where(cell_ids == cell + float(offset), row[corner : corner + 1], 0.0)
        selectors.append(selector)
        var_hots.append((var_ids == variable).astype(f32))
        precisions.append(row[4:5])
    selector = jnp.concatenate(selectors, axis=1)
    var_hot = jnp.concatenate(var_hots, axis=1)
    precision = jnp.concatenate(precisions, axis=1)
    selector_parts = parts_of(selector, 2)
    tangent_parts = parts_of(tangent, 3)
    picked = product(tangent_parts[0], selector_parts[0], TN)
    for left, right in ((1, 0), (0, 1), (2, 0)):
        picked = picked + product(tangent_parts[left], selector_parts[right], TN)
    at_obs = jnp.sum(picked * var_hot, axis=0, keepdims=True)
    at_obs_out[...] = jnp.transpose(
        jnp.concatenate([at_obs[:, k * devices : (k + 1) * devices] for k in range(SLOTS)], axis=0)
    )
    spread_parts = parts_of(var_hot * (at_obs * precision), 2)
    adjoint = product(selector_parts[0], spread_parts[0], NT)
    for left, right in ((1, 0), (0, 1)):
        adjoint = adjoint + product(selector_parts[left], spread_parts[right], NT)
    for i in range(WLAT):
        adjoint_out[i] = adjoint[i * WLON : (i + 1) * WLON]
    own_out[...] = quadrant_of(adjoint, HALF_LAT, HALF_LON).astype(bf16)
    lat_out[...] = quadrant_of(adjoint, 0, HALF_LON).astype(bf16)
    lon_out[...] = quadrant_of(adjoint, HALF_LAT, 0).astype(bf16)
    far_out[...] = quadrant_of(adjoint, 0, 0).astype(bf16)


def adjoint_kernel(
    own_hbm,
    lon_hbm,
    far_hbm,
    lat_hbm,
    block_hbm,
    decode_hbm,
    decode_gain_hbm,
    logit_hbm,
    outw_hbm,
    units_hbm,
    probs_hbm,
    scales_hbm,
    hidden_hbm,
    gain_hbm,
    embed_hbm,
    qkv_hbm,
    own_out,
    lat_out,
    lon_out,
    far_out,
    own_piece,
    lon_piece,
    far_piece,
    lat_piece,
    block_ref,
    decode_ref,
    decode_gain_ref,
    logit_ref,
    outw_ref,
    units_ref,
    probs_ref,
    scales_ref,
    hidden_ref,
    gain_ref,
    embed_ref,
    qkv_ref,
    packed_ref,
    sems,
):
    width = embed_ref.shape[1]
    quads = width // QUAD
    fetched = []

    def fetch(source, target):
        copy = pltpu.make_async_copy(source, target, sems.at[len(fetched)])
        copy.start()
        fetched.append(copy)

    for source, target in (
        (own_hbm, own_piece),
        (lon_hbm, lon_piece),
        (far_hbm, far_piece),
        (lat_hbm, lat_piece),
        (block_hbm, block_ref),
        (decode_hbm, decode_ref),
        (decode_gain_hbm, decode_gain_ref),
        (logit_hbm, logit_ref),
        (outw_hbm, outw_ref),
        (units_hbm, units_ref),
        (probs_hbm, probs_ref),
        (scales_hbm, scales_ref),
        (hidden_hbm, hidden_ref),
        (gain_hbm, gain_ref),
        (embed_hbm, embed_ref),
        (qkv_hbm, qkv_ref),
    ):
        fetch(source, target)

    def wait(start, stop):
        for copy in fetched[start:stop]:
            copy.wait()

    wait(0, 8)
    change = quadrants(*[piece[...].astype(f32) for piece in (own_piece, lat_piece, lon_piece, far_piece)])
    unit, scale = normed_rows(block_ref[...].astype(f32))
    normed_ct = product(change.astype(bf16), decode_ref[...], NN).astype(bf16).astype(f32) * decode_gain_ref[...]
    block_ct = norm_tangent(unit, scale, normed_ct).astype(bf16)
    wait(8, 9)
    mixed_ct = product(block_ct, outw_ref[...], NT).astype(bf16)

    lane = lax.broadcasted_iota(jnp.int32, (1, 128), 1)
    first = lane < 64
    same_head = same_head_block()
    logits = logit_ref[...]
    wait(9, 15)
    for quad in range(quads):
        cotangents = []
        for side in range(2):
            pair = quad * 2 + side
            here = pl.ds(pair * 128, 128)
            query, key, value = (units_ref[i * CELLS : (i + 1) * CELLS, here] for i in range(3))
            mixed_here = mixed_ct[:, pair * 128 : (pair + 1) * 128]
            probs = halves(probs_ref[pair])
            scores_ct = []
            for prob, prob_ct in zip(probs, halves(product(mixed_here, by_head(value, first), NT))):
                prob = prob.astype(f32)
                scores_ct.append((prob * (prob_ct - jnp.sum(prob * prob_ct, axis=-1, keepdims=True))).astype(bf16))
            head = pair * 2
            logit = jnp.where(first, logits[:, head : head + 1], logits[:, head + 1 : head + 2])
            query_ct = product(jnp.concatenate(scores_ct, axis=1), by_head(key, first), NN) * logit
            key_ct = product(jnp.concatenate(scores_ct, axis=0), by_head(query, first), TN) * logit
            value_ct = product(jnp.concatenate(probs, axis=0), by_head(mixed_here, first), TN)
            packed_ref[:, pl.ds(2 * width + pair * 128, 128)] = value_ct.astype(bf16)
            cotangents.append(jnp.concatenate([query_ct, key_ct], axis=0))
        unit_ct = jnp.concatenate(cotangents, axis=1)
        here = pl.ds(quad * QUAD, QUAD)
        units = units_ref[: 2 * CELLS, here].astype(f32)
        along = product((units * unit_ct).astype(bf16), same_head, NN)
        raw_ct = (scales_ref[:, here] * (unit_ct - units * along)).astype(bf16)
        packed_ref[:, here] = raw_ct[:CELLS]
        packed_ref[:, pl.ds(width + quad * QUAD, QUAD)] = raw_ct[CELLS:]

    unit, scale = normed_rows(hidden_ref[...].astype(f32))
    wait(15, 16)
    normed_ct = product(packed_ref[...], qkv_ref[...], NT).astype(bf16).astype(f32) * gain_ref[...]
    hidden_ct = (norm_tangent(unit, scale, normed_ct) + block_ct.astype(f32)).astype(bf16)
    state = product(hidden_ct, embed_ref[...], NT)
    lat_out[...] = quadrant_of(state, HALF_LAT, 0).astype(bf16)
    lon_out[...] = quadrant_of(state, 0, HALF_LON).astype(bf16)
    far_out[...] = quadrant_of(state, HALF_LAT, HALF_LON).astype(bf16)
    own_out[...] = quadrant_of(state, 0, 0).astype(bf16)


def shape(dims, dtype):
    return jax.ShapeDtypeStruct(dims, dtype)


def exchanged(lat_piece, lon_piece, far_piece, steps):
    lat_count, lon_count = lax.axis_size("lat"), lax.axis_size("lon")
    lat_piece = lax.ppermute(lat_piece, "lat", [(i, (i + steps) % lat_count) for i in range(lat_count)])
    lon_piece = lax.ppermute(lon_piece, "lon", [(i, (i + steps) % lon_count) for i in range(lon_count)])
    pairs = [
        (i * lat_count + j, ((i + steps) % lon_count) * lat_count + (j + steps) % lat_count)
        for i in range(lon_count)
        for j in range(lat_count)
    ]
    far_piece = lax.ppermute(far_piece, ("lon", "lat"), pairs)
    return lat_piece, lon_piece, far_piece


def run_forward(
    last_band, logit_scale, background, direction, strips, embed_weight, gain, decode_gain, decode_rows, qkv_weight, out_weight
):
    width = embed_weight.shape[1]
    quarter = shape((QUARTER, background.shape[2]), bf16)
    wide = shape((CELLS, width), bf16)
    kept = [
        wide,
        wide,
        shape((3 * CELLS, width), bf16),
        shape((2 * CELLS, width), f32),
        shape((HEADS // 2, CELLS, 2 * CELLS), bf16),
    ]
    inputs = (last_band, logit_scale, background, direction, *(pltpu.with_memory_space_constraint(strips[i], pltpu.VMEM) for i in (1, 2, 0)), embed_weight, gain, decode_gain, decode_rows, qkv_weight, out_weight)
    both = pltpu.VMEM((2 * CELLS, width), bf16)
    return pl.pallas_call(
        forward_kernel,
        out_shape=[pltpu.VMEM(quarter.shape, bf16)] * 4 + kept,
        in_specs=[ANY] * 13,
        out_specs=[VMEM] * 4 + [ANY] * 5,
        scratch_shapes=[pltpu.VMEM(item.shape, item.dtype) for item in inputs]
        + [both, both]
        + [pltpu.VMEM(item.shape, item.dtype) for item in kept[2:]]
        + [both, pltpu.SemaphoreType.DMA((18,)), pltpu.SemaphoreType.DMA((5,))],
        cost_estimate=pl.CostEstimate(flops=2_500_000_000, bytes_accessed=10_000_000, transcendentals=300_000),
        name="forward",
    )(*inputs)


def run_observe(direction, pieces, arrived):
    quarter = shape(pieces[0].shape, bf16)
    devices = arrived.shape[0]
    return pl.pallas_call(
        observe_kernel,
        out_shape=[pltpu.VMEM((devices, SLOTS), f32), shape(direction.shape, f32)] + [pltpu.VMEM(quarter.shape, bf16)] * 4,
        in_specs=[VMEM] * 6,
        out_specs=[VMEM] * 6,
        compiler_params=pltpu.CompilerParams(vmem_limit_bytes=2 * 1024 * 1024),
        name="observe",
    )(direction, pltpu.with_memory_space_constraint(pieces[0], pltpu.VMEM), *pieces[1:], arrived)


def run_adjoint(logit_scale, pieces, embed_weight, gain, decode_gain, decode_rows, kept, qkv_weight, out_weight):
    hidden, block, units, scales, probs = kept
    width = embed_weight.shape[1]
    pieces = [pltpu.with_memory_space_constraint(piece, pltpu.VMEM) for piece in pieces]
    inputs = (*pieces, block, decode_rows, decode_gain, logit_scale, out_weight, units, probs, scales)
    inputs = (*inputs, hidden, gain, embed_weight, qkv_weight)
    return pl.pallas_call(
        adjoint_kernel,
        out_shape=[pltpu.VMEM(pieces[0].shape, bf16)] * 4,
        in_specs=[ANY] * len(inputs),
        out_specs=[VMEM] * 4,
        scratch_shapes=[pltpu.VMEM(item.shape, item.dtype) for item in inputs]
        + [pltpu.VMEM((CELLS, 3 * width), bf16), pltpu.SemaphoreType.DMA((len(inputs),))],
        cost_estimate=pl.CostEstimate(flops=1_500_000_000, bytes_accessed=10_000_000, transcendentals=300_000),
        name="adjoint",
    )(*inputs)


def per_device(
    background,
    direction,
    obs_owner,
    obs_site,
    obs_weights,
    obs_precision,
    embed_weight,
    attn_gain,
    qkv_weight,
    logit_scale,
    out_weight,
    decode_gain,
    decode_weight,
):
    var_count = background.shape[2]
    width = embed_weight.shape[1]
    devices = lax.axis_size("lat") * lax.axis_size("lon")
    obs_rows = obs_site.shape[0]
    last_band = (lax.axis_index("lat") == lax.axis_size("lat") - 1).astype(f32).reshape(1, 1)
    logit_scale = logit_scale.reshape(1, HEADS)
    gain = attn_gain.reshape(1, width)
    decode_gain = decode_gain.reshape(1, width)
    decode_rows = decode_weight.T

    owners = obs_owner.reshape(1, obs_rows)
    *strips, outgoing, slots = pl.pallas_call(
        prepare_kernel,
        out_shape=[pltpu.VMEM((2 * QUARTER, var_count), bf16)] * 3
        + [pltpu.VMEM((devices, SLOTS * 8), f32), shape((1, obs_rows), f32)],
        in_specs=[VMEM] * 6,
        out_specs=[VMEM] * 5,
        name="prepare",
    )(
        background,
        direction,
        owners,
        obs_site.reshape(1, obs_rows),
        obs_weights.T,
        obs_precision.reshape(1, obs_rows),
    )
    strips = exchanged(*strips, -1)
    arrived = lax.all_to_all(outgoing, ("lon", "lat"), split_axis=0, concat_axis=0, tiled=True)

    lat_piece, lon_piece, far_piece, own_piece, *kept = run_forward(
        last_band, logit_scale, background, direction, strips, embed_weight, gain, decode_gain, decode_rows, qkv_weight, out_weight
    )
    lat_piece, lon_piece, far_piece = exchanged(lat_piece, lon_piece, far_piece, 1)

    at_obs, adjoint_field, own_piece, lat_piece, lon_piece, far_piece = run_observe(
        direction, (own_piece, lon_piece, far_piece, lat_piece), arrived
    )
    lat_piece, lon_piece, far_piece = exchanged(lat_piece, lon_piece, far_piece, -1)
    returned = lax.all_to_all(at_obs, ("lon", "lat"), split_axis=0, concat_axis=0, tiled=True)

    own_piece, lat_piece, lon_piece, far_piece = run_adjoint(
        logit_scale, (own_piece, lon_piece, far_piece, lat_piece), embed_weight, gain, decode_gain, decode_rows, kept, qkv_weight, out_weight
    )
    own_piece, returned = lax.optimization_barrier((own_piece, returned))
    lat_piece, lon_piece, far_piece = exchanged(lat_piece, lon_piece, far_piece, 1)

    hvp = adjoint_field
    for piece, row, col in (
        (lon_piece, HALF_LAT, 0),
        (far_piece, 0, 0),
        (lat_piece, 0, HALF_LON),
        (own_piece, HALF_LAT, HALF_LON),
    ):
        piece = piece.reshape(HALF_LAT, HALF_LON, var_count).astype(f32)
        around = ((row, HALF_LAT - row, 0), (col, HALF_LON - col, 0), (0, 0, 0))
        hvp = hvp + lax.pad(piece, jnp.zeros((), f32), around)
    obs_increment = pl.pallas_call(
        unpack_kernel,
        out_shape=shape((1, obs_rows), f32),
        in_specs=[VMEM] * 3,
        out_specs=VMEM,
        name="unpack",
    )(owners, slots, returned)
    return (hvp, obs_increment.reshape(obs_rows))


def solution(mesh):
    in_specs = (
        P("lat", "lon", None),
        P("lat", "lon", None),
        P(("lon", "lat"), None),
        P(("lon", "lat")),
        P(("lon", "lat"), None),
        P(("lon", "lat")),
        P(),
        P(),
        P(),
        P(),
        P(),
        P(),
        P(),
    )
    out_specs = (P("lat", "lon", None), P(("lon", "lat")))
    return jax.shard_map(
        per_device, mesh=mesh, in_specs=in_specs, out_specs=out_specs, check_vma=False
    )
```

```python
import jax
import jax.numpy as jnp
from jax import lax
from jax.experimental import pallas as pl
from jax.experimental.pallas import tpu as pltpu
from jax.sharding import PartitionSpec as P

HEADS = 16
WLAT = 8
WLON = 16
CELLS = WLAT * WLON
HALF_LAT = WLAT // 2
HALF_LON = WLON // 2
QUARTER = HALF_LAT * HALF_LON
SLOTS = 8
PIECES = 2
QUAD = 256

eps_norm = 1e-05
eps_head = 1e-06

f32 = jnp.float32
bf16 = jnp.bfloat16

NN = ((1,), (0,))
NT = ((1,), (1,))
TN = ((0,), (0,))

VMEM = pl.BlockSpec(memory_space=pltpu.VMEM)
SMEM = pl.BlockSpec(memory_space=pltpu.SMEM)
ANY = pl.BlockSpec(memory_space=pl.ANY)


def product(left, right, dims):
    return lax.dot_general(left, right, (dims, ((), ())), preferred_element_type=f32)


def parts_of(value, count):
    parts = []
    for _ in range(count):
        part = value.astype(bf16)
        parts.append(part)
        value = value - part.astype(f32)
    return parts


def quadrants(top_left, bottom_left, top_right, bottom_right):
    rows = []
    for left, right in ((top_left, top_right), (bottom_left, bottom_right)):
        for i in range(HALF_LAT):
            rows.append(left[i * HALF_LON : (i + 1) * HALF_LON])
            rows.append(right[i * HALF_LON : (i + 1) * HALF_LON])
    return jnp.concatenate(rows, axis=0)


def quadrant_of(cells, row, col):
    return jnp.concatenate(
        [cells[(row + i) * WLON + col : (row + i) * WLON + col + HALF_LON] for i in range(HALF_LAT)], axis=0
    )


def normed_rows(values):
    centred = values - jnp.mean(values, axis=-1, keepdims=True)
    scale = lax.rsqrt(jnp.mean(centred * centred, axis=-1, keepdims=True) + eps_norm)
    return centred * scale, scale


def norm_tangent(unit, scale, tangent):
    moved = tangent - jnp.mean(tangent, axis=-1, keepdims=True)
    return scale * (moved - unit * jnp.mean(unit * tangent, axis=-1, keepdims=True))


def normed_with_tangent(values, tangent):
    centred = values - jnp.mean(values, axis=-1, keepdims=True)
    moved = tangent - jnp.mean(tangent, axis=-1, keepdims=True)
    spread = jnp.mean(centred * centred, axis=-1, keepdims=True)
    along = jnp.mean(centred * moved, axis=-1, keepdims=True)
    scale = lax.rsqrt(spread + eps_norm)
    unit = centred * scale
    return unit, scale * (moved - unit * (scale * along))


def same_head_block():
    rows = lax.broadcasted_iota(jnp.int32, (QUAD, QUAD), 0) >> 6
    return (rows == lax.broadcasted_iota(jnp.int32, (QUAD, QUAD), 1) >> 6).astype(bf16)


def by_head(pair, first):
    zero = jnp.zeros((), pair.dtype)
    return jnp.concatenate([jnp.where(first, pair, zero), jnp.where(first, zero, pair)], axis=0)


def halves(value):
    return value[:, :CELLS], value[:, CELLS:]


def slots_of(owners, rows, devices):
    owner_hot = (lax.broadcasted_iota(jnp.int32, (devices, rows), 0) == owners).astype(f32)
    upper = (
        lax.broadcasted_iota(jnp.int32, (rows, rows), 0) <= lax.broadcasted_iota(jnp.int32, (rows, rows), 1)
    ).astype(bf16)
    counted = product(owner_hot.astype(bf16), upper, NN)
    slots = jnp.sum(counted * owner_hot, axis=0, keepdims=True) - 1.0
    return owner_hot, slots


def prepare_kernel(
    background_ref,
    direction_ref,
    owner_ref,
    site_ref,
    weights_ref,
    precision_ref,
    lat_out,
    lon_out,
    far_out,
    out_ref,
    slots_ref,
):
    for piece_out, row, col in ((lat_out, 0, HALF_LON), (lon_out, HALF_LAT, 0), (far_out, 0, 0)):
        pieces = []
        for source in (background_ref, direction_ref):
            for i in range(HALF_LAT):
                pieces.append(source[row + i, col : col + HALF_LON, :])
        piece_out[...] = jnp.concatenate(pieces, axis=0).astype(bf16)
    rows = owner_ref.shape[1]
    devices = out_ref.shape[0]
    owner_hot, slots = slots_of(owner_ref[...], rows, devices)
    slots_ref[...] = slots
    payload = jnp.concatenate(
        [weights_ref[...], precision_ref[...], site_ref[...].astype(f32), jnp.zeros((2, rows), f32)], axis=0
    )
    owner_hot = owner_hot.astype(bf16)
    spread = jnp.concatenate([jnp.where(slots == float(k), payload, 0.0) for k in range(SLOTS)], axis=0)
    out = jnp.zeros((devices, SLOTS * 8), f32)
    for part in parts_of(spread, PIECES):
        out = out + product(owner_hot, part, NT)
    out_ref[...] = out


def unpack_kernel(owner_ref, slots_ref, returned_ref, out_ref):
    rows = owner_ref.shape[1]
    devices = returned_ref.shape[0]
    owner_hot = (lax.broadcasted_iota(jnp.int32, (devices, rows), 0) == owner_ref[...]).astype(bf16)
    picked = jnp.zeros((SLOTS, rows), f32)
    for part in parts_of(returned_ref[...], PIECES):
        picked = picked + product(part, owner_hot, TN)
    slot_hot = lax.broadcasted_iota(jnp.int32, (SLOTS, rows), 0).astype(f32) == slots_ref[...]
    out_ref[...] = jnp.sum(jnp.where(slot_hot, picked, 0.0), axis=0, keepdims=True)


def forward_kernel(
    band_hbm,
    logit_hbm,
    background_hbm,
    direction_hbm,
    lon_piece,
    far_piece,
    lat_piece,
    embed_hbm,
    gain_hbm,
    decode_gain_hbm,
    decode_hbm,
    qkv_hbm,
    outw_hbm,
    lat_out,
    lon_out,
    far_out,
    own_out,
    hidden_hbm,
    block_hbm,
    units_hbm,
    scales_hbm,
    probs_hbm,
    band_ref,
    logit_ref,
    background_ref,
    direction_ref,
    embed_ref,
    gain_ref,
    decode_gain_ref,
    decode_ref,
    qkv_ref,
    outw_ref,
    hidden_ref,
    block_ref,
    units_ref,
    scales_ref,
    probs_ref,
    mixed_ref,
    sems_in,
    sems_out,
):
    width = embed_ref.shape[1]
    quads = width // QUAD
    count = 0

    def fetch(source, target):
        nonlocal count
        copy = pltpu.make_async_copy(source, target, sems_in.at[count])
        copy.start()
        count += 1
        return copy

    first_needed = [
        fetch(*pair)
        for pair in (
            (background_hbm, background_ref),
            (direction_hbm, direction_ref),
            (embed_hbm, embed_ref),
            (gain_hbm, gain_ref),
            (band_hbm, band_ref),
            (logit_hbm, logit_ref),
        )
    ]
    fetched = []
    for half in range(2):
        for third in range(3):
            columns = pl.ds(third * width + half * (width // 2), width // 2)
            fetched.append(fetch(qkv_hbm.at[:, columns], qkv_ref.at[:, columns]))
    last_needed = [
        fetch(*pair) for pair in ((outw_hbm, outw_ref), (decode_gain_hbm, decode_gain_ref), (decode_hbm, decode_ref))
    ]
    kept = []

    def keep(source, target):
        copy = pltpu.make_async_copy(source, target, sems_out.at[len(kept)])
        copy.start()
        kept.append(copy)

    lane = lax.broadcasted_iota(jnp.int32, (1, 128), 1)
    first = lane < 64
    same_head = same_head_block()
    for copy in first_needed:
        copy.wait()
    low_q = lax.broadcasted_iota(jnp.int32, (CELLS, CELLS), 0) < CELLS // 2
    low_k = lax.broadcasted_iota(jnp.int32, (CELLS, CELLS), 1) < CELLS // 2
    allowed = jnp.where(low_q == low_k, 1.0, 1.0 - band_ref[...])
    logits = logit_ref[...]
    states = []
    for number, source in enumerate((background_ref, direction_ref)):
        own = jnp.concatenate([source[HALF_LAT + i, HALF_LON:, :] for i in range(HALF_LAT)], axis=0)
        part = slice(number * QUARTER, (number + 1) * QUARTER)
        received = [piece[part, :].astype(f32) for piece in (lat_piece, lon_piece, far_piece)]
        states.append(quadrants(own, *received))
    states = jnp.concatenate(states, axis=0).astype(bf16)
    hidden = product(states, embed_ref[...], NN).astype(bf16)
    hidden_ref[...] = hidden
    keep(hidden_ref.at[:CELLS], hidden_hbm)
    hidden = hidden.astype(f32)
    gain = gain_ref[...]
    normed = jnp.concatenate(
        [part * gain for part in normed_with_tangent(hidden[:CELLS], hidden[CELLS:])], axis=0
    ).astype(bf16)

    def project(quad):
        here = pl.ds(quad * QUAD, QUAD)
        packed = []
        for third in range(3):
            packed.append(product(normed, qkv_ref[:, pl.ds(third * width + quad * QUAD, QUAD)], NN))
        raw = jnp.concatenate([packed[0][:CELLS], packed[1][:CELLS]], axis=0)
        raw_tan = jnp.concatenate([packed[0][CELLS:], packed[1][CELLS:]], axis=0)
        scale = lax.rsqrt(product((raw * raw).astype(bf16), same_head, NN) + eps_head)
        unit = raw * scale
        along = product((unit * raw_tan).astype(bf16), same_head, NN)
        unit_tan = (scale * (raw_tan - unit * along)).astype(bf16)
        unit = unit.astype(bf16)
        value = packed[2].astype(bf16)
        scales_ref[:, here] = scale
        units_ref[: 2 * CELLS, here] = unit
        units_ref[2 * CELLS :, here] = value[:CELLS]
        return unit, unit_tan, value

    def attend(quad, unit, unit_tan, value):
        for side in range(2):
            pair = quad * 2 + side
            lanes = slice(side * 128, (side + 1) * 128)
            query, key = unit[:CELLS, lanes], by_head(unit[CELLS:, lanes], first)
            query_tan, key_tan = unit_tan[:CELLS, lanes], by_head(unit_tan[CELLS:, lanes], first)
            values = jnp.concatenate(
                [by_head(value[:CELLS, lanes], first), by_head(value[CELLS:, lanes], first)], axis=1
            )
            scores = product(query, key, NT)
            scores_tan = product(
                jnp.concatenate([query, query_tan], axis=1), jnp.concatenate([key_tan, key], axis=1), NT
            )
            probs, probs_tan = [], []
            for half, (score, score_tan) in enumerate(zip(halves(scores), halves(scores_tan))):
                head = pair * 2 + half
                logit = logits[:, head : head + 1]
                weights = jnp.exp(score * logit) * allowed
                prob = weights * (1.0 / jnp.sum(weights, axis=-1, keepdims=True))
                score_tan = score_tan * logit
                prob_tan = prob * (score_tan - jnp.sum(prob * score_tan, axis=-1, keepdims=True))
                probs.append(prob.astype(bf16))
                probs_tan.append(prob_tan.astype(bf16))
            probs = jnp.concatenate(probs, axis=1)
            probs_ref[pair] = probs
            mixed, mixed_tan = halves(product(probs, values, NN))
            mixed_tan = mixed_tan + product(jnp.concatenate(probs_tan, axis=1), values[:, :128], NN)
            columns = pl.ds(pair * 128, 128)
            mixed_ref[:CELLS, columns] = mixed.astype(bf16)
            mixed_ref[CELLS:, columns] = mixed_tan.astype(bf16)

    for copy in fetched[0:3]:
        copy.wait()
    vals0 = project(0)
    vals1 = project(1)
    for copy in fetched[3:6]:
        copy.wait()
    vals2 = project(2)
    vals3 = project(3)
    attend(0, *vals0)
    attend(1, *vals1)
    attend(2, *vals2)
    attend(3, *vals3)

    keep(units_ref, units_hbm)
    keep(scales_ref, scales_hbm)
    keep(probs_ref, probs_hbm)
    for copy in last_needed:
        copy.wait()
    block = (hidden_ref[...].astype(f32) + product(mixed_ref[...], outw_ref[...], NN)).astype(bf16)
    block_ref[...] = block
    keep(block_ref.at[:CELLS], block_hbm)
    block = block.astype(f32)
    moved = normed_with_tangent(block[:CELLS], block[CELLS:])[1]
    change = product((moved * decode_gain_ref[...]).astype(bf16), decode_ref[...], NT)
    lat_out[...] = quadrant_of(change, HALF_LAT, 0).astype(bf16)
    lon_out[...] = quadrant_of(change, 0, HALF_LON).astype(bf16)
    far_out[...] = quadrant_of(change, HALF_LAT, HALF_LON).astype(bf16)
    own_out[...] = quadrant_of(change, 0, 0).astype(bf16)
    for copy in kept:
        copy.wait()


def observe_kernel(
    direction_ref,
    own_piece,
    lon_piece,
    far_piece,
    lat_piece,
    arrived_ref,
    at_obs_out,
    adjoint_out,
    own_out,
    lat_out,
    lon_out,
    far_out,
):
    var_count = direction_ref.shape[2]
    devices = arrived_ref.shape[0]
    pieces = [piece[...].astype(f32) for piece in (far_piece, lon_piece, lat_piece, own_piece)]
    moved = quadrants(*pieces)
    tangent = jnp.concatenate([direction_ref[i] for i in range(WLAT)], axis=0) + moved
    arrived = jnp.transpose(arrived_ref[...])
    cell_ids = lax.broadcasted_iota(jnp.int32, (CELLS, devices), 0).astype(f32)
    var_ids = lax.broadcasted_iota(jnp.int32, (var_count, devices), 0).astype(f32)
    selectors, var_hots, precisions = [], [], []
    for k in range(SLOTS):
        row = arrived[k * 8 : (k + 1) * 8]
        site = row[5:6]
        cell = jnp.floor((site + 0.5) * (1.0 / var_count))
        variable = site - cell * var_count
        selector = jnp.zeros((CELLS, devices), f32)
        for corner, offset in enumerate((0, 1, WLON, WLON + 1)):
            selector = selector + jnp.where(cell_ids == cell + float(offset), row[corner : corner + 1], 0.0)
        selectors.append(selector)
        var_hots.append((var_ids == variable).astype(f32))
        precisions.append(row[4:5])
    selector = jnp.concatenate(selectors, axis=1)
    var_hot = jnp.concatenate(var_hots, axis=1)
    precision = jnp.concatenate(precisions, axis=1)
    selector_parts = parts_of(selector, 2)
    tangent_parts = parts_of(tangent, 3)
    picked = product(tangent_parts[0], selector_parts[0], TN)
    for left, right in ((1, 0), (0, 1), (2, 0)):
        picked = picked + product(tangent_parts[left], selector_parts[right], TN)
    at_obs = jnp.sum(picked * var_hot, axis=0, keepdims=True)
    at_obs_out[...] = jnp.transpose(
        jnp.concatenate([at_obs[:, k * devices : (k + 1) * devices] for k in range(SLOTS)], axis=0)
    )
    spread_parts = parts_of(var_hot * (at_obs * precision), 2)
    adjoint = product(selector_parts[0], spread_parts[0], NT)
    for left, right in ((1, 0), (0, 1)):
        adjoint = adjoint + product(selector_parts[left], spread_parts[right], NT)
    for i in range(WLAT):
        adjoint_out[i] = adjoint[i * WLON : (i + 1) * WLON]
    own_out[...] = quadrant_of(adjoint, HALF_LAT, HALF_LON).astype(bf16)
    lat_out[...] = quadrant_of(adjoint, 0, HALF_LON).astype(bf16)
    lon_out[...] = quadrant_of(adjoint, HALF_LAT, 0).astype(bf16)
    far_out[...] = quadrant_of(adjoint, 0, 0).astype(bf16)


def adjoint_kernel(
    own_piece,
    lon_piece,
    far_piece,
    lat_piece,
    decode_ref,
    decode_gain_ref,
    logit_ref,
    block_hbm,
    outw_hbm,
    units_hbm,
    probs_hbm,
    scales_hbm,
    hidden_hbm,
    gain_hbm,
    embed_hbm,
    qkv_hbm,
    own_out,
    lat_out,
    lon_out,
    far_out,
    block_ref,
    outw_ref,
    units_ref,
    probs_ref,
    scales_ref,
    hidden_ref,
    gain_ref,
    embed_ref,
    qkv_ref,
    packed_ref,
    sems,
):
    width = embed_ref.shape[1]
    quads = width // QUAD
    fetched = []

    def fetch(source, target):
        copy = pltpu.make_async_copy(source, target, sems.at[len(fetched)])
        copy.start()
        fetched.append(copy)

    for source, target in (
        (block_hbm, block_ref),
        (outw_hbm, outw_ref),
        (units_hbm, units_ref),
        (probs_hbm, probs_ref),
        (scales_hbm, scales_ref),
        (hidden_hbm, hidden_ref),
        (gain_hbm, gain_ref),
        (embed_hbm, embed_ref),
        (qkv_hbm, qkv_ref),
    ):
        fetch(source, target)

    def wait(start, stop):
        for copy in fetched[start:stop]:
            copy.wait()

    wait(0, 1)
    change = quadrants(*[piece[...].astype(f32) for piece in (own_piece, lat_piece, lon_piece, far_piece)])
    unit, scale = normed_rows(block_ref[...].astype(f32))
    normed_ct = product(change.astype(bf16), decode_ref[...], NN).astype(bf16).astype(f32) * decode_gain_ref[...]
    block_ct = norm_tangent(unit, scale, normed_ct).astype(bf16)
    wait(1, 2)
    mixed_ct = product(block_ct, outw_ref[...], NT).astype(bf16)

    lane = lax.broadcasted_iota(jnp.int32, (1, 128), 1)
    first = lane < 64
    same_head = same_head_block()
    logits = logit_ref[...]
    wait(2, 8)
    for quad in range(quads):
        cotangents = []
        for side in range(2):
            pair = quad * 2 + side
            here = pl.ds(pair * 128, 128)
            query, key, value = (units_ref[i * CELLS : (i + 1) * CELLS, here] for i in range(3))
            mixed_here = mixed_ct[:, pair * 128 : (pair + 1) * 128]
            probs = halves(probs_ref[pair])
            scores_ct = []
            for prob, prob_ct in zip(probs, halves(product(mixed_here, by_head(value, first), NT))):
                prob = prob.astype(f32)
                scores_ct.append((prob * (prob_ct - jnp.sum(prob * prob_ct, axis=-1, keepdims=True))).astype(bf16))
            head = pair * 2
            logit = jnp.where(first, logits[:, head : head + 1], logits[:, head + 1 : head + 2])
            query_ct = product(jnp.concatenate(scores_ct, axis=1), by_head(key, first), NN) * logit
            key_ct = product(jnp.concatenate(scores_ct, axis=0), by_head(query, first), TN) * logit
            value_ct = product(jnp.concatenate(probs, axis=0), by_head(mixed_here, first), TN)
            packed_ref[:, pl.ds(2 * width + pair * 128, 128)] = value_ct.astype(bf16)
            cotangents.append(jnp.concatenate([query_ct, key_ct], axis=0))
        unit_ct = jnp.concatenate(cotangents, axis=1)
        here = pl.ds(quad * QUAD, QUAD)
        units = units_ref[: 2 * CELLS, here].astype(f32)
        along = product((units * unit_ct).astype(bf16), same_head, NN)
        raw_ct = (scales_ref[:, here] * (unit_ct - units * along)).astype(bf16)
        packed_ref[:, here] = raw_ct[:CELLS]
        packed_ref[:, pl.ds(width + quad * QUAD, QUAD)] = raw_ct[CELLS:]

    unit, scale = normed_rows(hidden_ref[...].astype(f32))
    wait(8, 9)
    normed_ct = product(packed_ref[...], qkv_ref[...], NT).astype(bf16).astype(f32) * gain_ref[...]
    hidden_ct = (norm_tangent(unit, scale, normed_ct) + block_ct.astype(f32)).astype(bf16)
    state = product(hidden_ct, embed_ref[...], NT)
    lat_out[...] = quadrant_of(state, HALF_LAT, 0).astype(bf16)
    lon_out[...] = quadrant_of(state, 0, HALF_LON).astype(bf16)
    far_out[...] = quadrant_of(state, HALF_LAT, HALF_LON).astype(bf16)
    own_out[...] = quadrant_of(state, 0, 0).astype(bf16)


def shape(dims, dtype):
    return jax.ShapeDtypeStruct(dims, dtype)


def exchanged(lat_piece, lon_piece, far_piece, steps):
    lat_count, lon_count = lax.axis_size("lat"), lax.axis_size("lon")
    lat_piece = lax.ppermute(lat_piece, "lat", [(i, (i + steps) % lat_count) for i in range(lat_count)])
    lon_piece = lax.ppermute(lon_piece, "lon", [(i, (i + steps) % lon_count) for i in range(lon_count)])
    pairs = [
        (i * lat_count + j, ((i + steps) % lon_count) * lat_count + (j + steps) % lat_count)
        for i in range(lon_count)
        for j in range(lat_count)
    ]
    far_piece = lax.ppermute(far_piece, ("lon", "lat"), pairs)
    return lat_piece, lon_piece, far_piece


def run_forward(
    last_band, logit_scale, background, direction, strips, embed_weight, gain, decode_gain, decode_rows, qkv_weight, out_weight
):
    width = embed_weight.shape[1]
    quarter = shape((QUARTER, background.shape[2]), bf16)
    wide = shape((CELLS, width), bf16)
    kept = [
        wide,
        wide,
        shape((3 * CELLS, width), bf16),
        shape((2 * CELLS, width), f32),
        shape((HEADS // 2, CELLS, 2 * CELLS), bf16),
    ]
    inputs = (last_band, logit_scale, background, direction, *(pltpu.with_memory_space_constraint(strips[i], pltpu.VMEM) for i in (1, 2, 0)), embed_weight, gain, decode_gain, decode_rows, qkv_weight, out_weight)
    both = pltpu.VMEM((2 * CELLS, width), bf16)
    return pl.pallas_call(
        forward_kernel,
        out_shape=[pltpu.VMEM(quarter.shape, bf16)] * 4 + kept,
        in_specs=[ANY] * 4 + [VMEM] * 3 + [ANY] * 6,
        out_specs=[VMEM] * 4 + [ANY] * 5,
        scratch_shapes=[pltpu.VMEM(item.shape, item.dtype) for item in (*inputs[:4], *inputs[7:])]
        + [both, both]
        + [pltpu.VMEM(item.shape, item.dtype) for item in kept[2:]]
        + [both, pltpu.SemaphoreType.DMA((18,)), pltpu.SemaphoreType.DMA((5,))],
        cost_estimate=pl.CostEstimate(flops=2_500_000_000, bytes_accessed=10_000_000, transcendentals=300_000),
        name="forward",
    )(*inputs)


def run_observe(direction, pieces, arrived):
    quarter = shape(pieces[0].shape, bf16)
    devices = arrived.shape[0]
    return pl.pallas_call(
        observe_kernel,
        out_shape=[pltpu.VMEM((devices, SLOTS), f32), shape(direction.shape, f32)] + [pltpu.VMEM(quarter.shape, bf16)] * 4,
        in_specs=[VMEM] * 6,
        out_specs=[VMEM] * 6,
        compiler_params=pltpu.CompilerParams(vmem_limit_bytes=2 * 1024 * 1024),
        name="observe",
    )(direction, pltpu.with_memory_space_constraint(pieces[0], pltpu.VMEM), *pieces[1:], arrived)


def run_adjoint(logit_scale, pieces, embed_weight, gain, decode_gain, decode_rows, kept, qkv_weight, out_weight):
    hidden, block, units, scales, probs = kept
    width = embed_weight.shape[1]
    near = [
        pltpu.with_memory_space_constraint(item, pltpu.VMEM)
        for item in (*pieces, decode_rows, decode_gain, logit_scale)
    ]
    late = (block, out_weight, units, probs, scales, hidden, gain, embed_weight, qkv_weight)
    return pl.pallas_call(
        adjoint_kernel,
        out_shape=[pltpu.VMEM(pieces[0].shape, bf16)] * 4,
        in_specs=[VMEM] * len(near) + [ANY] * len(late),
        out_specs=[VMEM] * 4,
        scratch_shapes=[pltpu.VMEM(item.shape, item.dtype) for item in late]
        + [pltpu.VMEM((CELLS, 3 * width), bf16), pltpu.SemaphoreType.DMA((len(late),))],
        cost_estimate=pl.CostEstimate(flops=1_500_000_000, bytes_accessed=10_000_000, transcendentals=300_000),
        name="adjoint",
    )(*near, *late)


def per_device(
    background,
    direction,
    obs_owner,
    obs_site,
    obs_weights,
    obs_precision,
    embed_weight,
    attn_gain,
    qkv_weight,
    logit_scale,
    out_weight,
    decode_gain,
    decode_weight,
):
    var_count = background.shape[2]
    width = embed_weight.shape[1]
    devices = lax.axis_size("lat") * lax.axis_size("lon")
    obs_rows = obs_site.shape[0]
    last_band = (lax.axis_index("lat") == lax.axis_size("lat") - 1).astype(f32).reshape(1, 1)
    logit_scale = logit_scale.reshape(1, HEADS)
    gain = attn_gain.reshape(1, width)
    decode_gain = decode_gain.reshape(1, width)
    decode_rows = decode_weight.T

    owners = obs_owner.reshape(1, obs_rows)
    *strips, outgoing, slots = pl.pallas_call(
        prepare_kernel,
        out_shape=[pltpu.VMEM((2 * QUARTER, var_count), bf16)] * 3
        + [pltpu.VMEM((devices, SLOTS * 8), f32), shape((1, obs_rows), f32)],
        in_specs=[VMEM] * 6,
        out_specs=[VMEM] * 5,
        name="prepare",
    )(
        background,
        direction,
        owners,
        obs_site.reshape(1, obs_rows),
        obs_weights.T,
        obs_precision.reshape(1, obs_rows),
    )
    strips = exchanged(*strips, -1)
    arrived = lax.all_to_all(outgoing, ("lon", "lat"), split_axis=0, concat_axis=0, tiled=True)

    lat_piece, lon_piece, far_piece, own_piece, *kept = run_forward(
        last_band, logit_scale, background, direction, strips, embed_weight, gain, decode_gain, decode_rows, qkv_weight, out_weight
    )
    lat_piece, lon_piece, far_piece = exchanged(lat_piece, lon_piece, far_piece, 1)

    at_obs, adjoint_field, own_piece, lat_piece, lon_piece, far_piece = run_observe(
        direction, (own_piece, lon_piece, far_piece, lat_piece), arrived
    )
    lat_piece, lon_piece, far_piece = exchanged(lat_piece, lon_piece, far_piece, -1)
    returned = lax.all_to_all(at_obs, ("lon", "lat"), split_axis=0, concat_axis=0, tiled=True)

    own_piece, lat_piece, lon_piece, far_piece = run_adjoint(
        logit_scale, (own_piece, lon_piece, far_piece, lat_piece), embed_weight, gain, decode_gain, decode_rows, kept, qkv_weight, out_weight
    )
    own_piece, returned = lax.optimization_barrier((own_piece, returned))
    lat_piece, lon_piece, far_piece = exchanged(lat_piece, lon_piece, far_piece, 1)

    hvp = adjoint_field
    for piece, row, col in (
        (lon_piece, HALF_LAT, 0),
        (far_piece, 0, 0),
        (lat_piece, 0, HALF_LON),
        (own_piece, HALF_LAT, HALF_LON),
    ):
        piece = piece.reshape(HALF_LAT, HALF_LON, var_count).astype(f32)
        around = ((row, HALF_LAT - row, 0), (col, HALF_LON - col, 0), (0, 0, 0))
        hvp = hvp + lax.pad(piece, jnp.zeros((), f32), around)
    obs_increment = pl.pallas_call(
        unpack_kernel,
        out_shape=shape((1, obs_rows), f32),
        in_specs=[VMEM] * 3,
        out_specs=VMEM,
        name="unpack",
    )(owners, slots, returned)
    return (hvp, obs_increment.reshape(obs_rows))


def solution(mesh):
    in_specs = (
        P("lat", "lon", None),
        P("lat", "lon", None),
        P(("lon", "lat"), None),
        P(("lon", "lat")),
        P(("lon", "lat"), None),
        P(("lon", "lat")),
        P(),
        P(),
        P(),
        P(),
        P(),
        P(),
        P(),
    )
    out_specs = (P("lat", "lon", None), P(("lon", "lat")))
    return jax.shard_map(
        per_device, mesh=mesh, in_specs=in_specs, out_specs=out_specs, check_vma=False
    )
```

```python
import jax
import jax.numpy as jnp
from jax import lax
from jax.experimental import pallas as pl
from jax.experimental.pallas import tpu as pltpu
from jax.sharding import PartitionSpec as P

HEADS = 16
WLAT = 8
WLON = 16
CELLS = WLAT * WLON
HALF_LAT = WLAT // 2
HALF_LON = WLON // 2
QUARTER = HALF_LAT * HALF_LON
SLOTS = 8
PIECES = 2
QUAD = 256

eps_norm = 1e-05
eps_head = 1e-06

f32 = jnp.float32
bf16 = jnp.bfloat16

NN = ((1,), (0,))
NT = ((1,), (1,))
TN = ((0,), (0,))

VMEM = pl.BlockSpec(memory_space=pltpu.VMEM)
SMEM = pl.BlockSpec(memory_space=pltpu.SMEM)
ANY = pl.BlockSpec(memory_space=pl.ANY)


def product(left, right, dims):
    return lax.dot_general(left, right, (dims, ((), ())), preferred_element_type=f32)


def parts_of(value, count):
    parts = []
    for _ in range(count):
        part = value.astype(bf16)
        parts.append(part)
        value = value - part.astype(f32)
    return parts


def quadrants(top_left, bottom_left, top_right, bottom_right):
    rows = []
    for left, right in ((top_left, top_right), (bottom_left, bottom_right)):
        for i in range(HALF_LAT):
            rows.append(left[i * HALF_LON : (i + 1) * HALF_LON])
            rows.append(right[i * HALF_LON : (i + 1) * HALF_LON])
    return jnp.concatenate(rows, axis=0)


def quadrant_of(cells, row, col):
    return jnp.concatenate(
        [cells[(row + i) * WLON + col : (row + i) * WLON + col + HALF_LON] for i in range(HALF_LAT)], axis=0
    )


def normed_rows(values):
    centred = values - jnp.mean(values, axis=-1, keepdims=True)
    scale = lax.rsqrt(jnp.mean(centred * centred, axis=-1, keepdims=True) + eps_norm)
    return centred * scale, scale


def norm_tangent(unit, scale, tangent):
    moved = tangent - jnp.mean(tangent, axis=-1, keepdims=True)
    return scale * (moved - unit * jnp.mean(unit * tangent, axis=-1, keepdims=True))


def normed_with_tangent(values, tangent):
    centred = values - jnp.mean(values, axis=-1, keepdims=True)
    moved = tangent - jnp.mean(tangent, axis=-1, keepdims=True)
    spread = jnp.mean(centred * centred, axis=-1, keepdims=True)
    along = jnp.mean(centred * moved, axis=-1, keepdims=True)
    scale = lax.rsqrt(spread + eps_norm)
    unit = centred * scale
    return unit, scale * (moved - unit * (scale * along))


def same_head_block():
    rows = lax.broadcasted_iota(jnp.int32, (QUAD, QUAD), 0) >> 6
    return (rows == lax.broadcasted_iota(jnp.int32, (QUAD, QUAD), 1) >> 6).astype(bf16)


def by_head(pair, first):
    zero = jnp.zeros((), pair.dtype)
    return jnp.concatenate([jnp.where(first, pair, zero), jnp.where(first, zero, pair)], axis=0)


def halves(value):
    return value[:, :CELLS], value[:, CELLS:]


def slots_of(owners, rows, devices):
    owner_hot = (lax.broadcasted_iota(jnp.int32, (devices, rows), 0) == owners).astype(f32)
    block = 128
    upper = (
        lax.broadcasted_iota(jnp.int32, (block, block), 0) <= lax.broadcasted_iota(jnp.int32, (block, block), 1)
    ).astype(bf16)
    before = jnp.zeros((devices, 1), f32)
    slots = []
    for start in range(0, rows, block):
        here = owner_hot[:, start : start + block]
        counted = product(here.astype(bf16), upper, NN) + before
        slots.append(jnp.sum(counted * here, axis=0, keepdims=True) - 1.0)
        before = counted[:, block - 1 : block]
    slots = jnp.concatenate(slots, axis=1)
    return owner_hot, slots


def prepare_kernel(
    background_ref,
    direction_ref,
    owner_ref,
    site_ref,
    weights_ref,
    precision_ref,
    lat_out,
    lon_out,
    far_out,
    out_ref,
    slots_ref,
):
    for piece_out, row, col in ((lat_out, 0, HALF_LON), (lon_out, HALF_LAT, 0), (far_out, 0, 0)):
        pieces = []
        for source in (background_ref, direction_ref):
            for i in range(HALF_LAT):
                pieces.append(source[row + i, col : col + HALF_LON, :])
        piece_out[...] = jnp.concatenate(pieces, axis=0).astype(bf16)
    rows = owner_ref.shape[1]
    devices = out_ref.shape[0]
    owner_hot, slots = slots_of(owner_ref[...], rows, devices)
    slots_ref[...] = slots
    payload = jnp.concatenate(
        [weights_ref[...], precision_ref[...], site_ref[...].astype(f32), jnp.zeros((2, rows), f32)], axis=0
    )
    owner_hot = owner_hot.astype(bf16)
    spread = jnp.concatenate([jnp.where(slots == float(k), payload, 0.0) for k in range(SLOTS)], axis=0)
    out = jnp.zeros((devices, SLOTS * 8), f32)
    for part in parts_of(spread, PIECES):
        out = out + product(owner_hot, part, NT)
    out_ref[...] = out


def unpack_kernel(owner_ref, slots_ref, returned_ref, out_ref):
    rows = owner_ref.shape[1]
    devices = returned_ref.shape[0]
    owner_hot = (lax.broadcasted_iota(jnp.int32, (devices, rows), 0) == owner_ref[...]).astype(bf16)
    picked = jnp.zeros((SLOTS, rows), f32)
    for part in parts_of(returned_ref[...], PIECES):
        picked = picked + product(part, owner_hot, TN)
    slot_hot = lax.broadcasted_iota(jnp.int32, (SLOTS, rows), 0).astype(f32) == slots_ref[...]
    out_ref[...] = jnp.sum(jnp.where(slot_hot, picked, 0.0), axis=0, keepdims=True)


def forward_kernel(
    band_hbm,
    logit_hbm,
    background_hbm,
    direction_hbm,
    lon_piece,
    far_piece,
    lat_piece,
    embed_hbm,
    gain_hbm,
    decode_gain_hbm,
    decode_hbm,
    qkv_hbm,
    outw_hbm,
    lat_out,
    lon_out,
    far_out,
    own_out,
    hidden_hbm,
    block_hbm,
    units_hbm,
    scales_hbm,
    probs_hbm,
    band_ref,
    logit_ref,
    background_ref,
    direction_ref,
    embed_ref,
    gain_ref,
    decode_gain_ref,
    decode_ref,
    qkv_ref,
    outw_ref,
    hidden_ref,
    block_ref,
    units_ref,
    scales_ref,
    probs_ref,
    mixed_ref,
    sems_in,
    sems_out,
):
    width = embed_ref.shape[1]
    quads = width // QUAD
    count = 0

    def fetch(source, target):
        nonlocal count
        copy = pltpu.make_async_copy(source, target, sems_in.at[count])
        copy.start()
        count += 1
        return copy

    first_needed = [
        fetch(*pair)
        for pair in (
            (background_hbm, background_ref),
            (direction_hbm, direction_ref),
            (embed_hbm, embed_ref),
            (gain_hbm, gain_ref),
            (band_hbm, band_ref),
            (logit_hbm, logit_ref),
        )
    ]
    fetched = []
    for half in range(2):
        for third in range(3):
            columns = pl.ds(third * width + half * (width // 2), width // 2)
            fetched.append(fetch(qkv_hbm.at[:, columns], qkv_ref.at[:, columns]))
    last_needed = [
        fetch(*pair) for pair in ((outw_hbm, outw_ref), (decode_gain_hbm, decode_gain_ref), (decode_hbm, decode_ref))
    ]
    kept = []

    def keep(source, target):
        copy = pltpu.make_async_copy(source, target, sems_out.at[len(kept)])
        copy.start()
        kept.append(copy)

    lane = lax.broadcasted_iota(jnp.int32, (1, 128), 1)
    first = lane < 64
    same_head = same_head_block()
    for copy in first_needed:
        copy.wait()
    low_q = lax.broadcasted_iota(jnp.int32, (CELLS, CELLS), 0) < CELLS // 2
    low_k = lax.broadcasted_iota(jnp.int32, (CELLS, CELLS), 1) < CELLS // 2
    allowed = jnp.where(low_q == low_k, 1.0, 1.0 - band_ref[...])
    logits = logit_ref[...]
    states = []
    for number, source in enumerate((background_ref, direction_ref)):
        own = jnp.concatenate([source[HALF_LAT + i, HALF_LON:, :] for i in range(HALF_LAT)], axis=0)
        part = slice(number * QUARTER, (number + 1) * QUARTER)
        received = [piece[part, :].astype(f32) for piece in (lat_piece, lon_piece, far_piece)]
        states.append(quadrants(own, *received))
    states = jnp.concatenate(states, axis=0).astype(bf16)
    hidden = product(states, embed_ref[...], NN).astype(bf16)
    hidden_ref[...] = hidden
    keep(hidden_ref.at[:CELLS], hidden_hbm)
    hidden = hidden.astype(f32)
    gain = gain_ref[...]
    normed = jnp.concatenate(
        [part * gain for part in normed_with_tangent(hidden[:CELLS], hidden[CELLS:])], axis=0
    ).astype(bf16)

    def project(quad):
        here = pl.ds(quad * QUAD, QUAD)
        packed = []
        for third in range(3):
            packed.append(product(normed, qkv_ref[:, pl.ds(third * width + quad * QUAD, QUAD)], NN))
        raw = jnp.concatenate([packed[0][:CELLS], packed[1][:CELLS]], axis=0)
        raw_tan = jnp.concatenate([packed[0][CELLS:], packed[1][CELLS:]], axis=0)
        scale = lax.rsqrt(product((raw * raw).astype(bf16), same_head, NN) + eps_head)
        unit = raw * scale
        along = product((unit * raw_tan).astype(bf16), same_head, NN)
        unit_tan = (scale * (raw_tan - unit * along)).astype(bf16)
        unit = unit.astype(bf16)
        value = packed[2].astype(bf16)
        scales_ref[:, here] = scale
        units_ref[: 2 * CELLS, here] = unit
        units_ref[2 * CELLS :, here] = value[:CELLS]
        return unit, unit_tan, value

    def attend(quad, unit, unit_tan, value):
        for side in range(2):
            pair = quad * 2 + side
            lanes = slice(side * 128, (side + 1) * 128)
            query, key = unit[:CELLS, lanes], by_head(unit[CELLS:, lanes], first)
            query_tan, key_tan = unit_tan[:CELLS, lanes], by_head(unit_tan[CELLS:, lanes], first)
            values = jnp.concatenate(
                [by_head(value[:CELLS, lanes], first), by_head(value[CELLS:, lanes], first)], axis=1
            )
            scores = product(query, key, NT)
            scores_tan = product(
                jnp.concatenate([query, query_tan], axis=1), jnp.concatenate([key_tan, key], axis=1), NT
            )
            probs, probs_tan = [], []
            for half, (score, score_tan) in enumerate(zip(halves(scores), halves(scores_tan))):
                head = pair * 2 + half
                logit = logits[:, head : head + 1]
                weights = jnp.exp(score * logit) * allowed
                prob = weights * (1.0 / jnp.sum(weights, axis=-1, keepdims=True))
                score_tan = score_tan * logit
                prob_tan = prob * (score_tan - jnp.sum(prob * score_tan, axis=-1, keepdims=True))
                probs.append(prob.astype(bf16))
                probs_tan.append(prob_tan.astype(bf16))
            probs = jnp.concatenate(probs, axis=1)
            probs_ref[pair] = probs
            mixed, mixed_tan = halves(product(probs, values, NN))
            mixed_tan = mixed_tan + product(jnp.concatenate(probs_tan, axis=1), values[:, :128], NN)
            columns = pl.ds(pair * 128, 128)
            mixed_ref[:CELLS, columns] = mixed.astype(bf16)
            mixed_ref[CELLS:, columns] = mixed_tan.astype(bf16)

    for copy in fetched[0:3]:
        copy.wait()
    vals0 = project(0)
    vals1 = project(1)
    for copy in fetched[3:6]:
        copy.wait()
    vals2 = project(2)
    vals3 = project(3)
    attend(0, *vals0)
    attend(1, *vals1)
    attend(2, *vals2)
    attend(3, *vals3)

    keep(units_ref, units_hbm)
    keep(scales_ref, scales_hbm)
    keep(probs_ref, probs_hbm)
    for copy in last_needed:
        copy.wait()
    block = (hidden_ref[...].astype(f32) + product(mixed_ref[...], outw_ref[...], NN)).astype(bf16)
    block_ref[...] = block
    keep(block_ref.at[:CELLS], block_hbm)
    block = block.astype(f32)
    moved = normed_with_tangent(block[:CELLS], block[CELLS:])[1]
    change = product((moved * decode_gain_ref[...]).astype(bf16), decode_ref[...], NT)
    lat_out[...] = quadrant_of(change, HALF_LAT, 0).astype(bf16)
    lon_out[...] = quadrant_of(change, 0, HALF_LON).astype(bf16)
    far_out[...] = quadrant_of(change, HALF_LAT, HALF_LON).astype(bf16)
    own_out[...] = quadrant_of(change, 0, 0).astype(bf16)
    for copy in kept:
        copy.wait()


def observe_kernel(
    direction_ref,
    own_piece,
    lon_piece,
    far_piece,
    lat_piece,
    arrived_ref,
    at_obs_out,
    adjoint_out,
    own_out,
    lat_out,
    lon_out,
    far_out,
):
    var_count = direction_ref.shape[2]
    devices = arrived_ref.shape[0]
    pieces = [piece[...].astype(f32) for piece in (far_piece, lon_piece, lat_piece, own_piece)]
    moved = quadrants(*pieces)
    tangent = jnp.concatenate([direction_ref[i] for i in range(WLAT)], axis=0) + moved
    arrived = jnp.transpose(arrived_ref[...])
    cell_ids = lax.broadcasted_iota(jnp.int32, (CELLS, devices), 0).astype(f32)
    var_ids = lax.broadcasted_iota(jnp.int32, (var_count, devices), 0).astype(f32)
    selectors, var_hots, precisions = [], [], []
    for k in range(SLOTS):
        row = arrived[k * 8 : (k + 1) * 8]
        site = row[5:6]
        cell = jnp.floor((site + 0.5) * (1.0 / var_count))
        variable = site - cell * var_count
        selector = jnp.zeros((CELLS, devices), f32)
        for corner, offset in enumerate((0, 1, WLON, WLON + 1)):
            selector = selector + jnp.where(cell_ids == cell + float(offset), row[corner : corner + 1], 0.0)
        selectors.append(selector)
        var_hots.append((var_ids == variable).astype(f32))
        precisions.append(row[4:5])
    selector = jnp.concatenate(selectors, axis=1)
    var_hot = jnp.concatenate(var_hots, axis=1)
    precision = jnp.concatenate(precisions, axis=1)
    selector_parts = parts_of(selector, 2)
    tangent_parts = parts_of(tangent, 3)
    picked = product(tangent_parts[0], selector_parts[0], TN)
    for left, right in ((1, 0), (0, 1), (2, 0)):
        picked = picked + product(tangent_parts[left], selector_parts[right], TN)
    at_obs = jnp.sum(picked * var_hot, axis=0, keepdims=True)
    at_obs_out[...] = jnp.transpose(
        jnp.concatenate([at_obs[:, k * devices : (k + 1) * devices] for k in range(SLOTS)], axis=0)
    )
    spread_parts = parts_of(var_hot * (at_obs * precision), 2)
    adjoint = product(selector_parts[0], spread_parts[0], NT)
    for left, right in ((1, 0), (0, 1)):
        adjoint = adjoint + product(selector_parts[left], spread_parts[right], NT)
    for i in range(WLAT):
        adjoint_out[i] = adjoint[i * WLON : (i + 1) * WLON]
    own_out[...] = quadrant_of(adjoint, HALF_LAT, HALF_LON).astype(bf16)
    lat_out[...] = quadrant_of(adjoint, 0, HALF_LON).astype(bf16)
    lon_out[...] = quadrant_of(adjoint, HALF_LAT, 0).astype(bf16)
    far_out[...] = quadrant_of(adjoint, 0, 0).astype(bf16)


def adjoint_kernel(
    own_piece,
    lon_piece,
    far_piece,
    lat_piece,
    decode_ref,
    decode_gain_ref,
    logit_ref,
    block_hbm,
    outw_hbm,
    units_hbm,
    probs_hbm,
    scales_hbm,
    hidden_hbm,
    gain_hbm,
    embed_hbm,
    qkv_hbm,
    own_out,
    lat_out,
    lon_out,
    far_out,
    block_ref,
    outw_ref,
    units_ref,
    probs_ref,
    scales_ref,
    hidden_ref,
    gain_ref,
    embed_ref,
    qkv_ref,
    packed_ref,
    sems,
):
    width = embed_ref.shape[1]
    quads = width // QUAD
    fetched = []

    def fetch(source, target):
        copy = pltpu.make_async_copy(source, target, sems.at[len(fetched)])
        copy.start()
        fetched.append(copy)

    for source, target in (
        (block_hbm, block_ref),
        (outw_hbm, outw_ref),
        (units_hbm, units_ref),
        (probs_hbm, probs_ref),
        (scales_hbm, scales_ref),
        (hidden_hbm, hidden_ref),
        (gain_hbm, gain_ref),
        (embed_hbm, embed_ref),
        (qkv_hbm, qkv_ref),
    ):
        fetch(source, target)

    def wait(start, stop):
        for copy in fetched[start:stop]:
            copy.wait()

    wait(0, 1)
    change = quadrants(*[piece[...].astype(f32) for piece in (own_piece, lat_piece, lon_piece, far_piece)])
    unit, scale = normed_rows(block_ref[...].astype(f32))
    normed_ct = product(change.astype(bf16), decode_ref[...], NN).astype(bf16).astype(f32) * decode_gain_ref[...]
    block_ct = norm_tangent(unit, scale, normed_ct).astype(bf16)
    wait(1, 2)
    mixed_ct = product(block_ct, outw_ref[...], NT).astype(bf16)

    lane = lax.broadcasted_iota(jnp.int32, (1, 128), 1)
    first = lane < 64
    same_head = same_head_block()
    logits = logit_ref[...]
    wait(2, 8)
    for quad in range(quads):
        cotangents = []
        for side in range(2):
            pair = quad * 2 + side
            here = pl.ds(pair * 128, 128)
            query, key, value = (units_ref[i * CELLS : (i + 1) * CELLS, here] for i in range(3))
            mixed_here = mixed_ct[:, pair * 128 : (pair + 1) * 128]
            probs = halves(probs_ref[pair])
            scores_ct = []
            for prob, prob_ct in zip(probs, halves(product(mixed_here, by_head(value, first), NT))):
                prob = prob.astype(f32)
                scores_ct.append((prob * (prob_ct - jnp.sum(prob * prob_ct, axis=-1, keepdims=True))).astype(bf16))
            head = pair * 2
            logit = jnp.where(first, logits[:, head : head + 1], logits[:, head + 1 : head + 2])
            query_ct = product(jnp.concatenate(scores_ct, axis=1), by_head(key, first), NN) * logit
            key_ct = product(jnp.concatenate(scores_ct, axis=0), by_head(query, first), TN) * logit
            value_ct = product(jnp.concatenate(probs, axis=0), by_head(mixed_here, first), TN)
            packed_ref[:, pl.ds(2 * width + pair * 128, 128)] = value_ct.astype(bf16)
            cotangents.append(jnp.concatenate([query_ct, key_ct], axis=0))
        unit_ct = jnp.concatenate(cotangents, axis=1)
        here = pl.ds(quad * QUAD, QUAD)
        units = units_ref[: 2 * CELLS, here].astype(f32)
        along = product((units * unit_ct).astype(bf16), same_head, NN)
        raw_ct = (scales_ref[:, here] * (unit_ct - units * along)).astype(bf16)
        packed_ref[:, here] = raw_ct[:CELLS]
        packed_ref[:, pl.ds(width + quad * QUAD, QUAD)] = raw_ct[CELLS:]

    unit, scale = normed_rows(hidden_ref[...].astype(f32))
    wait(8, 9)
    normed_ct = product(packed_ref[...], qkv_ref[...], NT).astype(bf16).astype(f32) * gain_ref[...]
    hidden_ct = (norm_tangent(unit, scale, normed_ct) + block_ct.astype(f32)).astype(bf16)
    state = product(hidden_ct, embed_ref[...], NT)
    lat_out[...] = quadrant_of(state, HALF_LAT, 0).astype(bf16)
    lon_out[...] = quadrant_of(state, 0, HALF_LON).astype(bf16)
    far_out[...] = quadrant_of(state, HALF_LAT, HALF_LON).astype(bf16)
    own_out[...] = quadrant_of(state, 0, 0).astype(bf16)


def shape(dims, dtype):
    return jax.ShapeDtypeStruct(dims, dtype)


def exchanged(lat_piece, lon_piece, far_piece, steps):
    lat_count, lon_count = lax.axis_size("lat"), lax.axis_size("lon")
    lat_piece = lax.ppermute(lat_piece, "lat", [(i, (i + steps) % lat_count) for i in range(lat_count)])
    lon_piece = lax.ppermute(lon_piece, "lon", [(i, (i + steps) % lon_count) for i in range(lon_count)])
    pairs = [
        (i * lat_count + j, ((i + steps) % lon_count) * lat_count + (j + steps) % lat_count)
        for i in range(lon_count)
        for j in range(lat_count)
    ]
    far_piece = lax.ppermute(far_piece, ("lon", "lat"), pairs)
    return lat_piece, lon_piece, far_piece


def run_forward(
    last_band, logit_scale, background, direction, strips, embed_weight, gain, decode_gain, decode_rows, qkv_weight, out_weight
):
    width = embed_weight.shape[1]
    quarter = shape((QUARTER, background.shape[2]), bf16)
    wide = shape((CELLS, width), bf16)
    kept = [
        wide,
        wide,
        shape((3 * CELLS, width), bf16),
        shape((2 * CELLS, width), f32),
        shape((HEADS // 2, CELLS, 2 * CELLS), bf16),
    ]
    inputs = (last_band, logit_scale, background, direction, *(pltpu.with_memory_space_constraint(strips[i], pltpu.VMEM) for i in (1, 2, 0)), embed_weight, gain, decode_gain, decode_rows, qkv_weight, out_weight)
    both = pltpu.VMEM((2 * CELLS, width), bf16)
    return pl.pallas_call(
        forward_kernel,
        out_shape=[pltpu.VMEM(quarter.shape, bf16)] * 4 + kept,
        in_specs=[ANY] * 4 + [VMEM] * 3 + [ANY] * 6,
        out_specs=[VMEM] * 4 + [ANY] * 5,
        scratch_shapes=[pltpu.VMEM(item.shape, item.dtype) for item in (*inputs[:4], *inputs[7:])]
        + [both, both]
        + [pltpu.VMEM(item.shape, item.dtype) for item in kept[2:]]
        + [both, pltpu.SemaphoreType.DMA((18,)), pltpu.SemaphoreType.DMA((5,))],
        cost_estimate=pl.CostEstimate(flops=2_500_000_000, bytes_accessed=10_000_000, transcendentals=300_000),
        name="forward",
    )(*inputs)


def run_observe(direction, pieces, arrived):
    quarter = shape(pieces[0].shape, bf16)
    devices = arrived.shape[0]
    return pl.pallas_call(
        observe_kernel,
        out_shape=[pltpu.VMEM((devices, SLOTS), f32), shape(direction.shape, f32)] + [pltpu.VMEM(quarter.shape, bf16)] * 4,
        in_specs=[VMEM] * 6,
        out_specs=[VMEM] * 6,
        compiler_params=pltpu.CompilerParams(vmem_limit_bytes=2 * 1024 * 1024),
        name="observe",
    )(direction, pltpu.with_memory_space_constraint(pieces[0], pltpu.VMEM), *pieces[1:], arrived)


def run_adjoint(logit_scale, pieces, embed_weight, gain, decode_gain, decode_rows, kept, qkv_weight, out_weight):
    hidden, block, units, scales, probs = kept
    width = embed_weight.shape[1]
    near = [
        pltpu.with_memory_space_constraint(item, pltpu.VMEM)
        for item in (*pieces, decode_rows, decode_gain, logit_scale)
    ]
    late = (block, out_weight, units, probs, scales, hidden, gain, embed_weight, qkv_weight)
    return pl.pallas_call(
        adjoint_kernel,
        out_shape=[pltpu.VMEM(pieces[0].shape, bf16)] * 4,
        in_specs=[VMEM] * len(near) + [ANY] * len(late),
        out_specs=[VMEM] * 4,
        scratch_shapes=[pltpu.VMEM(item.shape, item.dtype) for item in late]
        + [pltpu.VMEM((CELLS, 3 * width), bf16), pltpu.SemaphoreType.DMA((len(late),))],
        cost_estimate=pl.CostEstimate(flops=1_500_000_000, bytes_accessed=10_000_000, transcendentals=300_000),
        name="adjoint",
    )(*near, *late)


def per_device(
    background,
    direction,
    obs_owner,
    obs_site,
    obs_weights,
    obs_precision,
    embed_weight,
    attn_gain,
    qkv_weight,
    logit_scale,
    out_weight,
    decode_gain,
    decode_weight,
):
    var_count = background.shape[2]
    width = embed_weight.shape[1]
    devices = lax.axis_size("lat") * lax.axis_size("lon")
    obs_rows = obs_site.shape[0]
    last_band = (lax.axis_index("lat") == lax.axis_size("lat") - 1).astype(f32).reshape(1, 1)
    logit_scale = logit_scale.reshape(1, HEADS)
    gain = attn_gain.reshape(1, width)
    decode_gain = decode_gain.reshape(1, width)
    decode_rows = decode_weight.T

    owners = obs_owner.reshape(1, obs_rows)
    *strips, outgoing, slots = pl.pallas_call(
        prepare_kernel,
        out_shape=[pltpu.VMEM((2 * QUARTER, var_count), bf16)] * 3
        + [pltpu.VMEM((devices, SLOTS * 8), f32), pltpu.VMEM((1, obs_rows), f32)],
        in_specs=[VMEM] * 6,
        out_specs=[VMEM] * 5,
        name="prepare",
    )(
        background,
        direction,
        owners,
        obs_site.reshape(1, obs_rows),
        obs_weights.T,
        obs_precision.reshape(1, obs_rows),
    )
    strips = exchanged(*strips, -1)
    arrived = lax.all_to_all(outgoing, ("lon", "lat"), split_axis=0, concat_axis=0, tiled=True)

    lat_piece, lon_piece, far_piece, own_piece, *kept = run_forward(
        last_band, logit_scale, background, direction, strips, embed_weight, gain, decode_gain, decode_rows, qkv_weight, out_weight
    )
    lat_piece, lon_piece, far_piece = exchanged(lat_piece, lon_piece, far_piece, 1)

    at_obs, adjoint_field, own_piece, lat_piece, lon_piece, far_piece = run_observe(
        direction, (own_piece, lon_piece, far_piece, lat_piece), arrived
    )
    lat_piece, lon_piece, far_piece = exchanged(lat_piece, lon_piece, far_piece, -1)
    returned = lax.all_to_all(at_obs, ("lon", "lat"), split_axis=0, concat_axis=0, tiled=True)

    own_piece, lat_piece, lon_piece, far_piece = run_adjoint(
        logit_scale, (own_piece, lon_piece, far_piece, lat_piece), embed_weight, gain, decode_gain, decode_rows, kept, qkv_weight, out_weight
    )
    own_piece, returned = lax.optimization_barrier((own_piece, returned))
    lat_piece, lon_piece, far_piece = exchanged(lat_piece, lon_piece, far_piece, 1)

    hvp = adjoint_field
    for piece, row, col in (
        (lon_piece, HALF_LAT, 0),
        (far_piece, 0, 0),
        (lat_piece, 0, HALF_LON),
        (own_piece, HALF_LAT, HALF_LON),
    ):
        piece = piece.reshape(HALF_LAT, HALF_LON, var_count).astype(f32)
        around = ((row, HALF_LAT - row, 0), (col, HALF_LON - col, 0), (0, 0, 0))
        hvp = hvp + lax.pad(piece, jnp.zeros((), f32), around)
    obs_increment = pl.pallas_call(
        unpack_kernel,
        out_shape=shape((1, obs_rows), f32),
        in_specs=[VMEM] * 3,
        out_specs=VMEM,
        name="unpack",
    )(owners, *(pltpu.with_memory_space_constraint(item, pltpu.VMEM) for item in (slots, returned)))
    return (hvp, obs_increment.reshape(obs_rows))


def solution(mesh):
    in_specs = (
        P("lat", "lon", None),
        P("lat", "lon", None),
        P(("lon", "lat"), None),
        P(("lon", "lat")),
        P(("lon", "lat"), None),
        P(("lon", "lat")),
        P(),
        P(),
        P(),
        P(),
        P(),
        P(),
        P(),
    )
    out_specs = (P("lat", "lon", None), P(("lon", "lat")))
    return jax.shard_map(
        per_device, mesh=mesh, in_specs=in_specs, out_specs=out_specs, check_vma=False
    )
```
